32 devices in a mesh: seq: 32 (over z, y, x, core).
Axes of the slice: x: 2, y: 2, z: 4, core: 2. Of those that a mesh axis runs over, the one named last changes fastest.
Arguments:
- saved_input: bfloat16 [8192, 192], P('seq'), may hold values from -6 to 6
- cotangent: bfloat16 [8192, 192], P('seq'), may hold values from -15 to 15
- w_in: bfloat16 [384, 768], replicated, may hold values from -0.3125 to 0.3125
- bias_in: float32 [768], replicated, may hold values from -4 to 4
- w_out: bfloat16 [768, 384], replicated, may hold values from -0.21875 to 0.21875
- residual_logit: float32 [384], replicated, may hold values from -1 to 2
- branch_scale: float32 [384], replicated, may hold values from 0.1 to 1
Outputs:
- grad_input: bfloat16 [8192, 192], P('seq')
- grad_w_in: float32 [384, 768], replicated
- grad_w_out: float32 [768, 384], replicated
The draws below stay inside these ranges and needn't reach their ends.
All inputs are finite; a program needn't handle non-finite values.
Results may differ from the reference program's by a relative error of at most 0.02.
Values may be sent and summed in bfloat16 or wider, within the bound.
No kernel may reach another device: no remote copies, remote signals or barrier semaphores. Data moves between devices by JAX's collectives and lax.ppermute only.
A program may use at most 64 MiB of HBM per device.

```python
import math
import jax
import jax.numpy as jnp
from jax import lax

WIDTH = 192
SWITCH_UNITS = 768
POS_DEV = 256
POSITIONS = 8192
LEVELS = 5


def draw_cotangent(key, part):
    position = jnp.arange(POSITIONS, dtype=jnp.float32) / POSITIONS
    row_scale = jnp.exp(jnp.log(16.0) * position) / 6.8
    base_draw = jnp.clip(jax.random.normal(key, (POSITIONS, WIDTH), jnp.float32), -6.0, 6.0)
    return (base_draw * row_scale[:, None]).astype(jnp.bfloat16)


def level_of(key, extent, pieces, smallest, high):
    def one(dim, blocks):
        draws = jax.random.uniform(jax.random.fold_in(jax.random.fold_in(key, 6), dim), (blocks,), jnp.float32, smallest / len(pieces), high / len(pieces))
        return jnp.repeat(jnp.exp(draws), extent[dim] // blocks).reshape((-1,) + (1,) * (len(extent) - dim - 1))

    level = one(*pieces[0])
    for cut in pieces[1:]:
        level = level * one(*cut)
    return level


def scatter_about(key, extent, width, reach, split=(), held_as=jnp.bfloat16):
    level = level_of(key, extent, split, -0.22, 0.18) if split else 1.0
    array = jax.random.normal(key, extent, jnp.float32) * width * level
    return jnp.minimum(jnp.maximum(array, -reach), reach).astype(held_as)


def setup_inputs(seed: int = 0) -> dict:
    key_of = jax.random.split(jax.random.key(seed), 8)
    return {
        "saved_input": scatter_about(key_of[0], (POSITIONS, WIDTH), 1.0, 6.0, ((0, 32),)),
        "cotangent": draw_cotangent(jax.random.fold_in(key_of[7], 71), 0),
        "w_in": scatter_about(key_of[2], (2 * WIDTH, SWITCH_UNITS), (2 * WIDTH) ** -0.5, 0.3125),
        "bias_in": scatter_about(key_of[3], (SWITCH_UNITS,), 1.0, 4.0, (), jnp.float32),
        "w_out": scatter_about(key_of[4], (SWITCH_UNITS, 2 * WIDTH), SWITCH_UNITS ** -0.5, 0.21875),
        "residual_logit": jnp.clip(jax.random.uniform(key_of[5], (2 * WIDTH,), jnp.float32, -1.0, 2.0), -1.0, 2.0),
        "branch_scale": jnp.clip(jnp.exp(jax.random.uniform(key_of[6], (2 * WIDTH,), jnp.float32, math.log(0.1), math.log(1.0))), 0.1, 1.0),
    }


epsilon = 1e-05
tanh_scale = 0.7978845608028654
cubic_coef = 0.044715

def gelu_slope(preact):
    inner = tanh_scale * (preact + cubic_coef * preact * preact * preact)
    tangent = jnp.tanh(inner)
    return 0.5 * (1.0 + tangent) + 0.5 * preact * (1.0 - tangent * tangent) * tanh_scale * (1.0 + 3.0 * cubic_coef * preact * preact)

def contract_rows(left, right):
    return lax.dot_general(left.astype(jnp.float32), right.astype(jnp.float32), (((0,), (0,)), ((), ())))

def switch_parts(paired, w_in, bias_in):
    values = paired.astype(jnp.float32)
    average = lax.optimization_barrier(jnp.mean(values, axis=-1, keepdims=True))
    centered = values - average
    inverse = lax.rsqrt(lax.optimization_barrier(jnp.mean(centered * centered, axis=-1, keepdims=True)) + epsilon)
    normed = centered * inverse
    normed_low = normed.astype(jnp.bfloat16)
    preact = jnp.dot(normed_low, w_in, preferred_element_type=jnp.float32) + bias_in
    activated = jax.nn.gelu(preact, approximate=True).astype(jnp.bfloat16)
    return (normed, normed_low, inverse, preact, activated)

def switch_result(paired, parts, w_out, keep_gate, branch_scale):
    branch = jnp.dot(parts[4], w_out, preferred_element_type=jnp.float32)
    return (keep_gate * paired.astype(jnp.float32) + branch_scale * branch).astype(jnp.bfloat16)

def switch_backward(pair_grad, parts, w_in, w_out, keep_gate, branch_scale):
    normed, normed_low, inverse, preact, activated = parts
    upstream = pair_grad.astype(jnp.float32)
    branch_grad = (branch_scale * upstream).astype(jnp.bfloat16)
    act_grad = jnp.dot(branch_grad, w_out.T, preferred_element_type=jnp.float32)
    preact_grad = (act_grad * gelu_slope(preact)).astype(jnp.bfloat16)
    normed_grad = jnp.dot(preact_grad, w_in.T, preferred_element_type=jnp.float32)
    centered_grad = normed_grad - lax.optimization_barrier(jnp.mean(normed_grad, axis=-1, keepdims=True)) - normed * lax.optimization_barrier(jnp.mean(normed_grad * normed, axis=-1, keepdims=True))
    input_grad = (keep_gate * upstream + inverse * centered_grad).astype(jnp.bfloat16)
    return (input_grad, normed_low, preact_grad, activated, branch_grad)

def pair_view(state, stride):
    groups = state.shape[0] // (2 * stride)
    viewed = state.reshape(groups, 2, stride, WIDTH)
    return jnp.concatenate([viewed[:, 0], viewed[:, 1]], axis=-1).reshape(groups * stride, 2 * WIDTH)

def unpair(paired, stride):
    groups = paired.shape[0] // stride
    viewed = paired.reshape(groups, stride, 2 * WIDTH)
    return jnp.stack([viewed[:, :, :WIDTH], viewed[:, :, WIDTH:]], axis=1).reshape(groups * 2 * stride, WIDTH)

def reference(saved_input, cotangent, w_in, bias_in, w_out, residual_logit, branch_scale):
    keep_gate = jax.nn.sigmoid(residual_logit)
    current = saved_input
    stored = []
    for level in range(LEVELS):
        stride = POS_DEV * 2 ** level
        paired = pair_view(current, stride)
        stored.append(paired)
        parts = switch_parts(paired, w_in, bias_in)
        current = unpair(switch_result(paired, parts, w_out, keep_gate, branch_scale), stride)
    grad_state = cotangent
    grad_in = jnp.zeros((2 * WIDTH, w_in.shape[1]), jnp.float32)
    grad_out = jnp.zeros((w_in.shape[1], 2 * WIDTH), jnp.float32)
    for level in reversed(range(LEVELS)):
        stride = POS_DEV * 2 ** level
        parts = switch_parts(stored[level], w_in, bias_in)
        input_grad, normed_low, preact_grad, activated, branch_grad = switch_backward(pair_view(grad_state, stride), parts, w_in, w_out, keep_gate, branch_scale)
        grad_state = unpair(input_grad, stride)
        grad_in = grad_in + contract_rows(normed_low, preact_grad)
        grad_out = grad_out + contract_rows(activated, branch_grad)
    grad_scale = POSITIONS ** (-0.5)
    return (grad_state, grad_in * grad_scale, grad_out * grad_scale)
```

```python
import functools

import jax
import jax.numpy as jnp
from jax import lax
from jax.experimental import pallas as pl
from jax.experimental.pallas import tpu as pltpu
from jax.sharding import PartitionSpec as P

epsilon = 1e-05
tanh_scale = 0.7978845608028654
cubic_coef = 0.044715
f32 = jnp.float32
bf16 = jnp.bfloat16
VMEM = pl.BlockSpec(memory_space=pltpu.VMEM)
SMEM = pl.BlockSpec(memory_space=pltpu.SMEM)
tile = 16


def dot(left, right, contract):
    return lax.dot_general(left, right, ((contract[:1], contract[1:]), ((), ())), preferred_element_type=f32)


def pair_rows(state, stride):
    rows, width = state.shape
    groups = rows // (2 * stride)
    if stride >= 8:
        viewed = state.reshape(groups, 2, stride, width)
        halves = [viewed[:, side].reshape(rows // 2, width) for side in (0, 1)]
    else:
        halves = []
        for side in (0, 1):
            row = lax.broadcasted_iota(jnp.int32, (rows // 2, rows), 0)
            col = lax.broadcasted_iota(jnp.int32, (rows // 2, rows), 1)
            pick = (row // stride) * (2 * stride) + row % stride + side * stride
            halves.append(dot((col == pick).astype(bf16), state.astype(bf16), (1, 0)))
    return jnp.concatenate(halves, axis=1)


def unpair_rows(paired, stride):
    half, double = paired.shape
    width = double // 2
    groups = half // stride
    first, second = paired[:, :width], paired[:, width:]
    if stride >= 8:
        parts = [part.reshape(groups, 1, stride, width) for part in (first, second)]
        return jnp.concatenate(parts, axis=1).reshape(2 * half, width)
    total = jnp.zeros((2 * half, width), f32)
    for side, part in enumerate((first, second)):
        row = lax.broadcasted_iota(jnp.int32, (2 * half, half), 0)
        col = lax.broadcasted_iota(jnp.int32, (2 * half, half), 1)
        place = (col // stride) * (2 * stride) + col % stride + side * stride
        total = total + dot((row == place).astype(bf16), part.astype(bf16), (1, 0))
    return total


def switch_kernel(
    levels, block, me_ref, x_ref, g_ref, w_in_ref, bias_ref, w_out_ref, logit_ref, scale_ref,
    grad_ref, keep_ref, send_ref,
    low_s, act_s, slope_s, normed_s, inverse_s, pre_s, bg_s,
):
    rows, width = x_ref.shape
    half = rows // 2
    gate = jax.nn.sigmoid(logit_ref[...])
    scale = scale_ref[...]
    state = x_ref[...].astype(f32)
    for level in range(levels):
        at = pl.ds(level * half, half)
        paired = pair_rows(state, block * 2**level)
        centered = paired - jnp.mean(paired, axis=-1, keepdims=True)
        inverse = lax.rsqrt(jnp.mean(centered * centered, axis=-1, keepdims=True) + epsilon)
        normed = centered * inverse
        low = normed.astype(bf16)
        normed_s[at, :] = normed
        inverse_s[at, :] = inverse
        low_s[at, :] = low
        u = dot(low, w_in_ref[...], (1, 0)) + bias_ref[...]
        square = u * u
        tangent = jnp.tanh(tanh_scale * (u + cubic_coef * square * u))
        rise = 0.5 * (1.0 + tangent)
        act = (u * rise).astype(bf16)
        slope_s[at, :] = rise + 0.5 * u * (1.0 - tangent * tangent) * tanh_scale * (
            1.0 + 3.0 * cubic_coef * square
        )
        act_s[at, :] = act
        if level < levels - 1:
            branch = dot(act, w_out_ref[...], (1, 0))
            result = (gate * paired + scale * branch).astype(bf16).astype(f32)
            state = unpair_rows(result, block * 2**level)
    grad = g_ref[...].astype(f32)
    for level in reversed(range(levels)):
        at = pl.ds(level * half, half)
        upstream = pair_rows(grad, block * 2**level)
        branch_grad = (scale * upstream).astype(bf16)
        bg_s[at, :] = branch_grad
        act_grad = dot(branch_grad, w_out_ref[...], (1, 1))
        pre_grad = (act_grad * slope_s[at, :]).astype(bf16)
        pre_s[at, :] = pre_grad
        normed_grad = dot(pre_grad, w_in_ref[...], (1, 1))
        normed = normed_s[at, :]
        moved = (
            normed_grad
            - jnp.mean(normed_grad, axis=-1, keepdims=True)
            - normed * jnp.mean(normed_grad * normed, axis=-1, keepdims=True)
        )
        result = (gate * upstream + inverse_s[at, :] * moved).astype(bf16).astype(f32)
        grad = unpair_rows(result, block * 2**level)
    grad_ref[...] = grad.astype(bf16)
    grad_in = dot(low_s[...], pre_s[...], (0, 0))
    grad_out = dot(act_s[...], bg_s[...], (0, 0))
    double, units = grad_in.shape
    step = units // 16

    def put_in(ref):
        for piece in range(16):
            row, lane = (piece // 2) * step, (piece % 2) * double
            ref[piece * step : (piece + 1) * step, :] = grad_in[row : row + step, lane : lane + double].astype(
                ref.dtype
            )

    def put_out(ref):
        ref[...] = grad_out.astype(ref.dtype)

    core = me_ref[0] % 2

    @pl.when(core == 0)
    def _():
        put_in(keep_ref)
        put_out(send_ref)

    @pl.when(core == 1)
    def _():
        put_in(send_ref)
        put_out(keep_ref)


def split_kernel(radix, shift, me_ref, *refs):
    count = len(refs) - radix
    parts, outs = refs[:count], refs[count:]
    rows = parts[0].shape[0] // radix
    place = (me_ref[0] >> shift) & (radix - 1)
    for other in range(radix):
        at = pl.ds(pl.multiple_of((place ^ other) * rows, tile), rows)
        total = parts[0][at, :].astype(f32)
        for part in parts[1:]:
            total = total + part[at, :].astype(f32)
        outs[other][...] = total.astype(outs[other].dtype)


def total_kernel(factor, *refs):
    total = refs[0][...].astype(f32)
    for part in refs[1:-1]:
        total = total + part[...].astype(f32)
    refs[-1][...] = (total * factor).astype(refs[-1].dtype)


def place_kernel(phases, step, me_ref, mine_ref, other_ref, in_ref, out_ref):
    me = me_ref[0]
    core = me % 2
    double = mine_ref.shape[1]
    pieces = mine_ref.shape[0] // step
    base = 0
    for bit, radix in phases:
        base = base * radix + ((me >> bit) & (radix - 1))

    def write(first_ref, second_ref):
        for slot in range(pieces):
            piece = slot ^ base
            rows = pl.ds(slot * step, step)
            to = pl.ds(pl.multiple_of((piece // 2) * step, tile), step)
            lane = pl.ds(pl.multiple_of((piece % 2) * double, 128), double)
            in_ref[to, lane] = first_ref[rows, :].astype(f32)
            out_ref[pl.ds(pl.multiple_of(piece * step, tile), step), :] = second_ref[rows, :].astype(f32)

    @pl.when(core == 0)
    def _():
        write(mine_ref, other_ref)

    @pl.when(core == 1)
    def _():
        write(other_ref, mine_ref)


def call(kernel, outs, scratch=(), specs=None, count=0):
    return pl.pallas_call(
        kernel,
        out_shape=outs,
        in_specs=specs if specs is not None else [VMEM] * count,
        out_specs=jax.tree.map(lambda _: VMEM, outs),
        scratch_shapes=list(scratch),
        compiler_params=pltpu.CompilerParams(vmem_limit_bytes=40 * 2**20),
    )


def struct(shape, dtype):
    return jax.ShapeDtypeStruct(shape, dtype)


def exchange(value, masks, size):
    return [lax.ppermute(value if not isinstance(value, list) else value[i], "seq",
                         [(d, d ^ mask) for d in range(size)]) for i, mask in enumerate(masks)]


def sum_over_devices(me, keep, send, size, factor):
    bits = size.bit_length() - 1
    rows, double = keep.shape
    arrived = exchange([send], [1], size)
    parts = [keep] + arrived
    bit = 1
    phases = []
    while bit < bits and bit < 5:
        radix = 4 if bit + 1 < min(bits, 5) else 2
        phases.append((bit, radix))
        bit += 2 if radix == 4 else 1
    for bit, radix in phases:
        rows = rows // radix
        outs = [struct((rows, double), f32)] + [struct((rows, double), bf16)] * (radix - 1)
        pieces = call(
            functools.partial(split_kernel, radix, bit), outs, specs=[SMEM] + [VMEM] * len(parts)
        )(me, *parts)
        parts = [pieces[0]] + exchange(list(pieces[1:]), [m << bit for m in range(1, radix)], size)
    bit = phases[-1][0] + phases[-1][1].bit_length() - 1
    for rest in range(bit, bits):
        total = call(functools.partial(total_kernel, 1.0), struct((rows, double), bf16), count=len(parts))(*parts)
        parts = [total] + exchange([total], [1 << rest], size)
    mine = call(functools.partial(total_kernel, factor), struct((rows, double), bf16), count=len(parts))(*parts)
    for bit, radix in reversed(phases):
        got = exchange([mine] * (radix - 1), [m << bit for m in range(1, radix)], size)
        mine = jnp.concatenate([mine] + got, axis=0)
    (other,) = exchange([mine], [1], size)
    return mine, other, rows, phases


def shards(saved_input, cotangent, w_in, bias_in, w_out, residual_logit, branch_scale):
    size = lax.axis_size("seq")
    levels = size.bit_length() - 1
    rows, width = saved_input.shape
    double, units = w_in.shape
    block = rows // size
    half = rows // 2
    me = lax.axis_index("seq").astype(jnp.int32).reshape(1)
    both = jnp.concatenate(
        [saved_input.reshape(size, block, width), cotangent.reshape(size, block, width)], axis=1
    )
    both = lax.all_to_all(both, "seq", split_axis=0, concat_axis=0, tiled=True)
    state = both[:, :block].reshape(rows, width)
    grads = both[:, block:].reshape(rows, width)
    total = levels * half
    grad_state, keep, send = call(
        functools.partial(switch_kernel, levels, block),
        [struct((rows, width), bf16), struct((units, double), f32), struct((units, double), bf16)],
        scratch=[
            pltpu.VMEM((total, double), bf16),
            pltpu.VMEM((total, units), bf16),
            pltpu.VMEM((total, units), f32),
            pltpu.VMEM((total, double), f32),
            pltpu.VMEM((total, 1), f32),
            pltpu.VMEM((total, units), bf16),
            pltpu.VMEM((total, double), bf16),
        ],
        specs=[SMEM] + [VMEM] * 7,
    )(me, state, grads, w_in, bias_in.reshape(1, units), w_out, residual_logit.reshape(1, double),
      branch_scale.reshape(1, double))
    factor = float(rows * size) ** (-0.5)
    mine, other, step, phases = sum_over_devices(me, keep, send, size, factor)
    grad_state = lax.all_to_all(
        grad_state.reshape(size, block, width), "seq", split_axis=0, concat_axis=0, tiled=True
    ).reshape(rows, width)
    grad_in, grad_out = call(
        functools.partial(place_kernel, phases, step),
        [struct((double, units), f32), struct((units, double), f32)],
        specs=[SMEM, VMEM, VMEM],
    )(me, mine, other)
    return (grad_state, grad_in, grad_out)


def solution(mesh):
    in_specs = (P("seq", None), P("seq", None), P(), P(), P(), P(), P())
    out_specs = (P("seq", None), P(), P())
    return jax.shard_map(shards, mesh=mesh, in_specs=in_specs, out_specs=out_specs, check_vma=False)
```

```python
import functools

import jax
import jax.numpy as jnp
from jax import lax
from jax.experimental import pallas as pl
from jax.experimental.pallas import tpu as pltpu
from jax.sharding import PartitionSpec as P

epsilon = 1e-05
tanh_scale = 0.7978845608028654
cubic_coef = 0.044715
f32 = jnp.float32
bf16 = jnp.bfloat16
VMEM = pl.BlockSpec(memory_space=pltpu.VMEM)
SMEM = pl.BlockSpec(memory_space=pltpu.SMEM)
tile = 16


def dot(left, right, contract):
    return lax.dot_general(left, right, ((contract[:1], contract[1:]), ((), ())), preferred_element_type=f32)


def pair_rows(state, stride):
    rows, width = state.shape
    groups = rows // (2 * stride)
    if stride >= 8:
        viewed = state.reshape(groups, 2, stride, width)
        halves = [viewed[:, side].reshape(rows // 2, width) for side in (0, 1)]
    else:
        halves = []
        for side in (0, 1):
            row = lax.broadcasted_iota(jnp.int32, (rows // 2, rows), 0)
            col = lax.broadcasted_iota(jnp.int32, (rows // 2, rows), 1)
            pick = (row // stride) * (2 * stride) + row % stride + side * stride
            halves.append(dot((col == pick).astype(bf16), state.astype(bf16), (1, 0)))
    return jnp.concatenate(halves, axis=1)


def unpair_rows(paired, stride):
    half, double = paired.shape
    width = double // 2
    groups = half // stride
    first, second = paired[:, :width], paired[:, width:]
    if stride >= 8:
        parts = [part.reshape(groups, 1, stride, width) for part in (first, second)]
        return jnp.concatenate(parts, axis=1).reshape(2 * half, width)
    total = jnp.zeros((2 * half, width), f32)
    for side, part in enumerate((first, second)):
        row = lax.broadcasted_iota(jnp.int32, (2 * half, half), 0)
        col = lax.broadcasted_iota(jnp.int32, (2 * half, half), 1)
        place = (col // stride) * (2 * stride) + col % stride + side * stride
        total = total + dot((row == place).astype(bf16), part.astype(bf16), (1, 0))
    return total


def pack_kernel(x_ref, g_ref, out_ref):
    size, both, width = out_ref.shape
    for side, ref in enumerate((x_ref, g_ref)):
        rows = ref[...].astype(f32).reshape(size, both // 2, width)
        if side == 0:
            first = rows
        else:
            out_ref[...] = jnp.concatenate([first, rows], axis=1).astype(bf16)


def switch_kernel(
    levels, block, me_ref, both_ref, w_in_ref, bias_ref, w_out_ref, logit_ref, scale_ref,
    grad_ref, keep_ref, send_ref,
    low_s, act_s, slope_s, normed_s, inverse_s, pre_s, bg_s,
):
    rows, width = grad_ref.shape
    half = rows // 2
    both = both_ref[...].astype(f32)
    gate = jax.nn.sigmoid(logit_ref[...])
    scale = scale_ref[...]
    state = both[:, :block].reshape(rows, width)
    for level in range(levels):
        at = pl.ds(level * half, half)
        paired = pair_rows(state, block * 2**level)
        centered = paired - jnp.mean(paired, axis=-1, keepdims=True)
        inverse = lax.rsqrt(jnp.mean(centered * centered, axis=-1, keepdims=True) + epsilon)
        normed = centered * inverse
        low = normed.astype(bf16)
        normed_s[at, :] = normed
        inverse_s[at, :] = inverse
        low_s[at, :] = low
        u = dot(low, w_in_ref[...], (1, 0)) + bias_ref[...]
        square = u * u
        tangent = jnp.tanh(tanh_scale * (u + cubic_coef * square * u))
        rise = 0.5 * (1.0 + tangent)
        act = (u * rise).astype(bf16)
        slope_s[at, :] = rise + 0.5 * u * (1.0 - tangent * tangent) * tanh_scale * (
            1.0 + 3.0 * cubic_coef * square
        )
        act_s[at, :] = act
        if level < levels - 1:
            branch = dot(act, w_out_ref[...], (1, 0))
            result = (gate * paired + scale * branch).astype(bf16).astype(f32)
            state = unpair_rows(result, block * 2**level)
    grad = both[:, block:].reshape(rows, width)
    for level in reversed(range(levels)):
        at = pl.ds(level * half, half)
        upstream = pair_rows(grad, block * 2**level)
        branch_grad = (scale * upstream).astype(bf16)
        bg_s[at, :] = branch_grad
        act_grad = dot(branch_grad, w_out_ref[...], (1, 1))
        pre_grad = (act_grad * slope_s[at, :]).astype(bf16)
        pre_s[at, :] = pre_grad
        normed_grad = dot(pre_grad, w_in_ref[...], (1, 1))
        normed = normed_s[at, :]
        moved = (
            normed_grad
            - jnp.mean(normed_grad, axis=-1, keepdims=True)
            - normed * jnp.mean(normed_grad * normed, axis=-1, keepdims=True)
        )
        result = (gate * upstream + inverse_s[at, :] * moved).astype(bf16).astype(f32)
        grad = unpair_rows(result, block * 2**level)
    grad_ref[...] = grad.astype(bf16)
    grad_in = dot(low_s[...], pre_s[...], (0, 0))
    grad_out = dot(act_s[...], bg_s[...], (0, 0))
    double, units = grad_in.shape
    step = units // 16

    def put_in(ref):
        for piece in range(16):
            row, lane = (piece // 2) * step, (piece % 2) * double
            ref[piece * step : (piece + 1) * step, :] = grad_in[row : row + step, lane : lane + double].astype(
                ref.dtype
            )

    def put_out(ref):
        ref[...] = grad_out.astype(ref.dtype)

    core = me_ref[0] % 2

    @pl.when(core == 0)
    def _():
        put_in(keep_ref)
        put_out(send_ref)

    @pl.when(core == 1)
    def _():
        put_in(send_ref)
        put_out(keep_ref)


def split_kernel(radix, shift, me_ref, *refs):
    count = len(refs) - radix
    parts, outs = refs[:count], refs[count:]
    rows = parts[0].shape[0] // radix
    place = (me_ref[0] >> shift) & (radix - 1)
    for other in range(radix):
        at = pl.ds(pl.multiple_of((place ^ other) * rows, tile), rows)
        total = parts[0][at, :].astype(f32)
        for part in parts[1:]:
            total = total + part[at, :].astype(f32)
        outs[other][...] = total.astype(outs[other].dtype)


def total_kernel(factor, *refs):
    total = refs[0][...].astype(f32)
    for part in refs[1:-1]:
        total = total + part[...].astype(f32)
    refs[-1][...] = (total * factor).astype(refs[-1].dtype)


def place_kernel(phases, step, me_ref, mine_ref, other_ref, in_ref, out_ref):
    me = me_ref[0]
    core = me % 2
    double = mine_ref.shape[1]
    pieces = mine_ref.shape[0] // step
    base = 0
    for bit, radix in phases:
        base = base * radix + ((me >> bit) & (radix - 1))

    def write(first_ref, second_ref):
        for slot in range(pieces):
            piece = slot ^ base
            rows = pl.ds(slot * step, step)
            to = pl.ds(pl.multiple_of((piece // 2) * step, tile), step)
            lane = pl.ds(pl.multiple_of((piece % 2) * double, 128), double)
            in_ref[to, lane] = first_ref[rows, :].astype(f32)
            out_ref[pl.ds(pl.multiple_of(piece * step, tile), step), :] = second_ref[rows, :].astype(f32)

    @pl.when(core == 0)
    def _():
        write(mine_ref, other_ref)

    @pl.when(core == 1)
    def _():
        write(other_ref, mine_ref)


def call(kernel, outs, scratch=(), specs=None, count=0):
    return pl.pallas_call(
        kernel,
        out_shape=outs,
        in_specs=specs if specs is not None else [VMEM] * count,
        out_specs=jax.tree.map(lambda _: VMEM, outs),
        scratch_shapes=list(scratch),
        compiler_params=pltpu.CompilerParams(vmem_limit_bytes=40 * 2**20),
    )


def struct(shape, dtype):
    return jax.ShapeDtypeStruct(shape, dtype)


def exchange(value, masks, size):
    return [lax.ppermute(value if not isinstance(value, list) else value[i], "seq",
                         [(d, d ^ mask) for d in range(size)]) for i, mask in enumerate(masks)]


def sum_over_devices(me, keep, send, size, factor, beside):
    bits = size.bit_length() - 1
    rows, double = keep.shape
    arrived = exchange([send], [1], size)
    parts = [keep] + arrived
    bit = 1
    phases = []
    while bit < bits and bit < 5:
        radix = 4 if bit + 1 < min(bits, 5) else 2
        phases.append((bit, radix))
        bit += 2 if radix == 4 else 1
    for bit, radix in phases:
        rows = rows // radix
        outs = [struct((rows, double), f32)] + [struct((rows, double), bf16)] * (radix - 1)
        pieces = call(
            functools.partial(split_kernel, radix, bit), outs, specs=[SMEM] + [VMEM] * len(parts)
        )(me, *parts)
        parts = [pieces[0]] + exchange(list(pieces[1:]), [m << bit for m in range(1, radix)], size)
    bit = phases[-1][0] + phases[-1][1].bit_length() - 1
    for rest in range(bit, bits):
        total = call(functools.partial(total_kernel, 1.0), struct((rows, double), bf16), count=len(parts))(*parts)
        parts = [total] + exchange([total], [1 << rest], size)
    mine = call(functools.partial(total_kernel, factor), struct((rows, double), bf16), count=len(parts))(*parts)
    mine, beside = lax.optimization_barrier((mine, beside))
    for bit, radix in reversed(phases):
        got = exchange([mine] * (radix - 1), [m << bit for m in range(1, radix)], size)
        mine = jnp.concatenate([mine] + got, axis=0)
    (other,) = exchange([mine], [1], size)
    return mine, other, rows, phases, beside


def shards(saved_input, cotangent, w_in, bias_in, w_out, residual_logit, branch_scale):
    size = lax.axis_size("seq")
    levels = size.bit_length() - 1
    rows, width = saved_input.shape
    double, units = w_in.shape
    block = rows // size
    half = rows // 2
    me = lax.axis_index("seq").astype(jnp.int32).reshape(1)
    if block % 8 == 0:
        both = call(pack_kernel, struct((size, 2 * block, width), bf16), count=2)(saved_input, cotangent)
    else:
        both = jnp.concatenate(
            [saved_input.reshape(size, block, width), cotangent.reshape(size, block, width)], axis=1
        )
    both = lax.all_to_all(both, "seq", split_axis=0, concat_axis=0, tiled=True)
    total = levels * half
    grad_state, keep, send = call(
        functools.partial(switch_kernel, levels, block),
        [struct((rows, width), bf16), struct((units, double), f32), struct((units, double), bf16)],
        scratch=[
            pltpu.VMEM((total, double), bf16),
            pltpu.VMEM((total, units), bf16),
            pltpu.VMEM((total, units), f32),
            pltpu.VMEM((total, double), f32),
            pltpu.VMEM((total, 1), f32),
            pltpu.VMEM((total, units), bf16),
            pltpu.VMEM((total, double), bf16),
        ],
        specs=[SMEM] + [VMEM] * 6,
    )(me, both, w_in, bias_in.reshape(1, units), w_out, residual_logit.reshape(1, double),
      branch_scale.reshape(1, double))
    factor = float(rows * size) ** (-0.5)
    grad_state = lax.all_to_all(
        grad_state.reshape(size, block, width), "seq", split_axis=0, concat_axis=0, tiled=True
    ).reshape(rows, width)
    mine, other, step, phases, grad_state = sum_over_devices(me, keep, send, size, factor, grad_state)
    grad_in, grad_out = call(
        functools.partial(place_kernel, phases, step),
        [struct((double, units), f32), struct((units, double), f32)],
        specs=[SMEM, VMEM, VMEM],
    )(me, mine, other)
    return (grad_state, grad_in, grad_out)


def solution(mesh):
    in_specs = (P("seq", None), P("seq", None), P(), P(), P(), P(), P())
    out_specs = (P("seq", None), P(), P())
    return jax.shard_map(shards, mesh=mesh, in_specs=in_specs, out_specs=out_specs, check_vma=False)
```

```python
import functools

import jax
import jax.numpy as jnp
from jax import lax
from jax.experimental import pallas as pl
from jax.experimental.pallas import tpu as pltpu
from jax.sharding import PartitionSpec as P

epsilon = 1e-05
tanh_scale = 0.7978845608028654
cubic_coef = 0.044715
f32 = jnp.float32
bf16 = jnp.bfloat16
VMEM = pl.BlockSpec(memory_space=pltpu.VMEM)
SMEM = pl.BlockSpec(memory_space=pltpu.SMEM)
tile = 16


def dot(left, right, contract):
    return lax.dot_general(left, right, ((contract[:1], contract[1:]), ((), ())), preferred_element_type=f32)


def pair_rows(state, stride):
    rows, width = state.shape
    groups = rows // (2 * stride)
    if stride >= 8:
        viewed = state.reshape(groups, 2, stride, width)
        halves = [viewed[:, side].reshape(rows // 2, width) for side in (0, 1)]
    else:
        halves = []
        for side in (0, 1):
            row = lax.broadcasted_iota(jnp.int32, (rows // 2, rows), 0)
            col = lax.broadcasted_iota(jnp.int32, (rows // 2, rows), 1)
            pick = (row // stride) * (2 * stride) + row % stride + side * stride
            halves.append(dot((col == pick).astype(bf16), state.astype(bf16), (1, 0)))
    return jnp.concatenate(halves, axis=1)


def unpair_rows(paired, stride):
    half, double = paired.shape
    width = double // 2
    groups = half // stride
    first, second = paired[:, :width], paired[:, width:]
    if stride >= 8:
        parts = [part.reshape(groups, 1, stride, width) for part in (first, second)]
        return jnp.concatenate(parts, axis=1).reshape(2 * half, width)
    total = jnp.zeros((2 * half, width), f32)
    for side, part in enumerate((first, second)):
        row = lax.broadcasted_iota(jnp.int32, (2 * half, half), 0)
        col = lax.broadcasted_iota(jnp.int32, (2 * half, half), 1)
        place = (col // stride) * (2 * stride) + col % stride + side * stride
        total = total + dot((row == place).astype(bf16), part.astype(bf16), (1, 0))
    return total


def pack_kernel(x_ref, g_ref, out_ref):
    size, both, width = out_ref.shape
    for side, ref in enumerate((x_ref, g_ref)):
        rows = ref[...].astype(f32).T.reshape(size, both // 2, width)
        if side == 0:
            first = rows
        else:
            out_ref[...] = jnp.concatenate([first, rows], axis=1).astype(bf16)


def switch_kernel(
    levels, block, me_ref, both_ref, w_in_ref, bias_ref, w_out_ref, logit_ref, scale_ref,
    grad_ref, keep_ref, send_ref,
    low_s, act_s, slope_s, normed_s, inverse_s, pre_s, bg_s, paired_s,
):
    half, double = paired_s.shape
    rows, width = 2 * half, double // 2
    units = bias_ref.shape[1]
    riding = send_ref.shape[0] > units
    core = me_ref[0] % 2
    both = both_ref[...].astype(f32)
    gate = jax.nn.sigmoid(logit_ref[...])
    scale = scale_ref[...]
    state = both[:, :block].reshape(rows, width)
    for level in range(levels):
        at = pl.ds(level * half, half)
        paired = pair_rows(state, block * 2**level)
        centered = paired - jnp.mean(paired, axis=-1, keepdims=True)
        inverse = lax.rsqrt(jnp.mean(centered * centered, axis=-1, keepdims=True) + epsilon)
        normed = centered * inverse
        low = normed.astype(bf16)
        normed_s[at, :] = normed
        inverse_s[at, :] = inverse
        low_s[at, :] = low
        u = dot(low, w_in_ref[...], (1, 0)) + bias_ref[...]
        square = u * u
        tangent = jnp.tanh(tanh_scale * (u + cubic_coef * square * u))
        rise = 0.5 * (1.0 + tangent)
        act = (u * rise).astype(bf16)
        slope_s[at, :] = rise + 0.5 * u * (1.0 - tangent * tangent) * tanh_scale * (
            1.0 + 3.0 * cubic_coef * square
        )
        act_s[at, :] = act
        if level < levels - 1:
            branch = dot(act, w_out_ref[...], (1, 0))
            result = (gate * paired + scale * branch).astype(bf16).astype(f32)
            state = unpair_rows(result, block * 2**level)
    grad = both[:, block:].reshape(rows, width)
    for level in reversed(range(levels)):
        at = pl.ds(level * half, half)
        upstream = pair_rows(grad, block * 2**level)
        branch_grad = (scale * upstream).astype(bf16)
        bg_s[at, :] = branch_grad
        act_grad = dot(branch_grad, w_out_ref[...], (1, 1))
        pre_grad = (act_grad * slope_s[at, :]).astype(bf16)
        pre_s[at, :] = pre_grad
        normed_grad = dot(pre_grad, w_in_ref[...], (1, 1))
        normed = normed_s[at, :]
        moved = (
            normed_grad
            - jnp.mean(normed_grad, axis=-1, keepdims=True)
            - normed * jnp.mean(normed_grad * normed, axis=-1, keepdims=True)
        )
        result = (gate * upstream + inverse_s[at, :] * moved).astype(bf16).astype(f32)
        if level > 0 or not riding:
            grad = unpair_rows(result, block * 2**level)
    if riding:
        turned = jnp.concatenate([result[:, width:], result[:, :width]], axis=1)
        paired_s[...] = jnp.where(core == 0, result, turned)
        pairs = half // block
        kept, sent = [], []
        for plane in range(4):
            for low in range(pairs // 8):
                sides = []
                for high in range(2):
                    chip = ((high * (pairs // 8) + low) * 4 + plane) ^ (me_ref[0] >> 1)
                    sides.append(paired_s[pl.ds(pl.multiple_of(chip * block, 8), block), :])
                kept.append(jnp.concatenate([side[:, :width] for side in sides], axis=1))
                sent.append(jnp.concatenate([side[:, width:] for side in sides], axis=1))
        grad_ref[...] = jnp.concatenate(kept, axis=0).astype(bf16)
        send_ref[units:, :] = jnp.concatenate(sent, axis=0).astype(bf16)
    else:
        grad_ref[...] = grad.astype(bf16)
    grad_in = dot(low_s[...], pre_s[...], (0, 0))
    grad_out = dot(act_s[...], bg_s[...], (0, 0))
    step = units // 16

    def put_in(ref):
        for piece in range(16):
            row, lane = (piece // 2) * step, (piece % 2) * double
            ref[piece * step : (piece + 1) * step, :] = grad_in[row : row + step, lane : lane + double].astype(
                ref.dtype
            )

    def put_out(ref):
        ref[0:units, :] = grad_out.astype(ref.dtype)

    @pl.when(core == 0)
    def _():
        put_in(keep_ref)
        put_out(send_ref)

    @pl.when(core == 1)
    def _():
        put_in(send_ref)
        put_out(keep_ref)


def split_kernel(radix, shift, cut, me_ref, *refs):
    count = len(refs) - radix - (cut is not None)
    parts, outs = refs[:count], refs[count:]
    rows = outs[0].shape[0]
    if cut is not None:
        ride_ref, parts = parts[0], parts[1:]
        riders = cut(ride_ref, [part.at[rows * radix :, :] for part in parts[1:]])
        outs[-1][...] = riders[0]
        for other in range(1, radix):
            outs[other][rows:, :] = riders[other]
    place = (me_ref[0] >> shift) & (radix - 1)
    for other in range(radix):
        at = pl.ds(pl.multiple_of((place ^ other) * rows, tile), rows)
        total = parts[0][at, :].astype(f32)
        for part in parts[1:]:
            total = total + part[at, :].astype(f32)
        outs[other][0:rows, :] = total.astype(outs[other].dtype)


def cut_planes(kept_ref, arrived):
    rows = kept_ref.shape[0] // 4
    sources = [kept_ref[...], arrived[0][...]]
    return [jnp.concatenate([source[m * rows : (m + 1) * rows] for source in sources], axis=0) for m in range(4)]


def cut_lines(kept_ref, arrived):
    sources = [ref[...].astype(f32) for ref in [kept_ref] + arrived]
    rows, double = sources[0].shape
    width, block = double // 2, rows // 4
    pieces = []
    for high in range(2):
        for low in range(2):
            sides = []
            for side in range(2):
                blocks = []
                for source in sources[2 * side : 2 * side + 2]:
                    for core in range(2):
                        first = (core * 2 + low) * block
                        blocks.append(source[first : first + block, high * width : (high + 1) * width])
                sides.append(jnp.concatenate(blocks, axis=0))
            pieces.append(jnp.concatenate(sides, axis=1).astype(bf16))
    return pieces


def unpack_kernel(block, me_ref, *refs):
    parts, out_ref, rows_s = refs[:-2], refs[-2], refs[-1]
    width = rows_s.shape[1]
    for line, part in enumerate(parts):
        values = part[part.shape[0] - 4 * block :, :].astype(f32)
        for plane in range(4):
            for core in range(2):
                source = me_ref[0] ^ (line * 8 + plane * 2 + core)
                first = ((plane % 2) * 2 + core) * block
                side = plane // 2
                rows_s[pl.ds(pl.multiple_of(source * block, 8), block), :] = values[
                    first : first + block, side * width : (side + 1) * width
                ]
    out_ref[...] = rows_s[...].T.astype(bf16)


def total_kernel(factor, *refs):
    rows = refs[0].shape[0]
    total = refs[0][...].astype(f32)
    for part in refs[1:-1]:
        total = total + part[0:rows, :].astype(f32)
    refs[-1][...] = (total * factor).astype(refs[-1].dtype)


def place_kernel(phases, step, me_ref, mine_ref, other_ref, in_ref, out_ref):
    me = me_ref[0]
    core = me % 2
    double = mine_ref.shape[1]
    pieces = mine_ref.shape[0] // step
    base = 0
    for bit, radix in phases:
        base = base * radix + ((me >> bit) & (radix - 1))

    def write(first_ref, second_ref):
        for slot in range(pieces):
            piece = slot ^ base
            rows = pl.ds(slot * step, step)
            to = pl.ds(pl.multiple_of((piece // 2) * step, tile), step)
            lane = pl.ds(pl.multiple_of((piece % 2) * double, 128), double)
            in_ref[to, lane] = first_ref[rows, :].astype(f32)
            out_ref[pl.ds(pl.multiple_of(piece * step, tile), step), :] = second_ref[rows, :].astype(f32)

    @pl.when(core == 0)
    def _():
        write(mine_ref, other_ref)

    @pl.when(core == 1)
    def _():
        write(other_ref, mine_ref)


def call(kernel, outs, scratch=(), specs=None, count=0):
    return pl.pallas_call(
        kernel,
        out_shape=outs,
        in_specs=specs if specs is not None else [VMEM] * count,
        out_specs=jax.tree.map(lambda _: VMEM, outs),
        scratch_shapes=list(scratch),
        compiler_params=pltpu.CompilerParams(vmem_limit_bytes=40 * 2**20),
    )


def struct(shape, dtype):
    return jax.ShapeDtypeStruct(shape, dtype)


def exchange(value, masks, size):
    return [lax.ppermute(value if not isinstance(value, list) else value[i], "seq",
                         [(d, d ^ mask) for d in range(size)]) for i, mask in enumerate(masks)]


def phases_of(size, units):
    bits = size.bit_length() - 1
    phases, bit, rows = [], 1, units
    while bit < bits and rows % (2 * tile) == 0:
        radix = 4 if bit + 1 < bits and rows % (4 * tile) == 0 else 2
        phases.append((bit, radix))
        rows //= radix
        bit += radix.bit_length() - 1
    return phases, bit


def sum_over_devices(me, ride, keep, send, size, factor, riding):
    bits = size.bit_length() - 1
    rows, double = keep.shape
    phases, bit = phases_of(size, rows)
    riding_rows = ride.shape[0] // 2
    parts = [keep] + exchange([send], [1], size)
    for phase, (low, radix) in enumerate(phases):
        rows = rows // radix
        cut = (cut_planes, cut_lines)[phase] if riding else None
        extra = riding_rows if riding else 0
        outs = [struct((rows, double), f32)] + [struct((rows + extra, double), bf16)] * (radix - 1)
        if riding:
            outs.append(struct((extra, double), bf16))
            parts = [ride] + parts
        pieces = call(
            functools.partial(split_kernel, radix, low, cut), outs, specs=[SMEM] + [VMEM] * len(parts)
        )(me, *parts)
        ride = pieces[-1] if riding else ride
        parts = [pieces[0]] + exchange(list(pieces[1:radix]), [m << low for m in range(1, radix)], size)
    riders = [ride] + parts[1:]
    for rest in range(bit, bits):
        total = call(functools.partial(total_kernel, 1.0), struct((rows, double), bf16), count=len(parts))(*parts)
        parts = [total] + exchange([total], [1 << rest], size)
    mine = call(functools.partial(total_kernel, factor), struct((rows, double), bf16), count=len(parts))(*parts)
    if not riding:
        mine, ride = lax.optimization_barrier((mine, ride))
    for low, radix in reversed(phases):
        got = exchange([mine] * (radix - 1), [m << low for m in range(1, radix)], size)
        mine = jnp.concatenate([mine] + got, axis=0)
    (other,) = exchange([mine], [1], size)
    return mine, other, rows, phases, riders if riding else ride


def shards(saved_input, cotangent, w_in, bias_in, w_out, residual_logit, branch_scale):
    size = lax.axis_size("seq")
    levels = size.bit_length() - 1
    rows, width = saved_input.shape
    double, units = w_in.shape
    block = rows // size
    half = rows // 2
    me = lax.axis_index("seq").astype(jnp.int32).reshape(1)
    if block % 8 == 0:
        both = call(pack_kernel, struct((size, 2 * block, width), bf16), count=2)(saved_input.T, cotangent.T)
    else:
        both = jnp.concatenate(
            [saved_input.reshape(size, block, width), cotangent.reshape(size, block, width)], axis=1
        )
    both = lax.all_to_all(both, "seq", split_axis=0, concat_axis=0, tiled=True)
    total = levels * half
    phases, bit = phases_of(size, units)
    riding = block % 8 == 0 and [radix for _, radix in phases] == [4, 4] and bit == levels
    rider = struct((rows // 4, double), bf16)
    grad_state, keep, send = call(
        functools.partial(switch_kernel, levels, block),
        [
            rider if riding else struct((rows, width), bf16),
            struct((units, double), f32),
            struct((units + rider.shape[0] * riding, double), bf16),
        ],
        scratch=[
            pltpu.VMEM((total, double), bf16),
            pltpu.VMEM((total, units), bf16),
            pltpu.VMEM((total, units), f32),
            pltpu.VMEM((total, double), f32),
            pltpu.VMEM((total, 1), f32),
            pltpu.VMEM((total, units), bf16),
            pltpu.VMEM((total, double), bf16),
            pltpu.VMEM((half, double), f32),
        ],
        specs=[SMEM] + [VMEM] * 6,
    )(me, both, w_in, bias_in.reshape(1, units), w_out, residual_logit.reshape(1, double),
      branch_scale.reshape(1, double))
    factor = float(rows * size) ** (-0.5)
    if not riding:
        grad_state = lax.all_to_all(
            grad_state.reshape(size, block, width), "seq", split_axis=0, concat_axis=0, tiled=True
        ).reshape(rows, width)
    mine, other, step, phases, grad_state = sum_over_devices(me, grad_state, keep, send, size, factor, riding)
    if riding:
        grad_state = call(
            functools.partial(unpack_kernel, block),
            struct((width, rows), bf16),
            scratch=[pltpu.VMEM((rows, width), f32)],
            specs=[SMEM] + [VMEM] * len(grad_state),
        )(me, *grad_state).T
    grad_in, grad_out = call(
        functools.partial(place_kernel, phases, step),
        [struct((double, units), f32), struct((units, double), f32)],
        specs=[SMEM, VMEM, VMEM],
    )(me, mine, other)
    return (grad_state, grad_in, grad_out)


def solution(mesh):
    in_specs = (P("seq", None), P("seq", None), P(), P(), P(), P(), P())
    out_specs = (P("seq", None), P(), P())
    return jax.shard_map(shards, mesh=mesh, in_specs=in_specs, out_specs=out_specs, check_vma=False)
```

```python
import functools

import jax
import jax.numpy as jnp
from jax import lax
from jax.experimental import pallas as pl
from jax.experimental.pallas import tpu as pltpu
from jax.sharding import PartitionSpec as P

epsilon = 1e-05
tanh_scale = 0.7978845608028654
cubic_coef = 0.044715
f32 = jnp.float32
bf16 = jnp.bfloat16
VMEM = pl.BlockSpec(memory_space=pltpu.VMEM)
SMEM = pl.BlockSpec(memory_space=pltpu.SMEM)
HBM = pl.BlockSpec(memory_space=pltpu.HBM)
tile = 16


def dot(left, right, contract):
    return lax.dot_general(left, right, ((contract[:1], contract[1:]), ((), ())), preferred_element_type=f32)


def pair_rows(state, stride):
    rows, width = state.shape
    groups = rows // (2 * stride)
    if stride >= 8:
        viewed = state.reshape(groups, 2, stride, width)
        halves = [viewed[:, side].reshape(rows // 2, width) for side in (0, 1)]
    else:
        halves = []
        for side in (0, 1):
            row = lax.broadcasted_iota(jnp.int32, (rows // 2, rows), 0)
            col = lax.broadcasted_iota(jnp.int32, (rows // 2, rows), 1)
            pick = (row // stride) * (2 * stride) + row % stride + side * stride
            halves.append(dot((col == pick).astype(bf16), state.astype(bf16), (1, 0)))
    return jnp.concatenate(halves, axis=1)


def unpair_rows(paired, stride):
    half, double = paired.shape
    width = double // 2
    groups = half // stride
    first, second = paired[:, :width], paired[:, width:]
    if stride >= 8:
        parts = [part.reshape(groups, 1, stride, width) for part in (first, second)]
        return jnp.concatenate(parts, axis=1).reshape(2 * half, width)
    total = jnp.zeros((2 * half, width), f32)
    for side, part in enumerate((first, second)):
        row = lax.broadcasted_iota(jnp.int32, (2 * half, half), 0)
        col = lax.broadcasted_iota(jnp.int32, (2 * half, half), 1)
        place = (col // stride) * (2 * stride) + col % stride + side * stride
        total = total + dot((row == place).astype(bf16), part.astype(bf16), (1, 0))
    return total


def pack_kernel(x_ref, g_ref, out_ref, x_s, g_s, sem):
    size, both, width = out_ref.shape
    copies = [
        pltpu.make_async_copy(ref, scratch, sem.at[side])
        for side, (ref, scratch) in enumerate(((x_ref, x_s), (g_ref, g_s)))
    ]
    for copy in copies:
        copy.start()
    parts = []
    for copy, scratch in zip(copies, (x_s, g_s)):
        copy.wait()
        parts.append(scratch[...].astype(f32).T.reshape(size, both // 2, width))
    out_ref[...] = jnp.concatenate(parts, axis=1).astype(bf16)


def switch_kernel(
    levels, block, me_ref, both_ref, w_in_ref, bias_ref, w_out_ref, logit_ref, scale_ref,
    grad_ref, keep_ref, send_ref,
    low_s, act_s, slope_s, normed_s, inverse_s, pre_s, bg_s, paired_s,
):
    half, double = paired_s.shape
    rows, width = 2 * half, double // 2
    units = bias_ref.shape[1]
    riding = send_ref.shape[0] > units
    core = me_ref[0] % 2
    both = both_ref[...].astype(f32)
    gate = jax.nn.sigmoid(logit_ref[...])
    scale = scale_ref[...]
    state = both[:, :block].reshape(rows, width)
    for level in range(levels):
        at = pl.ds(level * half, half)
        paired = pair_rows(state, block * 2**level)
        centered = paired - jnp.mean(paired, axis=-1, keepdims=True)
        inverse = lax.rsqrt(jnp.mean(centered * centered, axis=-1, keepdims=True) + epsilon)
        normed = centered * inverse
        low = normed.astype(bf16)
        normed_s[at, :] = normed
        inverse_s[at, :] = inverse
        low_s[at, :] = low
        u = dot(low, w_in_ref[...], (1, 0)) + bias_ref[...]
        square = u * u
        tangent = jnp.tanh(tanh_scale * (u + cubic_coef * square * u))
        rise = 0.5 * (1.0 + tangent)
        act = (u * rise).astype(bf16)
        slope_s[at, :] = rise + 0.5 * u * (1.0 - tangent * tangent) * tanh_scale * (
            1.0 + 3.0 * cubic_coef * square
        )
        act_s[at, :] = act
        if level < levels - 1:
            branch = dot(act, w_out_ref[...], (1, 0))
            result = (gate * paired + scale * branch).astype(bf16).astype(f32)
            state = unpair_rows(result, block * 2**level)
    grad = both[:, block:].reshape(rows, width)
    for level in reversed(range(levels)):
        at = pl.ds(level * half, half)
        upstream = pair_rows(grad, block * 2**level)
        branch_grad = (scale * upstream).astype(bf16)
        bg_s[at, :] = branch_grad
        act_grad = dot(branch_grad, w_out_ref[...], (1, 1))
        pre_grad = (act_grad * slope_s[at, :]).astype(bf16)
        pre_s[at, :] = pre_grad
        normed_grad = dot(pre_grad, w_in_ref[...], (1, 1))
        normed = normed_s[at, :]
        moved = (
            normed_grad
            - jnp.mean(normed_grad, axis=-1, keepdims=True)
            - normed * jnp.mean(normed_grad * normed, axis=-1, keepdims=True)
        )
        result = (gate * upstream + inverse_s[at, :] * moved).astype(bf16).astype(f32)
        if level > 0 or not riding:
            grad = unpair_rows(result, block * 2**level)
    if riding:
        turned = jnp.concatenate([result[:, width:], result[:, :width]], axis=1)
        paired_s[...] = jnp.where(core == 0, result, turned)
        pairs = half // block
        kept, sent = [], []
        for plane in range(4):
            for low in range(pairs // 8):
                sides = []
                for high in range(2):
                    chip = ((high * (pairs // 8) + low) * 4 + plane) ^ (me_ref[0] >> 1)
                    sides.append(paired_s[pl.ds(pl.multiple_of(chip * block, 8), block), :])
                kept.append(jnp.concatenate([side[:, :width] for side in sides], axis=1))
                sent.append(jnp.concatenate([side[:, width:] for side in sides], axis=1))
        grad_ref[...] = jnp.concatenate(kept, axis=0).astype(bf16)
        send_ref[units:, :] = jnp.concatenate(sent, axis=0).astype(bf16)
    else:
        grad_ref[...] = grad.astype(bf16)
    grad_in = dot(low_s[...], pre_s[...], (0, 0))
    grad_out = dot(act_s[...], bg_s[...], (0, 0))

    def put_in(ref):
        for first in range(0, units, double):
            ref[first : first + double, :] = grad_in[:, first : first + double].astype(ref.dtype)

    def put_out(ref):
        ref[0:units, :] = grad_out.astype(ref.dtype)

    @pl.when(core == 0)
    def _():
        put_in(keep_ref)
        put_out(send_ref)

    @pl.when(core == 1)
    def _():
        put_in(send_ref)
        put_out(keep_ref)


def split_kernel(radix, shift, riding, me_ref, *refs):
    count = 2 + riding
    parts, outs = refs[:count], refs[count:]
    rows = outs[0].shape[0]
    if riding:
        ride_ref, parts = parts[0], parts[1:]
        sources = [ride_ref[...], parts[1][rows * radix :, :]]
        each = ride_ref.shape[0] // radix
        for other in range(radix):
            riders = jnp.concatenate([source[other * each : (other + 1) * each] for source in sources], axis=0)
            if other == 0:
                outs[-1][...] = riders
            else:
                outs[other][rows:, :] = riders
    place = (me_ref[0] >> shift) & (radix - 1)
    for other in range(radix):
        at = pl.ds(pl.multiple_of((place ^ other) * rows, tile), rows)
        total = parts[0][at, :].astype(f32) + parts[1][at, :].astype(f32)
        outs[other][0:rows, :] = total.astype(outs[other].dtype)


def lines_kernel(*refs):
    parts, outs = refs[:4], refs[4:]
    rows, double = parts[0].shape
    sources = [part[part.shape[0] - rows :, :].astype(f32) for part in parts]
    width, block = double // 2, rows // 4
    for high in range(2):
        for low in range(2):
            sides = []
            for side in range(2):
                blocks = []
                for source in sources[2 * side : 2 * side + 2]:
                    for core in range(2):
                        first = (core * 2 + low) * block
                        blocks.append(source[first : first + block, high * width : (high + 1) * width])
                sides.append(jnp.concatenate(blocks, axis=0))
            outs[high * 2 + low][...] = jnp.concatenate(sides, axis=1).astype(bf16)


def unpack_kernel(block, me_ref, *refs):
    parts, out_ref, rows_s = refs[:-2], refs[-2], refs[-1]
    width = rows_s.shape[1]
    for line, part in enumerate(parts):
        values = part[part.shape[0] - 4 * block :, :].astype(f32)
        for plane in range(4):
            for core in range(2):
                source = me_ref[0] ^ (line * 8 + plane * 2 + core)
                first = ((plane % 2) * 2 + core) * block
                side = plane // 2
                rows_s[pl.ds(pl.multiple_of(source * block, 8), block), :] = values[
                    first : first + block, side * width : (side + 1) * width
                ]
    out_ref[...] = rows_s[...].T.astype(bf16)


def total_kernel(factor, *refs):
    rows = refs[0].shape[0]
    total = refs[0][...].astype(f32)
    for part in refs[1:-1]:
        total = total + part[0:rows, :].astype(f32)
    refs[-1][...] = (total * factor).astype(refs[-1].dtype)


def place_kernel(phases, step, other, me_ref, half_ref, *refs):
    in_ref, out_ref, wide_s, sem = refs[-4:]
    me = me_ref[0]
    double = half_ref.shape[1]
    pieces = half_ref.shape[0] // step
    base = 0
    for bit, radix in phases:
        base = base * radix + ((me >> bit) & (radix - 1))

    def targets(side):
        for slot in range(pieces):
            first = (slot ^ base) * step
            rows = pl.ds(slot * step, step)
            if side == 0:
                lane = (first // double) * double
                to = in_ref.at[
                    pl.ds(pl.multiple_of(first - lane, tile), step), pl.ds(pl.multiple_of(lane, 128), double)
                ]
            else:
                to = out_ref.at[pl.ds(pl.multiple_of(first, tile), step), :]
            yield slot, rows, pltpu.make_async_copy(wide_s.at[rows, :], to, sem.at[slot])

    for side in range(2):

        @pl.when(me % 2 == (side ^ other))
        def _():
            copies = []
            for slot, rows, copy in targets(side):
                wide_s[rows, :] = half_ref[rows, :].astype(f32)
                copy.start()
                copies.append(copy)
            for copy in copies:
                copy.wait()


def call(kernel, outs, scratch=(), specs=None, count=0, grant=8, **more):
    return pl.pallas_call(
        kernel,
        out_shape=outs,
        in_specs=specs if specs is not None else [VMEM] * count,
        out_specs=more.pop("out_specs", jax.tree.map(lambda _: VMEM, outs)),
        scratch_shapes=list(scratch),
        compiler_params=pltpu.CompilerParams(vmem_limit_bytes=grant * 2**20),
        **more,
    )


def struct(shape, dtype):
    return jax.ShapeDtypeStruct(shape, dtype)


def exchange(value, masks, size):
    return [lax.ppermute(value if not isinstance(value, list) else value[i], "seq",
                         [(d, d ^ mask) for d in range(size)]) for i, mask in enumerate(masks)]


def sum_over_devices(me, ride, keep, send, size, factor, riding):
    bits = size.bit_length() - 1
    rows, double = keep.shape
    radix = min(4, size // 2)
    masks = [m << 1 for m in range(1, radix)]
    rows = rows // radix
    parts = [keep] + exchange([send], [1], size)
    extra = ride.shape[0] // 2 if riding else 0
    outs = [struct((rows, double), f32)] + [struct((rows + extra, double), bf16)] * (radix - 1)
    if riding:
        outs.append(struct((extra, double), bf16))
        parts = [ride] + parts
    pieces = call(
        functools.partial(split_kernel, radix, 1, riding), outs, specs=[SMEM] + [VMEM] * len(parts)
    )(me, *parts)
    arrived = exchange(list(pieces[1:radix]), masks, size)
    parts = [pieces[0]] + arrived
    if riding:
        riders = call(lines_kernel, [struct((extra, double), bf16)] * 4, count=4)(pieces[-1], *arrived)
    for rest in range(radix.bit_length(), bits):
        total = call(functools.partial(total_kernel, 1.0), struct((rows, double), bf16), count=len(parts))(*parts)
        parts = [total] + exchange([total], [1 << rest], size)
    mine = call(functools.partial(total_kernel, factor), struct((rows, double), bf16), count=len(parts))(*parts)
    if riding:
        mine, *riders = lax.optimization_barrier((mine, *riders))
    else:
        mine, ride = lax.optimization_barrier((mine, ride))
    got = exchange([mine] * (radix - 1), masks, size)
    if riding:
        ride = [riders[0]] + exchange(list(riders[1:]), [m << 3 for m in range(1, 4)], size)
    mine = jnp.concatenate([mine] + got, axis=0)
    (other,) = exchange([mine], [1], size)
    return mine, other, rows, [(1, radix)], ride


def shards(saved_input, cotangent, w_in, bias_in, w_out, residual_logit, branch_scale):
    size = lax.axis_size("seq")
    levels = size.bit_length() - 1
    rows, width = saved_input.shape
    double, units = w_in.shape
    block = rows // size
    half = rows // 2
    me = lax.axis_index("seq").astype(jnp.int32).reshape(1)
    if block % 8 == 0:
        both = call(
            pack_kernel,
            struct((size, 2 * block, width), bf16),
            scratch=[pltpu.VMEM((width, rows), bf16)] * 2 + [pltpu.SemaphoreType.DMA((2,))],
            specs=[HBM] * 2,
        )(saved_input.T, cotangent.T)
    else:
        both = jnp.concatenate(
            [saved_input.reshape(size, block, width), cotangent.reshape(size, block, width)], axis=1
        )
    both = lax.all_to_all(both, "seq", split_axis=0, concat_axis=0, tiled=True)
    total = levels * half
    riding = block % 8 == 0 and levels == 5
    rider = struct((rows // 4, double), bf16)
    grad_state, keep, send = call(
        functools.partial(switch_kernel, levels, block),
        [
            rider if riding else struct((rows, width), bf16),
            struct((units, double), f32),
            struct((units + rider.shape[0] * riding, double), bf16),
        ],
        scratch=[
            pltpu.VMEM((total, double), bf16),
            pltpu.VMEM((total, units), bf16),
            pltpu.VMEM((total, units), f32),
            pltpu.VMEM((total, double), f32),
            pltpu.VMEM((total, 1), f32),
            pltpu.VMEM((total, units), bf16),
            pltpu.VMEM((total, double), bf16),
            pltpu.VMEM((half, double), f32),
        ],
        specs=[SMEM] + [VMEM] * 6,
        grant=20,
    )(me, both, w_in, bias_in.reshape(1, units), w_out, residual_logit.reshape(1, double),
      branch_scale.reshape(1, double))
    factor = float(rows * size) ** (-0.5)
    if not riding:
        grad_state = lax.all_to_all(
            grad_state.reshape(size, block, width), "seq", split_axis=0, concat_axis=0, tiled=True
        ).reshape(rows, width)
    mine, other, step, phases, grad_state = sum_over_devices(me, grad_state, keep, send, size, factor, riding)
    if riding:
        grad_state = call(
            functools.partial(unpack_kernel, block),
            struct((width, rows), bf16),
            scratch=[pltpu.VMEM((rows, width), f32)],
            specs=[SMEM] + [VMEM] * len(grad_state),
        )(me, *grad_state).T
    shapes = [struct((double, units), f32), struct((units, double), f32)]
    scratch = [pltpu.VMEM((units, double), f32), pltpu.SemaphoreType.DMA((units // step,))]
    placed = call(
        functools.partial(place_kernel, phases, step, 0),
        shapes, scratch=scratch, specs=[SMEM, VMEM], out_specs=[HBM] * 2,
    )(me, mine)
    grad_in, grad_out = call(
        functools.partial(place_kernel, phases, step, 1),
        shapes, scratch=scratch, specs=[SMEM, VMEM, HBM, HBM], out_specs=[HBM] * 2,
        input_output_aliases={2: 0, 3: 1},
    )(me, other, *placed)
    return (grad_state, grad_in, grad_out)


def solution(mesh):
    in_specs = (P("seq", None), P("seq", None), P(), P(), P(), P(), P())
    out_specs = (P("seq", None), P(), P())
    return jax.shard_map(shards, mesh=mesh, in_specs=in_specs, out_specs=out_specs, check_vma=False)
```

```python
import functools

import jax
import jax.numpy as jnp
from jax import lax
from jax.experimental import pallas as pl
from jax.experimental.pallas import tpu as pltpu
from jax.sharding import PartitionSpec as P

epsilon = 1e-05
tanh_scale = 0.7978845608028654
cubic_coef = 0.044715
f32 = jnp.float32
bf16 = jnp.bfloat16
VMEM = pl.BlockSpec(memory_space=pltpu.VMEM)
SMEM = pl.BlockSpec(memory_space=pltpu.SMEM)
HBM = pl.BlockSpec(memory_space=pltpu.HBM)
tile = 16


def dot(left, right, contract):
    return lax.dot_general(left, right, ((contract[:1], contract[1:]), ((), ())), preferred_element_type=f32)


def pair_rows(state, stride):
    rows, width = state.shape
    groups = rows // (2 * stride)
    if stride >= 8:
        viewed = state.reshape(groups, 2, stride, width)
        halves = [viewed[:, side].reshape(rows // 2, width) for side in (0, 1)]
    else:
        halves = []
        for side in (0, 1):
            row = lax.broadcasted_iota(jnp.int32, (rows // 2, rows), 0)
            col = lax.broadcasted_iota(jnp.int32, (rows // 2, rows), 1)
            pick = (row // stride) * (2 * stride) + row % stride + side * stride
            halves.append(dot((col == pick).astype(bf16), state.astype(bf16), (1, 0)))
    return jnp.concatenate(halves, axis=1)


def unpair_rows(paired, stride):
    half, double = paired.shape
    width = double // 2
    groups = half // stride
    first, second = paired[:, :width], paired[:, width:]
    if stride >= 8:
        parts = [part.reshape(groups, 1, stride, width) for part in (first, second)]
        return jnp.concatenate(parts, axis=1).reshape(2 * half, width)
    total = jnp.zeros((2 * half, width), f32)
    for side, part in enumerate((first, second)):
        row = lax.broadcasted_iota(jnp.int32, (2 * half, half), 0)
        col = lax.broadcasted_iota(jnp.int32, (2 * half, half), 1)
        place = (col // stride) * (2 * stride) + col % stride + side * stride
        total = total + dot((row == place).astype(bf16), part.astype(bf16), (1, 0))
    return total


def pack_kernel(x_ref, g_ref, out_ref, x_s, g_s, sem):
    size, both, width = out_ref.shape
    copies = [
        pltpu.make_async_copy(ref, scratch, sem.at[side])
        for side, (ref, scratch) in enumerate(((x_ref, x_s), (g_ref, g_s)))
    ]
    for copy in copies:
        copy.start()
    parts = []
    for copy, scratch in zip(copies, (x_s, g_s)):
        copy.wait()
        parts.append(scratch[...].astype(f32).T.reshape(size, both // 2, width))
    out_ref[...] = jnp.concatenate(parts, axis=1).astype(bf16)


def fetch_kernel(*refs):
    count = len(refs) // 2
    copies = [pltpu.make_async_copy(refs[i], refs[count + i], refs[-1].at[i]) for i in range(count)]
    for copy in copies:
        copy.start()
    for copy in copies:
        copy.wait()


def switch_kernel(
    levels, block, me_ref, both_ref, w_in_ref, bias_ref, w_out_ref, logit_ref, scale_ref,
    grad_ref, keep_ref, send_ref,
    low_s, act_s, slope_s, normed_s, inverse_s, pre_s, bg_s, paired_s,
):
    half, double = paired_s.shape
    rows, width = 2 * half, double // 2
    units = bias_ref.shape[1]
    riding = send_ref.shape[0] > units
    core = me_ref[0] % 2
    both = both_ref[...].astype(f32)
    gate = jax.nn.sigmoid(logit_ref[...])
    scale = scale_ref[...]
    state = both[:, :block].reshape(rows, width)
    for level in range(levels):
        at = pl.ds(level * half, half)
        paired = pair_rows(state, block * 2**level)
        centered = paired - jnp.mean(paired, axis=-1, keepdims=True)
        inverse = lax.rsqrt(jnp.mean(centered * centered, axis=-1, keepdims=True) + epsilon)
        normed = centered * inverse
        low = normed.astype(bf16)
        normed_s[at, :] = normed
        inverse_s[at, :] = inverse
        low_s[at, :] = low
        u = dot(low, w_in_ref[...], (1, 0)) + bias_ref[...]
        square = u * u
        tangent = jnp.tanh(tanh_scale * (u + cubic_coef * square * u))
        rise = 0.5 * (1.0 + tangent)
        act = (u * rise).astype(bf16)
        slope_s[at, :] = rise + 0.5 * u * (1.0 - tangent * tangent) * tanh_scale * (
            1.0 + 3.0 * cubic_coef * square
        )
        act_s[at, :] = act
        if level < levels - 1:
            branch = dot(act, w_out_ref[...], (1, 0))
            result = (gate * paired + scale * branch).astype(bf16).astype(f32)
            state = unpair_rows(result, block * 2**level)
    grad = both[:, block:].reshape(rows, width)
    for level in reversed(range(levels)):
        at = pl.ds(level * half, half)
        upstream = pair_rows(grad, block * 2**level)
        branch_grad = (scale * upstream).astype(bf16)
        bg_s[at, :] = branch_grad
        act_grad = dot(branch_grad, w_out_ref[...], (1, 1))
        pre_grad = (act_grad * slope_s[at, :]).astype(bf16)
        pre_s[at, :] = pre_grad
        normed_grad = dot(pre_grad, w_in_ref[...], (1, 1))
        normed = normed_s[at, :]
        moved = (
            normed_grad
            - jnp.mean(normed_grad, axis=-1, keepdims=True)
            - normed * jnp.mean(normed_grad * normed, axis=-1, keepdims=True)
        )
        result = (gate * upstream + inverse_s[at, :] * moved).astype(bf16).astype(f32)
        if level > 0 or not riding:
            grad = unpair_rows(result, block * 2**level)
    if riding:
        turned = jnp.concatenate([result[:, width:], result[:, :width]], axis=1)
        paired_s[...] = jnp.where(core == 0, result, turned)
        pairs = half // block
        kept, sent = [], []
        for low in range(pairs // 8):
            for plane in range(4):
                sides = []
                for high in range(2):
                    chip = ((high * (pairs // 8) + low) * 4 + plane) ^ (me_ref[0] >> 1)
                    sides.append(paired_s[pl.ds(pl.multiple_of(chip * block, 8), block), :])
                kept.append(jnp.concatenate([side[:, :width] for side in sides], axis=1))
                sent.append(jnp.concatenate([side[:, width:] for side in sides], axis=1))
        grad_ref[...] = jnp.concatenate(kept, axis=0).astype(bf16)
        send_ref[units:, :] = jnp.concatenate(sent, axis=0).astype(bf16)
    else:
        grad_ref[...] = grad.astype(bf16)
    grad_in = dot(low_s[...], pre_s[...], (0, 0))
    grad_out = dot(act_s[...], bg_s[...], (0, 0))

    def put_in(ref):
        for first in range(0, units, double):
            ref[first : first + double, :] = grad_in[:, first : first + double].astype(ref.dtype)

    def put_out(ref):
        ref[0:units, :] = grad_out.astype(ref.dtype)

    @pl.when(core == 0)
    def _():
        put_in(keep_ref)
        put_out(send_ref)

    @pl.when(core == 1)
    def _():
        put_in(send_ref)
        put_out(keep_ref)


def split_kernel(radix, shift, riding, me_ref, *refs):
    parts, outs = refs[: 2 + riding], refs[2 + riding :]
    rows = outs[0].shape[0]
    if riding:
        ride_ref, parts = parts[0], parts[1:]
        width = ride_ref.shape[1] // 2
        sources = [ride_ref[...].astype(f32), parts[1][rows * radix :, :].astype(f32)]
        for high in range(2):
            lanes = [source[:, high * width : (high + 1) * width] for source in sources]
            outs[radix + high][...] = jnp.concatenate(lanes, axis=1).astype(bf16)
    place = (me_ref[0] >> shift) & (radix - 1)
    for other in range(radix):
        at = pl.ds(pl.multiple_of((place ^ other) * rows, tile), rows)
        total = parts[0][at, :].astype(f32) + parts[1][at, :].astype(f32)
        outs[other][...] = total.astype(outs[other].dtype)


def total_of(refs):
    rows = refs[-1].shape[0]
    total = refs[0][0:rows, :].astype(f32)
    for ref in refs[1:-1]:
        total = total + ref[0:rows, :].astype(f32)
    return total


def total_kernel(factor, *refs):
    refs[-1][...] = (total_of(refs) * factor).astype(refs[-1].dtype)


def line_kernel(*refs):
    parts, sources, (out_ref, kept_ref) = refs[:-4], refs[-4:-2], refs[-2:]
    rows = parts[0].shape[0]
    out_ref[0:rows, :] = total_of([*parts, parts[0]]).astype(bf16)
    half = sources[0].shape[0] // 2
    for first, ref, at in ((0, kept_ref, 0), (half, out_ref, rows)):
        for source in sources:
            ref[at : at + half, :] = source[first : first + half, :]
            at += half


def plane_kernel(factor, *refs):
    parts, (kept_ref, came_ref), outs = refs[:2], refs[2:4], refs[4:]
    rows = outs[0].shape[0]
    mine = (total_of([*parts, outs[0]]) * factor).astype(bf16)
    outs[0][...] = mine
    sources = [kept_ref[...].astype(f32), came_ref[rows:, :].astype(f32)]
    block = sources[0].shape[0] // 8
    for plane in range(4):
        riders = jnp.concatenate(
            [
                source[(high * 4 + plane) * block : (high * 4 + plane + 1) * block]
                for source in sources
                for high in range(2)
            ],
            axis=0,
        ).astype(bf16)
        if plane == 0:
            outs[4][...] = riders
        else:
            outs[plane][0:rows, :] = mine
            outs[plane][rows:, :] = riders


def unpack_kernel(block, me_ref, *refs):
    parts, out_ref, rows_s = refs[:-2], refs[-2], refs[-1]
    width = rows_s.shape[1]
    for plane, part in enumerate(parts):
        values = part[part.shape[0] - 4 * block :, :].astype(f32)
        for low in range(2):
            for high in range(2):
                for core in range(2):
                    source = me_ref[0] ^ (high * 16 + low * 8 + plane * 2 + core)
                    first = (low * 2 + high) * block
                    rows_s[pl.ds(pl.multiple_of(source * block, 8), block), :] = values[
                        first : first + block, core * width : (core + 1) * width
                    ]
    out_ref[...] = rows_s[...].T.astype(bf16)


def place_kernel(phases, step, other, me_ref, half_ref, *refs):
    in_ref, out_ref, wide_s, sem = refs[-4:]
    me = me_ref[0]
    double = half_ref.shape[1]
    pieces = half_ref.shape[0] // step
    base = 0
    for bit, radix in phases:
        base = base * radix + ((me >> bit) & (radix - 1))

    def targets(side):
        for slot in range(pieces):
            first = (slot ^ base) * step
            rows = pl.ds(slot * step, step)
            if side == 0:
                lane = (first // double) * double
                to = in_ref.at[
                    pl.ds(pl.multiple_of(first - lane, tile), step), pl.ds(pl.multiple_of(lane, 128), double)
                ]
            else:
                to = out_ref.at[pl.ds(pl.multiple_of(first, tile), step), :]
            yield slot, rows, pltpu.make_async_copy(wide_s.at[rows, :], to, sem.at[slot])

    for side in range(2):

        @pl.when(me % 2 == (side ^ other))
        def _():
            copies = []
            for slot, rows, copy in targets(side):
                wide_s[rows, :] = half_ref[rows, :].astype(f32)
                copy.start()
                copies.append(copy)
            for copy in copies:
                copy.wait()


def call(kernel, outs, scratch=(), specs=None, count=0, grant=8, **more):
    return pl.pallas_call(
        kernel,
        out_shape=outs,
        in_specs=specs if specs is not None else [VMEM] * count,
        out_specs=more.pop("out_specs", jax.tree.map(lambda _: VMEM, outs)),
        scratch_shapes=list(scratch),
        compiler_params=pltpu.CompilerParams(vmem_limit_bytes=grant and grant * 2**20),
        **more,
    )


def struct(shape, dtype):
    return jax.ShapeDtypeStruct(shape, dtype)


def exchange(value, masks, size):
    return [lax.ppermute(value if not isinstance(value, list) else value[i], "seq",
                         [(d, d ^ mask) for d in range(size)]) for i, mask in enumerate(masks)]


def sum_over_devices(me, ride, keep, send, size, factor, riding):
    bits = size.bit_length() - 1
    rows, double = keep.shape
    radix = min(4, size // 2)
    masks = [m << 1 for m in range(1, radix)]
    rows = rows // radix
    piece, rider = struct((rows, double), bf16), struct(ride.shape, bf16)
    parts = [keep] + exchange([send], [1], size)
    outs = [struct((rows, double), f32)] + [piece] * (radix - 1) + [rider] * 2 * riding
    operands = [ride] * riding + parts
    pieces = call(
        functools.partial(split_kernel, radix, 1, riding), outs, specs=[SMEM] + [VMEM] * len(operands)
    )(me, *operands)
    parts = [pieces[0]] + exchange(list(pieces[1:radix]), masks, size)
    if riding:
        riders = [pieces[radix]] + exchange([pieces[radix + 1]], [16], size)
        total, kept = call(
            line_kernel, [struct((rows + ride.shape[0], double), bf16), rider], count=len(parts) + 2
        )(*parts, *riders)
        (came,) = exchange([total], [8], size)
        second = call(functools.partial(total_kernel, 1.0), piece, count=2)
        total = second(total, came)
        (last,) = exchange([total], [24], size)
        joined = struct((rows + ride.shape[0] // 2, double), bf16)
        mine, *sends, ride = call(
            functools.partial(plane_kernel, factor),
            [piece] + [joined] * 3 + [struct((ride.shape[0] // 2, double), bf16)],
            count=4,
        )(total, last, kept, came)
        got = exchange(sends, masks, size)
        ride = [ride] + got
        got = [part[:rows] for part in got]
    else:
        for rest in range(radix.bit_length(), bits):
            total = call(functools.partial(total_kernel, 1.0), piece, count=len(parts))(*parts)
            parts = [total] + exchange([total], [1 << rest], size)
        mine = call(functools.partial(total_kernel, factor), piece, count=len(parts))(*parts)
        mine, ride = lax.optimization_barrier((mine, ride))
        got = exchange([mine] * (radix - 1), masks, size)
    mine = jnp.concatenate([mine] + got, axis=0)
    (other,) = exchange([mine], [1], size)
    return mine, other, rows, [(1, radix)], ride


def shards(saved_input, cotangent, w_in, bias_in, w_out, residual_logit, branch_scale):
    size = lax.axis_size("seq")
    levels = size.bit_length() - 1
    rows, width = saved_input.shape
    double, units = w_in.shape
    block = rows // size
    half = rows // 2
    me = lax.axis_index("seq").astype(jnp.int32).reshape(1)
    if block % 8 == 0:
        both = call(
            pack_kernel,
            struct((size, 2 * block, width), bf16),
            scratch=[pltpu.VMEM((width, rows), bf16)] * 2 + [pltpu.SemaphoreType.DMA((2,))],
            specs=[HBM] * 2,
            grant=None,
        )(saved_input.T, cotangent.T)
    else:
        both = jnp.concatenate(
            [saved_input.reshape(size, block, width), cotangent.reshape(size, block, width)], axis=1
        )
    both = lax.all_to_all(both, "seq", split_axis=0, concat_axis=0, tiled=True)
    w_in, w_out = call(
        fetch_kernel,
        [struct(w_in.shape, bf16), struct(w_out.shape, bf16)],
        scratch=[pltpu.SemaphoreType.DMA((2,))],
        specs=[HBM] * 2,
        grant=None,
    )(w_in, w_out)
    total = levels * half
    riding = block % 8 == 0 and levels == 5
    rider = struct((rows // 4, double), bf16)
    grad_state, keep, send = call(
        functools.partial(switch_kernel, levels, block),
        [
            rider if riding else struct((rows, width), bf16),
            struct((units, double), f32),
            struct((units + rider.shape[0] * riding, double), bf16),
        ],
        scratch=[
            pltpu.VMEM((total, double), bf16),
            pltpu.VMEM((total, units), bf16),
            pltpu.VMEM((total, units), f32),
            pltpu.VMEM((total, double), f32),
            pltpu.VMEM((total, 1), f32),
            pltpu.VMEM((total, units), bf16),
            pltpu.VMEM((total, double), bf16),
            pltpu.VMEM((half, double), f32),
        ],
        specs=[SMEM] + [VMEM] * 6,
        grant=20,
    )(me, both, w_in, bias_in.reshape(1, units), w_out, residual_logit.reshape(1, double),
      branch_scale.reshape(1, double))
    factor = float(rows * size) ** (-0.5)
    if not riding:
        grad_state = lax.all_to_all(
            grad_state.reshape(size, block, width), "seq", split_axis=0, concat_axis=0, tiled=True
        ).reshape(rows, width)
    mine, other, step, phases, grad_state = sum_over_devices(me, grad_state, keep, send, size, factor, riding)
    if riding:
        grad_state = call(
            functools.partial(unpack_kernel, block),
            struct((width, rows), bf16),
            scratch=[pltpu.VMEM((rows, width), f32)],
            specs=[SMEM] + [VMEM] * len(grad_state),
        )(me, *grad_state).T
    shapes = [struct((double, units), f32), struct((units, double), f32)]
    scratch = [pltpu.VMEM((units, double), f32), pltpu.SemaphoreType.DMA((units // step,))]
    placed = call(
        functools.partial(place_kernel, phases, step, 0),
        shapes, scratch=scratch, specs=[SMEM, VMEM], out_specs=[HBM] * 2,
    )(me, mine)
    grad_in, grad_out = call(
        functools.partial(place_kernel, phases, step, 1),
        shapes, scratch=scratch, specs=[SMEM, VMEM, HBM, HBM], out_specs=[HBM] * 2,
        input_output_aliases={2: 0, 3: 1},
    )(me, other, *placed)
    return (grad_state, grad_in, grad_out)


def solution(mesh):
    in_specs = (P("seq", None), P("seq", None), P(), P(), P(), P(), P())
    out_specs = (P("seq", None), P(), P())
    return jax.shard_map(shards, mesh=mesh, in_specs=in_specs, out_specs=out_specs, check_vma=False)
```

```python
import functools

import jax
import jax.numpy as jnp
from jax import lax
from jax.experimental import pallas as pl
from jax.experimental.pallas import tpu as pltpu
from jax.sharding import PartitionSpec as P

epsilon = 1e-05
tanh_scale = 0.7978845608028654
cubic_coef = 0.044715
f32 = jnp.float32
bf16 = jnp.bfloat16
VMEM = pl.BlockSpec(memory_space=pltpu.VMEM)
SMEM = pl.BlockSpec(memory_space=pltpu.SMEM)
HBM = pl.BlockSpec(memory_space=pltpu.HBM)
tile = 16


def dot(left, right, contract):
    return lax.dot_general(left, right, ((contract[:1], contract[1:]), ((), ())), preferred_element_type=f32)


def pair_rows(state, stride):
    rows, width = state.shape
    groups = rows // (2 * stride)
    if stride >= 8:
        viewed = state.reshape(groups, 2, stride, width)
        return [viewed[:, side].reshape(rows // 2, width) for side in (0, 1)]
    halves = []
    for side in (0, 1):
        row = lax.broadcasted_iota(jnp.int32, (rows // 2, rows), 0)
        col = lax.broadcasted_iota(jnp.int32, (rows // 2, rows), 1)
        pick = (row // stride) * (2 * stride) + row % stride + side * stride
        halves.append(dot((col == pick).astype(bf16), state.astype(bf16), (1, 0)))
    return halves


def unpair_rows(halves, stride):
    half, width = halves[0].shape
    if stride >= 8:
        parts = [part.reshape(half // stride, 1, stride, width) for part in halves]
        return jnp.concatenate(parts, axis=1).reshape(2 * half, width)
    total = jnp.zeros((2 * half, width), f32)
    for side, part in enumerate(halves):
        row = lax.broadcasted_iota(jnp.int32, (2 * half, half), 0)
        col = lax.broadcasted_iota(jnp.int32, (2 * half, half), 1)
        place = (col // stride) * (2 * stride) + col % stride + side * stride
        total = total + dot((row == place).astype(bf16), part.astype(bf16), (1, 0))
    return total


def mean_of(halves, count):
    return jnp.sum(halves[0] + halves[1], axis=-1, keepdims=True) * (1.0 / count)


def widen(part, lanes):
    rows, width = part.shape
    return part if width == lanes else jnp.concatenate([part, jnp.zeros((rows, lanes - width), part.dtype)], axis=1)


def pack_kernel(x_ref, g_ref, out_ref, x_s, g_s, sem):
    copies = [
        pltpu.make_async_copy(ref, scratch, sem.at[side])
        for side, (ref, scratch) in enumerate(((x_ref, x_s), (g_ref, g_s)))
    ]
    for copy in copies:
        copy.start()
    parts = []
    for copy, scratch in zip(copies, (x_s, g_s)):
        copy.wait()
        parts.append(scratch[...].astype(f32).T)
    out_ref[...] = jnp.concatenate(parts, axis=1).reshape(out_ref.shape).astype(bf16)


def fetch_kernel(w_in_ref, w_out_ref, bias_ref, logit_ref, scale_ref, *refs):
    w_in_o, w_out_o, bias_o, gate_o, scale_o, w_in_s, w_out_s, sem = refs
    copies = [
        pltpu.make_async_copy(ref, to, sem.at[i])
        for i, (ref, to) in enumerate(((w_in_ref, w_in_s), (w_out_ref, w_out_s)))
    ]
    for copy in copies:
        copy.start()
    width, lanes = w_in_ref.shape[0] // 2, w_in_o.shape[0] // 2
    bias_o[...] = bias_ref[...].reshape(bias_o.shape)
    gate = jax.nn.sigmoid(logit_ref[...].reshape(1, 2 * width))
    scale = scale_ref[...].reshape(1, 2 * width)
    for copy in copies:
        copy.wait()
    for side in range(2):
        first, at = side * width, side * lanes
        gate_o[:, at : at + lanes] = widen(gate[:, first : first + width], lanes)
        scale_o[:, at : at + lanes] = widen(scale[:, first : first + width], lanes)
        w_out_o[:, at : at + lanes] = widen(w_out_s[:, first : first + width], lanes)
        w_in_o[at : at + width, :] = w_in_s[first : first + width, :]
        if lanes > width:
            w_in_o[at + width : at + lanes, :] = jnp.zeros((lanes - width, w_in_o.shape[1]), bf16)


def switch_kernel(
    levels, block, me_ref, both_ref, w_in_ref, w_out_ref, bias_ref, gate_ref, scale_ref,
    grad_ref, keep_ref, send_ref,
    low_s, act_s, slope_s, normed_s, inverse_s, pre_s, bg_s, paired_s,
):
    half, double = paired_s.shape
    rows, width = 2 * half, double // 2
    units = bias_ref.shape[1]
    riding = send_ref.shape[0] > units
    core = me_ref[0] % 2
    sides = range(2)
    lanes = w_in_ref.shape[0] // 2
    gate = [gate_ref[:, side * lanes : (side + 1) * lanes] for side in sides]
    scale = [scale_ref[:, side * lanes : (side + 1) * lanes] for side in sides]
    both = both_ref[...].astype(f32).reshape(rows, double)
    state = widen(both[:, :width], lanes)
    inside = lax.broadcasted_iota(jnp.int32, (half, lanes), 1) < width
    for level in range(levels):
        at = pl.ds(level * half, half)
        paired = pair_rows(state, block * 2**level)
        average = mean_of(paired, double)
        centered = [jnp.where(inside, part - average, 0.0) for part in paired]
        inverse = lax.rsqrt(mean_of([part * part for part in centered], double) + epsilon)
        normed = [part * inverse for part in centered]
        low = jnp.concatenate([part.astype(bf16) for part in normed], axis=1)
        low_s[at, :] = low
        inverse_s[at, :] = inverse
        for side in sides:
            normed_s[side, at, :] = normed[side]
        u = dot(low, w_in_ref[...], (1, 0)) + bias_ref[...]
        square = u * u
        tangent = jnp.tanh(u * (tanh_scale + tanh_scale * cubic_coef * square))
        rise = 0.5 + 0.5 * tangent
        value = u * rise
        act = value.astype(bf16)
        slope_s[at, :] = rise + value * (1.0 - tangent) * (tanh_scale + 3.0 * tanh_scale * cubic_coef * square)
        act_s[at, :] = act
        if level < levels - 1:
            branch = dot(act, w_out_ref[...], (1, 0))
            result = [
                (gate[side] * paired[side] + scale[side] * branch[:, side * lanes : (side + 1) * lanes])
                .astype(bf16)
                .astype(f32)
                for side in sides
            ]
            state = unpair_rows(result, block * 2**level)
    grad = widen(both[:, width:], lanes)
    for level in reversed(range(levels)):
        at = pl.ds(level * half, half)
        upstream = pair_rows(grad, block * 2**level)
        branch_grad = [(scale[side] * upstream[side]).astype(bf16) for side in sides]
        bg_s[at, :] = jnp.concatenate([part[:, :width] for part in branch_grad], axis=1)
        act_grad = dot(jnp.concatenate(branch_grad, axis=1), w_out_ref[...], (1, 1))
        pre_grad = (act_grad * slope_s[at, :]).astype(bf16)
        pre_s[at, :] = pre_grad
        normed_grad = dot(pre_grad, w_in_ref[...], (1, 1))
        normed_grad = [normed_grad[:, side * lanes : (side + 1) * lanes] for side in sides]
        normed = [normed_s[side, at, :] for side in sides]
        average = mean_of(normed_grad, double)
        product = mean_of([normed_grad[side] * normed[side] for side in sides], double)
        inverse = inverse_s[at, :]
        result = [
            (gate[side] * upstream[side] + inverse * (normed_grad[side] - average - normed[side] * product))
            .astype(bf16)
            .astype(f32)
            for side in sides
        ]
        if level > 0 or not riding:
            grad = unpair_rows(result, block * 2**level)
    if riding:
        paired_s[:, :width] = jnp.where(core == 0, result[0], result[1])[:, :width]
        paired_s[:, width:] = jnp.where(core == 0, result[1], result[0])[:, :width]
        pairs = half // block
        kept, sent = [], []
        for low in range(pairs // 8):
            for plane in range(4):
                found = []
                for high in range(2):
                    chip = ((high * (pairs // 8) + low) * 4 + plane) ^ (me_ref[0] >> 1)
                    found.append(paired_s[pl.ds(pl.multiple_of(chip * block, 8), block), :])
                kept.append(jnp.concatenate([part[:, :width] for part in found], axis=1))
                sent.append(jnp.concatenate([part[:, width:] for part in found], axis=1))
        grad_ref[...] = jnp.concatenate(kept, axis=0).astype(bf16)
        send_ref[units:, :] = jnp.concatenate(sent, axis=0).astype(bf16)
    else:
        grad_ref[...] = grad[:, :width].astype(bf16)
    grad_in = dot(low_s[...], pre_s[...], (0, 0))
    grad_in = jnp.concatenate([grad_in[side * lanes : side * lanes + width] for side in sides], axis=0)
    grad_out = dot(act_s[...], bg_s[...], (0, 0))

    def put_in(ref):
        for first in range(0, units, double):
            ref[first : first + double, :] = grad_in[:, first : first + double].astype(ref.dtype)

    def put_out(ref):
        ref[0:units, :] = grad_out.astype(ref.dtype)

    @pl.when(core == 0)
    def _():
        put_in(keep_ref)
        put_out(send_ref)

    @pl.when(core == 1)
    def _():
        put_in(send_ref)
        put_out(keep_ref)


def split_kernel(radix, shift, riding, me_ref, *refs):
    parts, outs = refs[: 2 + riding], refs[2 + riding :]
    rows = outs[0].shape[0]
    if riding:
        ride_ref, parts = parts[0], parts[1:]
        width = ride_ref.shape[1] // 2
        sources = [ride_ref[...].astype(f32), parts[1][rows * radix :, :].astype(f32)]
        for high in range(2):
            lanes = [source[:, high * width : (high + 1) * width] for source in sources]
            outs[radix + high][...] = jnp.concatenate(lanes, axis=1).astype(bf16)
    place = (me_ref[0] >> shift) & (radix - 1)
    for other in range(radix):
        at = pl.ds(pl.multiple_of((place ^ other) * rows, tile), rows)
        total = parts[0][at, :].astype(f32) + parts[1][at, :].astype(f32)
        outs[other][...] = total.astype(outs[other].dtype)


def total_of(refs):
    rows = refs[-1].shape[0]
    total = refs[0][0:rows, :].astype(f32)
    for ref in refs[1:-1]:
        total = total + ref[0:rows, :].astype(f32)
    return total


def total_kernel(factor, *refs):
    refs[-1][...] = (total_of(refs) * factor).astype(refs[-1].dtype)


def line_kernel(*refs):
    parts, sources, (out_ref, kept_ref) = refs[:-4], refs[-4:-2], refs[-2:]
    rows = parts[0].shape[0]
    out_ref[0:rows, :] = total_of([*parts, parts[0]]).astype(bf16)
    half = sources[0].shape[0] // 2
    for first, ref, at in ((0, kept_ref, 0), (half, out_ref, rows)):
        for source in sources:
            ref[at : at + half, :] = source[first : first + half, :]
            at += half


def plane_kernel(factor, *refs):
    parts, (kept_ref, came_ref), outs = refs[:2], refs[2:4], refs[4:]
    rows = outs[0].shape[0]
    mine = (total_of([*parts, outs[0]]) * factor).astype(bf16)
    outs[0][...] = mine
    sources = [kept_ref[...].astype(f32), came_ref[rows:, :].astype(f32)]
    block = sources[0].shape[0] // 8
    for plane in range(4):
        riders = jnp.concatenate(
            [
                source[(high * 4 + plane) * block : (high * 4 + plane + 1) * block]
                for source in sources
                for high in range(2)
            ],
            axis=0,
        ).astype(bf16)
        if plane == 0:
            outs[4][...] = riders
        else:
            outs[plane][0:rows, :] = mine
            outs[plane][rows:, :] = riders


def unpack_kernel(block, me_ref, *refs):
    parts, out_ref, rows_s = refs[:-2], refs[-2], refs[-1]
    width = rows_s.shape[1]
    for plane, part in enumerate(parts):
        values = part[part.shape[0] - 4 * block :, :].astype(f32)
        for low in range(2):
            for high in range(2):
                for core in range(2):
                    source = me_ref[0] ^ (high * 16 + low * 8 + plane * 2 + core)
                    first = (low * 2 + high) * block
                    rows_s[pl.ds(pl.multiple_of(source * block, 8), block), :] = values[
                        first : first + block, core * width : (core + 1) * width
                    ]
    out_ref[...] = rows_s[...].T.astype(bf16)


def place_kernel(bit, me_ref, *refs):
    in_ref, out_ref, wide_s, sem = refs[-4:]
    count, step, double = wide_s.shape
    me = me_ref[0]
    pieces = count // 2
    base = (me >> bit) & (pieces - 1)

    def write(parts):
        copies = []
        for i, part in enumerate(parts):
            first = ((i % pieces) ^ base) * step
            if i < pieces:
                lane = (first // double) * double
                to = in_ref.at[
                    pl.ds(pl.multiple_of(first - lane, tile), step), pl.ds(pl.multiple_of(lane, 128), double)
                ]
            else:
                to = out_ref.at[pl.ds(pl.multiple_of(first, tile), step), :]
            wide_s[i] = part[0:step, :].astype(f32)
            copy = pltpu.make_async_copy(wide_s.at[i], to, sem.at[i])
            copy.start()
            copies.append(copy)
        for copy in copies:
            copy.wait()

    @pl.when(me % 2 == 0)
    def _():
        write(refs[:count])

    @pl.when(me % 2 == 1)
    def _():
        write(refs[pieces:count] + refs[:pieces])


def call(kernel, outs, scratch=(), specs=None, count=0, grant=8, **more):
    return pl.pallas_call(
        kernel,
        out_shape=outs,
        in_specs=specs if specs is not None else [VMEM] * count,
        out_specs=more.pop("out_specs", jax.tree.map(lambda _: VMEM, outs)),
        scratch_shapes=list(scratch),
        compiler_params=pltpu.CompilerParams(vmem_limit_bytes=grant and grant * 2**20),
        **more,
    )


def struct(shape, dtype):
    return jax.ShapeDtypeStruct(shape, dtype)


def exchange(value, masks, size):
    return [lax.ppermute(value if not isinstance(value, list) else value[i], "seq",
                         [(d, d ^ mask) for d in range(size)]) for i, mask in enumerate(masks)]


def sum_over_devices(me, ride, keep, send, size, factor, riding):
    bits = size.bit_length() - 1
    rows, double = keep.shape
    radix = min(4, size // 2)
    masks = [m << 1 for m in range(1, radix)]
    rows = rows // radix
    piece, rider = struct((rows, double), bf16), struct(ride.shape, bf16)
    parts = [keep] + exchange([send], [1], size)
    outs = [struct((rows, double), f32)] + [piece] * (radix - 1) + [rider] * 2 * riding
    operands = [ride] * riding + parts
    pieces = call(
        functools.partial(split_kernel, radix, 1, riding), outs, specs=[SMEM] + [VMEM] * len(operands)
    )(me, *operands)
    parts = [pieces[0]] + exchange(list(pieces[1:radix]), masks, size)
    if riding:
        riders = [pieces[radix]] + exchange([pieces[radix + 1]], [16], size)
        total, kept = call(
            line_kernel, [struct((rows + ride.shape[0], double), bf16), rider], count=len(parts) + 2
        )(*parts, *riders)
        (came,) = exchange([total], [8], size)
        second = call(functools.partial(total_kernel, 1.0), piece, count=2)
        total = second(total, came)
        (last,) = exchange([total], [24], size)
        joined = struct((rows + ride.shape[0] // 2, double), bf16)
        mine, *sends, ride = call(
            functools.partial(plane_kernel, factor),
            [piece] + [joined] * 3 + [struct((ride.shape[0] // 2, double), bf16)],
            count=4,
        )(total, last, kept, came)
        got = exchange(sends, masks, size)
        ride = [ride] + got
    else:
        for rest in range(radix.bit_length(), bits):
            total = call(functools.partial(total_kernel, 1.0), piece, count=len(parts))(*parts)
            parts = [total] + exchange([total], [1 << rest], size)
        mine = call(functools.partial(total_kernel, factor), piece, count=len(parts))(*parts)
        mine, ride = lax.optimization_barrier((mine, ride))
        got = exchange([mine] * (radix - 1), masks, size)
    mine = [mine] + got
    return mine, exchange(mine, [1] * radix, size), rows, ride


def shards(saved_input, cotangent, w_in, bias_in, w_out, residual_logit, branch_scale):
    size = lax.axis_size("seq")
    levels = size.bit_length() - 1
    rows, width = saved_input.shape
    double, units = w_in.shape
    block = rows // size
    half = rows // 2
    me = lax.axis_index("seq").astype(jnp.int32).reshape(1)
    if block % 8 == 0:
        both = call(
            pack_kernel,
            struct((size, block, double), bf16),
            scratch=[pltpu.VMEM((width, rows), bf16)] * 2 + [pltpu.SemaphoreType.DMA((2,))],
            specs=[HBM] * 2,
            grant=None,
            cost_estimate=pl.CostEstimate(flops=0, bytes_accessed=7 * 10**6, transcendentals=0),
        )(saved_input.T, cotangent.T)
    else:
        both = jnp.concatenate([saved_input, cotangent], axis=1).reshape(size, block, double)
    both = lax.all_to_all(both, "seq", split_axis=0, concat_axis=0, tiled=True)
    lanes = -(-width // 128) * 128
    parameters = call(
        fetch_kernel,
        [struct((2 * lanes, units), bf16), struct((units, 2 * lanes), bf16)]
        + [struct((1, count), f32) for count in (units, 2 * lanes, 2 * lanes)],
        scratch=[pltpu.VMEM(w_in.shape, bf16), pltpu.VMEM(w_out.shape, bf16), pltpu.SemaphoreType.DMA((2,))],
        specs=[HBM] * 2 + [VMEM] * 3,
    )(w_in, w_out, bias_in, residual_logit, branch_scale)
    total = levels * half
    riding = block % 8 == 0 and levels == 5
    rider = struct((rows // 4, double), bf16)
    grad_state, keep, send = call(
        functools.partial(switch_kernel, levels, block),
        [
            rider if riding else struct((rows, width), bf16),
            struct((units, double), f32),
            struct((units + rider.shape[0] * riding, double), bf16),
        ],
        scratch=[
            pltpu.VMEM((total, 2 * lanes), bf16),
            pltpu.VMEM((total, units), bf16),
            pltpu.VMEM((total, units), f32),
            pltpu.VMEM((2, total, lanes), f32),
            pltpu.VMEM((total, 1), f32),
            pltpu.VMEM((total, units), bf16),
            pltpu.VMEM((total, double), bf16),
            pltpu.VMEM((half, double), f32),
        ],
        specs=[SMEM] + [VMEM] * 6,
        grant=20,
    )(me, both, *parameters)
    factor = float(rows * size) ** (-0.5)
    if not riding:
        grad_state = lax.all_to_all(
            grad_state.reshape(size, block, width), "seq", split_axis=0, concat_axis=0, tiled=True
        ).reshape(rows, width)
    mine, other, step, grad_state = sum_over_devices(me, grad_state, keep, send, size, factor, riding)
    if riding:
        grad_state = call(
            functools.partial(unpack_kernel, block),
            struct((width, rows), bf16),
            scratch=[pltpu.VMEM((rows, width), f32)],
            specs=[SMEM] + [VMEM] * len(grad_state),
        )(me, *grad_state).T
    shapes = [struct((double, units), f32), struct((units, double), f32)]
    count = 2 * len(mine)
    grad_in, grad_out = call(
        functools.partial(place_kernel, 1),
        shapes,
        scratch=[pltpu.VMEM((count, step, double), f32), pltpu.SemaphoreType.DMA((count,))],
        specs=[SMEM] + [VMEM] * count,
        out_specs=[HBM] * 2,
    )(me, *mine, *other)
    return (grad_state, grad_in, grad_out)


def solution(mesh):
    in_specs = (P("seq", None), P("seq", None), P(), P(), P(), P(), P())
    out_specs = (P("seq", None), P(), P())
    return jax.shard_map(shards, mesh=mesh, in_specs=in_specs, out_specs=out_specs, check_vma=False)
```

```python
import functools

import jax
import jax.numpy as jnp
from jax import lax
from jax.experimental import pallas as pl
from jax.experimental.pallas import tpu as pltpu
from jax.sharding import PartitionSpec as P

epsilon = 1e-05
tanh_scale = 0.7978845608028654
cubic_coef = 0.044715
f32 = jnp.float32
bf16 = jnp.bfloat16
VMEM = pl.BlockSpec(memory_space=pltpu.VMEM)
SMEM = pl.BlockSpec(memory_space=pltpu.SMEM)
HBM = pl.BlockSpec(memory_space=pltpu.HBM)
tile = 16


def dot(left, right, contract):
    return lax.dot_general(left, right, ((contract[:1], contract[1:]), ((), ())), preferred_element_type=f32)


def pair_rows(state, stride):
    rows, width = state.shape
    groups = rows // (2 * stride)
    if stride >= 8:
        viewed = state.reshape(groups, 2, stride, width)
        return [viewed[:, side].reshape(rows // 2, width) for side in (0, 1)]
    halves = []
    for side in (0, 1):
        row = lax.broadcasted_iota(jnp.int32, (rows // 2, rows), 0)
        col = lax.broadcasted_iota(jnp.int32, (rows // 2, rows), 1)
        pick = (row // stride) * (2 * stride) + row % stride + side * stride
        halves.append(dot((col == pick).astype(bf16), state.astype(bf16), (1, 0)))
    return halves


def unpair_rows(halves, stride):
    half, width = halves[0].shape
    if stride >= 8:
        parts = [part.reshape(half // stride, 1, stride, width) for part in halves]
        return jnp.concatenate(parts, axis=1).reshape(2 * half, width)
    total = jnp.zeros((2 * half, width), f32)
    for side, part in enumerate(halves):
        row = lax.broadcasted_iota(jnp.int32, (2 * half, half), 0)
        col = lax.broadcasted_iota(jnp.int32, (2 * half, half), 1)
        place = (col // stride) * (2 * stride) + col % stride + side * stride
        total = total + dot((row == place).astype(bf16), part.astype(bf16), (1, 0))
    return total


def mean_of(halves, count):
    return jnp.sum(halves[0] + halves[1], axis=-1, keepdims=True) * (1.0 / count)


def widen(part, lanes):
    rows, width = part.shape
    return part if width == lanes else jnp.concatenate([part, jnp.zeros((rows, lanes - width), part.dtype)], axis=1)


def pack_kernel(x_ref, g_ref, out_ref, x_s, g_s, sem):
    copies = [
        pltpu.make_async_copy(ref, scratch, sem.at[side])
        for side, (ref, scratch) in enumerate(((x_ref, x_s), (g_ref, g_s)))
    ]
    for copy in copies:
        copy.start()
    for copy in copies:
        copy.wait()
    both = jnp.concatenate([x_s[...], g_s[...]], axis=0).T
    out_ref[...] = both.astype(f32).reshape(out_ref.shape).astype(bf16)


def fetch_kernel(w_in_ref, w_out_ref, bias_ref, logit_ref, scale_ref, *refs):
    w_in_o, w_out_o, bias_o, gate_o, scale_o, w_in_s, w_out_s, sem = refs
    copies = [
        pltpu.make_async_copy(ref, to, sem.at[i])
        for i, (ref, to) in enumerate(((w_in_ref, w_in_s), (w_out_ref, w_out_s)))
    ]
    for copy in copies:
        copy.start()
    width, lanes = w_in_ref.shape[0] // 2, w_in_o.shape[0] // 2
    bias_o[...] = bias_ref[...].reshape(bias_o.shape)
    gate = jax.nn.sigmoid(logit_ref[...].reshape(1, 2 * width))
    scale = scale_ref[...].reshape(1, 2 * width)
    for copy in copies:
        copy.wait()
    for side in range(2):
        first, at = side * width, side * lanes
        gate_o[:, at : at + lanes] = widen(gate[:, first : first + width], lanes)
        scale_o[:, at : at + lanes] = widen(scale[:, first : first + width], lanes)
        w_out_o[:, at : at + lanes] = widen(w_out_s[:, first : first + width], lanes)
        w_in_o[at : at + width, :] = w_in_s[first : first + width, :]
        if lanes > width:
            w_in_o[at + width : at + lanes, :] = jnp.zeros((lanes - width, w_in_o.shape[1]), bf16)


def switch_kernel(
    levels, block, me_ref, both_ref, w_in_ref, w_out_ref, bias_ref, gate_ref, scale_ref,
    grad_ref, send_ref, low_s, pre_s, act_s, bg_s,
    slope_s, normed_s, inverse_s, paired_s,
):
    half, double = paired_s.shape
    rows, width = 2 * half, double // 2
    units = bias_ref.shape[1]
    riding = send_ref.shape[0] > units
    core = me_ref[0] % 2
    sides = range(2)
    lanes = w_in_ref.shape[0] // 2
    gate = [gate_ref[:, side * lanes : (side + 1) * lanes] for side in sides]
    scale = [scale_ref[:, side * lanes : (side + 1) * lanes] for side in sides]
    both = both_ref[...].astype(f32).reshape(rows, double)
    state = widen(both[:, :width], lanes)
    inside = lax.broadcasted_iota(jnp.int32, (half, lanes), 1) < width
    for level in range(levels):
        at = pl.ds(level * half, half)
        paired = pair_rows(state, block * 2**level)
        average = mean_of(paired, double)
        centered = [jnp.where(inside, part - average, 0.0) for part in paired]
        inverse = lax.rsqrt(mean_of([part * part for part in centered], double) + epsilon)
        normed = [part * inverse for part in centered]
        low = jnp.concatenate([part.astype(bf16) for part in normed], axis=1)
        low_s[at, :] = low
        inverse_s[at, :] = inverse
        for side in sides:
            normed_s[side, at, :] = normed[side]
        u = dot(low, w_in_ref[...], (1, 0)) + bias_ref[...]
        square = u * u
        tangent = jnp.tanh(u * (tanh_scale + tanh_scale * cubic_coef * square))
        rise = 0.5 + 0.5 * tangent
        value = u * rise
        act = value.astype(bf16)
        slope_s[at, :] = rise + value * (1.0 - tangent) * (tanh_scale + 3.0 * tanh_scale * cubic_coef * square)
        act_s[at, :] = act
        if level < levels - 1:
            branch = dot(act, w_out_ref[...], (1, 0))
            result = [
                (gate[side] * paired[side] + scale[side] * branch[:, side * lanes : (side + 1) * lanes])
                .astype(bf16)
                .astype(f32)
                for side in sides
            ]
            state = unpair_rows(result, block * 2**level)
    grad = widen(both[:, width:], lanes)
    for level in reversed(range(levels)):
        at = pl.ds(level * half, half)
        upstream = pair_rows(grad, block * 2**level)
        branch_grad = [(scale[side] * upstream[side]).astype(bf16) for side in sides]
        bg_s[at, :] = jnp.concatenate([part[:, :width] for part in branch_grad], axis=1)
        act_grad = dot(jnp.concatenate(branch_grad, axis=1), w_out_ref[...], (1, 1))
        pre_grad = (act_grad * slope_s[at, :]).astype(bf16)
        pre_s[at, :] = pre_grad
        normed_grad = dot(pre_grad, w_in_ref[...], (1, 1))
        normed_grad = [normed_grad[:, side * lanes : (side + 1) * lanes] for side in sides]
        normed = [normed_s[side, at, :] for side in sides]
        average = mean_of(normed_grad, double)
        product = mean_of([normed_grad[side] * normed[side] for side in sides], double)
        inverse = inverse_s[at, :]
        result = [
            (gate[side] * upstream[side] + inverse * (normed_grad[side] - average - normed[side] * product))
            .astype(bf16)
            .astype(f32)
            for side in sides
        ]
        if level > 0 or not riding:
            grad = unpair_rows(result, block * 2**level)
    if riding:
        paired_s[:, :width] = jnp.where(core == 0, result[0], result[1])[:, :width]
        paired_s[:, width:] = jnp.where(core == 0, result[1], result[0])[:, :width]
        pairs = half // block
        kept, sent = [], []
        for low in range(pairs // 8):
            for plane in range(4):
                found = []
                for high in range(2):
                    chip = ((high * (pairs // 8) + low) * 4 + plane) ^ (me_ref[0] >> 1)
                    found.append(paired_s[pl.ds(pl.multiple_of(chip * block, 8), block), :])
                kept.append(jnp.concatenate([part[:, :width] for part in found], axis=1))
                sent.append(jnp.concatenate([part[:, width:] for part in found], axis=1))
        grad_ref[...] = jnp.concatenate(kept, axis=0).astype(bf16)
        send_ref[units:, :] = jnp.concatenate(sent, axis=0).astype(bf16)
    else:
        grad_ref[...] = grad[:, :width].astype(bf16)
    put_products(core == 0, send_ref, low_s, pre_s, act_s, bg_s)


def put_products(out_first, half_ref, low_ref, pre_ref, act_ref, bg_ref):
    units, double = pre_ref.shape[1], bg_ref.shape[1]
    width, lanes = double // 2, low_ref.shape[1] // 2

    @pl.when(out_first)
    def _():
        half_ref[0:units, :] = dot(act_ref[...], bg_ref[...], (0, 0)).astype(half_ref.dtype)

    @pl.when(jnp.logical_not(out_first))
    def _():
        grad_in = dot(low_ref[...], pre_ref[...], (0, 0))
        grad_in = jnp.concatenate([grad_in[side * lanes : side * lanes + width] for side in range(2)], axis=0)
        for first in range(0, units, double):
            half_ref[first : first + double, :] = grad_in[:, first : first + double].astype(half_ref.dtype)


def keep_kernel(me_ref, *refs):
    put_products(me_ref[0] % 2 == 1, refs[-1], *refs[:-1])


def split_kernel(radix, shift, riding, me_ref, *refs):
    parts, outs = refs[: 2 + riding], refs[2 + riding :]
    rows = outs[0].shape[0]
    if riding:
        ride_ref, parts = parts[0], parts[1:]
        width = ride_ref.shape[1] // 2
        sources = [ride_ref[...].astype(f32), parts[1][rows * radix :, :].astype(f32)]
        for high in range(2):
            lanes = [source[:, high * width : (high + 1) * width] for source in sources]
            outs[radix + high][...] = jnp.concatenate(lanes, axis=1).astype(bf16)
    place = (me_ref[0] >> shift) & (radix - 1)
    for other in range(radix):
        at = pl.ds(pl.multiple_of((place ^ other) * rows, tile), rows)
        total = parts[0][at, :].astype(f32) + parts[1][at, :].astype(f32)
        outs[other][...] = total.astype(outs[other].dtype)


def total_of(refs):
    rows = refs[-1].shape[0]
    total = refs[0][0:rows, :].astype(f32)
    for ref in refs[1:-1]:
        total = total + ref[0:rows, :].astype(f32)
    return total


def total_kernel(factor, *refs):
    refs[-1][...] = (total_of(refs) * factor).astype(refs[-1].dtype)


def line_kernel(*refs):
    parts, sources, (out_ref, kept_ref) = refs[:-4], refs[-4:-2], refs[-2:]
    rows = parts[0].shape[0]
    out_ref[0:rows, :] = total_of([*parts, parts[0]]).astype(bf16)
    half = sources[0].shape[0] // 2
    for first, ref, at in ((0, kept_ref, 0), (half, out_ref, rows)):
        for source in sources:
            ref[at : at + half, :] = source[first : first + half, :]
            at += half


def plane_kernel(factor, *refs):
    parts, (kept_ref, came_ref), outs = refs[:2], refs[2:4], refs[4:]
    rows = outs[0].shape[0]
    mine = (total_of([*parts, outs[0]]) * factor).astype(bf16)
    outs[0][...] = mine
    sources = [kept_ref[...].astype(f32), came_ref[rows:, :].astype(f32)]
    block = sources[0].shape[0] // 8
    for plane in range(4):
        riders = jnp.concatenate(
            [
                source[(high * 4 + plane) * block : (high * 4 + plane + 1) * block]
                for source in sources
                for high in range(2)
            ],
            axis=0,
        ).astype(bf16)
        if plane == 0:
            outs[4][...] = riders
        else:
            outs[plane][0:rows, :] = mine
            outs[plane][rows:, :] = riders


def unpack_kernel(block, me_ref, *refs):
    parts, out_ref, rows_s = refs[:-2], refs[-2], refs[-1]
    width = rows_s.shape[1]
    for plane, part in enumerate(parts):
        values = part[part.shape[0] - 4 * block :, :].astype(f32)
        for low in range(2):
            for high in range(2):
                for core in range(2):
                    source = me_ref[0] ^ (high * 16 + low * 8 + plane * 2 + core)
                    first = (low * 2 + high) * block
                    rows_s[pl.ds(pl.multiple_of(source * block, 8), block), :] = values[
                        first : first + block, core * width : (core + 1) * width
                    ]
    out_ref[...] = rows_s[...].T.astype(bf16)


def place_kernel(bit, me_ref, *refs):
    in_ref, out_ref, wide_s, sem = refs[-4:]
    count, step, double = wide_s.shape
    me = me_ref[0]
    pieces = count // 2
    base = (me >> bit) & (pieces - 1)

    def write(parts):
        copies = []
        for i, part in enumerate(parts):
            first = ((i % pieces) ^ base) * step
            if i < pieces:
                lane = (first // double) * double
                to = in_ref.at[
                    pl.ds(pl.multiple_of(first - lane, tile), step), pl.ds(pl.multiple_of(lane, 128), double)
                ]
            else:
                to = out_ref.at[pl.ds(pl.multiple_of(first, tile), step), :]
            wide_s[i] = part[0:step, :].astype(f32)
            copy = pltpu.make_async_copy(wide_s.at[i], to, sem.at[i])
            copy.start()
            copies.append(copy)
        for copy in copies:
            copy.wait()

    @pl.when(me % 2 == 0)
    def _():
        write(refs[:count])

    @pl.when(me % 2 == 1)
    def _():
        write(refs[pieces:count] + refs[:pieces])


def call(kernel, outs, scratch=(), specs=None, count=0, grant=8, **more):
    return pl.pallas_call(
        kernel,
        out_shape=outs,
        in_specs=specs if specs is not None else [VMEM] * count,
        out_specs=more.pop("out_specs", jax.tree.map(lambda _: VMEM, outs)),
        scratch_shapes=list(scratch),
        compiler_params=pltpu.CompilerParams(vmem_limit_bytes=grant and grant * 2**20),
        **more,
    )


def struct(shape, dtype):
    return jax.ShapeDtypeStruct(shape, dtype)


def exchange(value, masks, size):
    return [lax.ppermute(value if not isinstance(value, list) else value[i], "seq",
                         [(d, d ^ mask) for d in range(size)]) for i, mask in enumerate(masks)]


def sum_over_devices(me, ride, keep, send, size, factor, riding):
    bits = size.bit_length() - 1
    rows, double = keep.shape
    radix = min(4, size // 2)
    masks = [m << 1 for m in range(1, radix)]
    rows = rows // radix
    piece, rider = struct((rows, double), bf16), struct(ride.shape, bf16)
    parts = [keep] + exchange([send], [1], size)
    outs = [struct((rows, double), f32)] + [piece] * (radix - 1) + [rider] * 2 * riding
    operands = [ride] * riding + parts
    pieces = call(
        functools.partial(split_kernel, radix, 1, riding), outs, specs=[SMEM] + [VMEM] * len(operands)
    )(me, *operands)
    parts = [pieces[0]] + exchange(list(pieces[1:radix]), masks, size)
    if riding:
        riders = [pieces[radix]] + exchange([pieces[radix + 1]], [16], size)
        total, kept = call(
            line_kernel, [struct((rows + ride.shape[0], double), bf16), rider], count=len(parts) + 2
        )(*parts, *riders)
        (came,) = exchange([total], [8], size)
        second = call(functools.partial(total_kernel, 1.0), piece, count=2)
        total = second(total, came)
        (last,) = exchange([total], [24], size)
        joined = struct((rows + ride.shape[0] // 2, double), bf16)
        mine, *sends, ride = call(
            functools.partial(plane_kernel, factor),
            [piece] + [joined] * 3 + [struct((ride.shape[0] // 2, double), bf16)],
            count=4,
        )(total, last, kept, came)
        got = exchange(sends, masks, size)
        ride = [ride] + got
    else:
        for rest in range(radix.bit_length(), bits):
            total = call(functools.partial(total_kernel, 1.0), piece, count=len(parts))(*parts)
            parts = [total] + exchange([total], [1 << rest], size)
        mine = call(functools.partial(total_kernel, factor), piece, count=len(parts))(*parts)
        mine, ride = lax.optimization_barrier((mine, ride))
        got = exchange([mine] * (radix - 1), masks, size)
    (first,) = exchange([mine], [1], size)
    got[0], first = lax.optimization_barrier((got[0], first))
    return [mine] + got, [first] + exchange(got, [1] * (radix - 1), size), rows, ride


def shards(saved_input, cotangent, w_in, bias_in, w_out, residual_logit, branch_scale):
    size = lax.axis_size("seq")
    levels = size.bit_length() - 1
    rows, width = saved_input.shape
    double, units = w_in.shape
    block = rows // size
    half = rows // 2
    me = lax.axis_index("seq").astype(jnp.int32).reshape(1)
    if block % 8 == 0:
        both = call(
            pack_kernel,
            struct((size, block, double), bf16),
            scratch=[pltpu.VMEM((width, rows), bf16)] * 2 + [pltpu.SemaphoreType.DMA((2,))],
            specs=[HBM] * 2,
            grant=None,
            cost_estimate=pl.CostEstimate(flops=0, bytes_accessed=7 * 10**6, transcendentals=0),
        )(saved_input.T, cotangent.T)
    else:
        both = jnp.concatenate([saved_input, cotangent], axis=1).reshape(size, block, double)
    both = lax.all_to_all(both, "seq", split_axis=0, concat_axis=0, tiled=True)
    lanes = -(-width // 128) * 128
    parameters = call(
        fetch_kernel,
        [struct((2 * lanes, units), bf16), struct((units, 2 * lanes), bf16)]
        + [struct((1, count), f32) for count in (units, 2 * lanes, 2 * lanes)],
        scratch=[pltpu.VMEM(w_in.shape, bf16), pltpu.VMEM(w_out.shape, bf16), pltpu.SemaphoreType.DMA((2,))],
        specs=[HBM] * 2 + [VMEM] * 3,
    )(w_in, w_out, bias_in, residual_logit, branch_scale)
    total = levels * half
    riding = block % 8 == 0 and levels == 5
    rider = struct((rows // 4, double), bf16)
    grad_state, send, *factors = call(
        functools.partial(switch_kernel, levels, block),
        [
            rider if riding else struct((rows, width), bf16),
            struct((units + rider.shape[0] * riding, double), bf16),
            struct((total, 2 * lanes), bf16),
            struct((total, units), bf16),
            struct((total, units), bf16),
            struct((total, double), bf16),
        ],
        scratch=[
            pltpu.VMEM((total, units), f32),
            pltpu.VMEM((2, total, lanes), f32),
            pltpu.VMEM((total, 1), f32),
            pltpu.VMEM((half, double), f32),
        ],
        specs=[SMEM] + [VMEM] * 6,
        grant=20,
    )(me, both, *parameters)
    keep = call(
        keep_kernel,
        struct((units, double), f32),
        specs=[SMEM] + [VMEM] * 4,
        grant=16,
        cost_estimate=pl.CostEstimate(
            flops=2 * total * units * double, bytes_accessed=8 * total * units, transcendentals=0
        ),
    )(me, *factors)
    factor = float(rows * size) ** (-0.5)
    if not riding:
        grad_state = lax.all_to_all(
            grad_state.reshape(size, block, width), "seq", split_axis=0, concat_axis=0, tiled=True
        ).reshape(rows, width)
    mine, other, step, grad_state = sum_over_devices(me, grad_state, keep, send, size, factor, riding)
    if riding:
        grad_state = call(
            functools.partial(unpack_kernel, block),
            struct((width, rows), bf16),
            scratch=[pltpu.VMEM((rows, width), f32)],
            specs=[SMEM] + [VMEM] * len(grad_state),
        )(me, *grad_state).T
    shapes = [struct((double, units), f32), struct((units, double), f32)]
    count = 2 * len(mine)
    grad_in, grad_out = call(
        functools.partial(place_kernel, 1),
        shapes,
        scratch=[pltpu.VMEM((count, step, double), f32), pltpu.SemaphoreType.DMA((count,))],
        specs=[SMEM] + [VMEM] * count,
        out_specs=[HBM] * 2,
    )(me, *mine, *other)
    return (grad_state, grad_in, grad_out)


def solution(mesh):
    in_specs = (P("seq", None), P("seq", None), P(), P(), P(), P(), P())
    out_specs = (P("seq", None), P(), P())
    return jax.shard_map(shards, mesh=mesh, in_specs=in_specs, out_specs=out_specs, check_vma=False)
```

```python
import functools

import jax
import jax.numpy as jnp
from jax import lax
from jax.experimental import pallas as pl
from jax.experimental.pallas import tpu as pltpu
from jax.sharding import PartitionSpec as P

epsilon = 1e-05
tanh_scale = 0.7978845608028654
cubic_coef = 0.044715
f32 = jnp.float32
bf16 = jnp.bfloat16
VMEM = pl.BlockSpec(memory_space=pltpu.VMEM)
SMEM = pl.BlockSpec(memory_space=pltpu.SMEM)
HBM = pl.BlockSpec(memory_space=pltpu.HBM)
tile = 16


def dot(left, right, contract):
    return lax.dot_general(left, right, ((contract[:1], contract[1:]), ((), ())), preferred_element_type=f32)


def pair_rows(state, stride):
    rows, width = state.shape
    groups = rows // (2 * stride)
    if stride >= 8:
        viewed = state.reshape(groups, 2, stride, width)
        return [viewed[:, side].reshape(rows // 2, width) for side in (0, 1)]
    halves = []
    for side in (0, 1):
        row = lax.broadcasted_iota(jnp.int32, (rows // 2, rows), 0)
        col = lax.broadcasted_iota(jnp.int32, (rows // 2, rows), 1)
        pick = (row // stride) * (2 * stride) + row % stride + side * stride
        halves.append(dot((col == pick).astype(bf16), state.astype(bf16), (1, 0)))
    return halves


def unpair_rows(halves, stride):
    half, width = halves[0].shape
    if stride >= 8:
        parts = [part.reshape(half // stride, 1, stride, width) for part in halves]
        return jnp.concatenate(parts, axis=1).reshape(2 * half, width)
    total = jnp.zeros((2 * half, width), f32)
    for side, part in enumerate(halves):
        row = lax.broadcasted_iota(jnp.int32, (2 * half, half), 0)
        col = lax.broadcasted_iota(jnp.int32, (2 * half, half), 1)
        place = (col // stride) * (2 * stride) + col % stride + side * stride
        total = total + dot((row == place).astype(bf16), part.astype(bf16), (1, 0))
    return total


def mean_of(halves, count):
    return jnp.sum(halves[0] + halves[1], axis=-1, keepdims=True) * (1.0 / count)


def widen(part, lanes):
    rows, width = part.shape
    return part if width == lanes else jnp.concatenate([part, jnp.zeros((rows, lanes - width), part.dtype)], axis=1)


def pack_kernel(x_ref, g_ref, out_ref, x_s, g_s, sem):
    copies = [
        pltpu.make_async_copy(ref, scratch, sem.at[side])
        for side, (ref, scratch) in enumerate(((x_ref, x_s), (g_ref, g_s)))
    ]
    for copy in copies:
        copy.start()
    for copy in copies:
        copy.wait()
    both = jnp.concatenate([x_s[...], g_s[...]], axis=0).T
    out_ref[...] = both.astype(f32).reshape(out_ref.shape).astype(bf16)


def fetch_kernel(w_in_ref, w_out_ref, bias_ref, logit_ref, scale_ref, *refs):
    w_in_o, w_out_o, w_in_turned_o, w_out_turned_o, bias_o, gate_o, scale_o, w_in_s, w_out_s, sem = refs
    copies = [
        pltpu.make_async_copy(ref, to, sem.at[i])
        for i, (ref, to) in enumerate(((w_in_ref, w_in_s), (w_out_ref, w_out_s)))
    ]
    for copy in copies:
        copy.start()
    width, lanes = w_in_ref.shape[0] // 2, w_in_o.shape[0] // 2
    bias_o[...] = bias_ref[...].reshape(bias_o.shape)
    gate = jax.nn.sigmoid(logit_ref[...].reshape(1, 2 * width))
    scale = scale_ref[...].reshape(1, 2 * width)
    for copy in copies:
        copy.wait()
    for side in range(2):
        first, at = side * width, side * lanes
        gate_o[:, at : at + lanes] = widen(gate[:, first : first + width], lanes)
        scale_o[:, at : at + lanes] = widen(scale[:, first : first + width], lanes)
        w_out_o[:, at : at + lanes] = widen(w_out_s[:, first : first + width], lanes)
        w_in_o[at : at + width, :] = w_in_s[first : first + width, :]
        if lanes > width:
            w_in_o[at + width : at + lanes, :] = jnp.zeros((lanes - width, w_in_o.shape[1]), bf16)
    w_in_turned_o[...] = w_in_o[...].astype(f32).T.astype(bf16)
    w_out_turned_o[...] = w_out_o[...].astype(f32).T.astype(bf16)


def switch_kernel(
    levels, block, me_ref, both_ref, w_in_ref, w_out_ref, w_in_turned_ref, w_out_turned_ref, bias_ref, gate_ref, scale_ref,
    grad_ref, send_ref, low_s, pre_s, act_s, bg_s,
    slope_s, normed_s, inverse_s, paired_s,
):
    half, double = paired_s.shape
    rows, width = 2 * half, double // 2
    units = bias_ref.shape[1]
    riding = send_ref.shape[0] > units
    core = me_ref[0] % 2
    sides = range(2)
    lanes = w_in_ref.shape[0] // 2
    gate = [gate_ref[:, side * lanes : (side + 1) * lanes] for side in sides]
    scale = [scale_ref[:, side * lanes : (side + 1) * lanes] for side in sides]
    both = both_ref[...].astype(f32).reshape(rows, double)
    state = widen(both[:, :width], lanes)
    inside = lax.broadcasted_iota(jnp.int32, (half, lanes), 1) < width
    for level in range(levels):
        at = pl.ds(level * half, half)
        paired = pair_rows(state, block * 2**level)
        average = mean_of(paired, double)
        centered = [jnp.where(inside, part - average, 0.0) for part in paired]
        inverse = lax.rsqrt(mean_of([part * part for part in centered], double) + epsilon)
        normed = [part * inverse for part in centered]
        low = jnp.concatenate([part.astype(bf16) for part in normed], axis=1)
        low_s[at, :] = low
        inverse_s[at, :] = inverse
        for side in sides:
            normed_s[side, at, :] = normed[side]
        u = dot(low, w_in_ref[...], (1, 0)) + bias_ref[...]
        square = u * u
        tangent = jnp.tanh(u * (tanh_scale + tanh_scale * cubic_coef * square))
        rise = 0.5 + 0.5 * tangent
        value = u * rise
        act = value.astype(bf16)
        slope_s[at, :] = rise + value * (1.0 - tangent) * (tanh_scale + 3.0 * tanh_scale * cubic_coef * square)
        act_s[at, :] = act
        if level < levels - 1:
            branch = dot(act, w_out_ref[...], (1, 0))
            result = [
                (gate[side] * paired[side] + scale[side] * branch[:, side * lanes : (side + 1) * lanes])
                .astype(bf16)
                .astype(f32)
                for side in sides
            ]
            state = unpair_rows(result, block * 2**level)
    grad = widen(both[:, width:], lanes)
    for level in reversed(range(levels)):
        at = pl.ds(level * half, half)
        upstream = pair_rows(grad, block * 2**level)
        branch_grad = [(scale[side] * upstream[side]).astype(bf16) for side in sides]
        bg_s[at, :] = jnp.concatenate([part[:, :width] for part in branch_grad], axis=1)
        act_grad = dot(jnp.concatenate(branch_grad, axis=1), w_out_turned_ref[...], (1, 0))
        pre_grad = (act_grad * slope_s[at, :]).astype(bf16)
        pre_s[at, :] = pre_grad
        normed_grad = dot(pre_grad, w_in_turned_ref[...], (1, 0))
        normed_grad = [normed_grad[:, side * lanes : (side + 1) * lanes] for side in sides]
        normed = [normed_s[side, at, :] for side in sides]
        average = mean_of(normed_grad, double)
        product = mean_of([normed_grad[side] * normed[side] for side in sides], double)
        inverse = inverse_s[at, :]
        result = [
            (gate[side] * upstream[side] + inverse * (normed_grad[side] - average - normed[side] * product))
            .astype(bf16)
            .astype(f32)
            for side in sides
        ]
        if level > 0 or not riding:
            grad = unpair_rows(result, block * 2**level)
    if riding:
        paired_s[:, :width] = jnp.where(core == 0, result[0], result[1])[:, :width]
        paired_s[:, width:] = jnp.where(core == 0, result[1], result[0])[:, :width]
        pairs = half // block
        kept, sent = [], []
        for low in range(pairs // 8):
            for plane in range(4):
                found = []
                for high in range(2):
                    chip = ((high * (pairs // 8) + low) * 4 + plane) ^ (me_ref[0] >> 1)
                    found.append(paired_s[pl.ds(pl.multiple_of(chip * block, 8), block), :])
                kept.append(jnp.concatenate([part[:, :width] for part in found], axis=1))
                sent.append(jnp.concatenate([part[:, width:] for part in found], axis=1))
        grad_ref[...] = jnp.concatenate(kept, axis=0).astype(bf16)
        send_ref[units:, :] = jnp.concatenate(sent, axis=0).astype(bf16)
    else:
        grad_ref[...] = grad[:, :width].astype(bf16)
    put_products(core == 0, send_ref, low_s, pre_s, act_s, bg_s)


def put_products(out_first, half_ref, low_ref, pre_ref, act_ref, bg_ref):
    units, double = pre_ref.shape[1], bg_ref.shape[1]
    width, lanes = double // 2, low_ref.shape[1] // 2

    @pl.when(out_first)
    def _():
        half_ref[0:units, :] = dot(act_ref[...], bg_ref[...], (0, 0)).astype(half_ref.dtype)

    @pl.when(jnp.logical_not(out_first))
    def _():
        grad_in = dot(low_ref[...], pre_ref[...], (0, 0))
        grad_in = jnp.concatenate([grad_in[side * lanes : side * lanes + width] for side in range(2)], axis=0)
        for first in range(0, units, double):
            half_ref[first : first + double, :] = grad_in[:, first : first + double].astype(half_ref.dtype)


def keep_kernel(me_ref, *refs):
    put_products(me_ref[0] % 2 == 1, refs[-1], *refs[:-1])


def split_kernel(radix, shift, riding, me_ref, *refs):
    parts, outs = refs[: 2 + riding], refs[2 + riding :]
    rows = outs[0].shape[0]
    if riding:
        ride_ref, parts = parts[0], parts[1:]
        width = ride_ref.shape[1] // 2
        sources = [ride_ref[...].astype(f32), parts[1][rows * radix :, :].astype(f32)]
        for high in range(2):
            lanes = [source[:, high * width : (high + 1) * width] for source in sources]
            outs[radix + high][...] = jnp.concatenate(lanes, axis=1).astype(bf16)
    place = (me_ref[0] >> shift) & (radix - 1)
    for other in range(radix):
        at = pl.ds(pl.multiple_of((place ^ other) * rows, tile), rows)
        total = parts[0][at, :].astype(f32) + parts[1][at, :].astype(f32)
        outs[other][...] = total.astype(outs[other].dtype)


def total_of(refs):
    rows = refs[-1].shape[0]
    total = refs[0][0:rows, :].astype(f32)
    for ref in refs[1:-1]:
        total = total + ref[0:rows, :].astype(f32)
    return total


def total_kernel(factor, *refs):
    refs[-1][...] = (total_of(refs) * factor).astype(refs[-1].dtype)


def line_kernel(*refs):
    parts, sources, (out_ref, kept_ref) = refs[:-4], refs[-4:-2], refs[-2:]
    rows = parts[0].shape[0]
    out_ref[0:rows, :] = total_of([*parts, parts[0]]).astype(bf16)
    half = sources[0].shape[0] // 2
    for first, ref, at in ((0, kept_ref, 0), (half, out_ref, rows)):
        for source in sources:
            ref[at : at + half, :] = source[first : first + half, :]
            at += half


def plane_kernel(factor, *refs):
    parts, (kept_ref, came_ref), outs = refs[:2], refs[2:4], refs[4:]
    rows = outs[0].shape[0]
    mine = (total_of([*parts, outs[0]]) * factor).astype(bf16)
    outs[0][...] = mine
    sources = [kept_ref[...].astype(f32), came_ref[rows:, :].astype(f32)]
    block = sources[0].shape[0] // 8
    for plane in range(4):
        riders = jnp.concatenate(
            [
                source[(high * 4 + plane) * block : (high * 4 + plane + 1) * block]
                for source in sources
                for high in range(2)
            ],
            axis=0,
        ).astype(bf16)
        if plane == 0:
            outs[4][...] = riders
        else:
            outs[plane][0:rows, :] = mine
            outs[plane][rows:, :] = riders


def unpack_kernel(block, me_ref, *refs):
    parts, out_ref, rows_s = refs[:-2], refs[-2], refs[-1]
    width = rows_s.shape[1]
    for plane, part in enumerate(parts):
        values = part[part.shape[0] - 4 * block :, :].astype(f32)
        for low in range(2):
            for high in range(2):
                for core in range(2):
                    source = me_ref[0] ^ (high * 16 + low * 8 + plane * 2 + core)
                    first = (low * 2 + high) * block
                    rows_s[pl.ds(pl.multiple_of(source * block, 8), block), :] = values[
                        first : first + block, core * width : (core + 1) * width
                    ]
    out_ref[...] = rows_s[...].T.astype(bf16)


def place_kernel(bit, pieces, slots, placed, me_ref, *refs):
    parts, (in_ref, out_ref, wide_s, sem) = refs[: len(slots)], refs[len(slots) + placed :]
    step, double = wide_s.shape[1:]
    me = me_ref[0]
    base = (me >> bit) & (pieces - 1)
    for core in range(2):

        @pl.when(me % 2 == core)
        def _():
            copies = []
            for i, slot in enumerate(slots):
                first = ((slot % pieces) ^ base) * step
                if (slot >= pieces) == (core == 1):
                    lane = (first // double) * double
                    to = in_ref.at[
                        pl.ds(pl.multiple_of(first - lane, tile), step), pl.ds(pl.multiple_of(lane, 128), double)
                    ]
                else:
                    to = out_ref.at[pl.ds(pl.multiple_of(first, tile), step), :]
                wide_s[i] = parts[i][0:step, :].astype(f32)
                copy = pltpu.make_async_copy(wide_s.at[i], to, sem.at[i])
                copy.start()
                copies.append(copy)
            for copy in copies:
                copy.wait()


def place(me, shapes, quarters, slots, placed):
    pieces = len(quarters) // 2
    step, double = min(quarter.shape for quarter in quarters if quarter is not None)
    return call(
        functools.partial(place_kernel, 1, pieces, slots, len(placed)),
        shapes,
        scratch=[pltpu.VMEM((len(slots), step, double), f32), pltpu.SemaphoreType.DMA((len(slots),))],
        specs=[SMEM] + [VMEM] * len(slots) + [HBM] * len(placed),
        out_specs=[HBM] * 2,
        input_output_aliases={1 + len(slots) + i: i for i in range(len(placed))},
    )(me, *[quarters[slot] for slot in slots], *placed)


def call(kernel, outs, scratch=(), specs=None, count=0, grant=8, **more):
    return pl.pallas_call(
        kernel,
        out_shape=outs,
        in_specs=specs if specs is not None else [VMEM] * count,
        out_specs=more.pop("out_specs", jax.tree.map(lambda _: VMEM, outs)),
        scratch_shapes=list(scratch),
        compiler_params=pltpu.CompilerParams(vmem_limit_bytes=grant and grant * 2**20),
        **more,
    )


def struct(shape, dtype):
    return jax.ShapeDtypeStruct(shape, dtype)


def exchange(value, masks, size):
    return [lax.ppermute(value if not isinstance(value, list) else value[i], "seq",
                         [(d, d ^ mask) for d in range(size)]) for i, mask in enumerate(masks)]


def sum_over_devices(me, ride, keep, send, size, factor, riding, shapes):
    bits = size.bit_length() - 1
    rows, double = keep.shape
    radix = min(4, size // 2)
    masks = [m << 1 for m in range(1, radix)]
    rows = rows // radix
    piece, rider = struct((rows, double), bf16), struct(ride.shape, bf16)
    parts = [keep] + exchange([send], [1], size)
    outs = [struct((rows, double), f32)] + [piece] * (radix - 1) + [rider] * 2 * riding
    operands = [ride] * riding + parts
    pieces = call(
        functools.partial(split_kernel, radix, 1, riding), outs, specs=[SMEM] + [VMEM] * len(operands)
    )(me, *operands)
    parts = [pieces[0]] + exchange(list(pieces[1:radix]), masks, size)
    if riding:
        riders = [pieces[radix]] + exchange([pieces[radix + 1]], [16], size)
        total, kept = call(
            line_kernel, [struct((rows + ride.shape[0], double), bf16), rider], count=len(parts) + 2
        )(*parts, *riders)
        (came,) = exchange([total], [8], size)
        second = call(functools.partial(total_kernel, 1.0), piece, count=2)
        total = second(total, came)
        (last,) = exchange([total], [24], size)
        joined = struct((rows + ride.shape[0] // 2, double), bf16)
        mine, *sends, ride = call(
            functools.partial(plane_kernel, factor),
            [piece] + [joined] * 3 + [struct((ride.shape[0] // 2, double), bf16)],
            count=4,
        )(total, last, kept, came)
        got = exchange(sends, masks, size)
        ride = [ride] + got
    else:
        for rest in range(radix.bit_length(), bits):
            total = call(functools.partial(total_kernel, 1.0), piece, count=len(parts))(*parts)
            parts = [total] + exchange([total], [1 << rest], size)
        mine = call(functools.partial(total_kernel, factor), piece, count=len(parts))(*parts)
        mine, ride = lax.optimization_barrier((mine, ride))
        got = exchange([mine] * (radix - 1), masks, size)
    (first,) = exchange([mine], [1], size)
    got[0], first = lax.optimization_barrier((got[0], first))
    quarters = [mine] + got + [first] + [None] * (radix - 1)
    early = [slot for slot in (0, radix, 1) if riding]
    placed = place(me, shapes, quarters, early, []) if early else []
    if early:
        *got[1:], placed = lax.optimization_barrier((*got[1:], placed))
    quarters = [mine] + got + [first] + exchange(got, [1] * (radix - 1), size)
    placed = place(me, shapes, quarters, [slot for slot in range(2 * radix) if slot not in early], placed)
    return placed, ride


def shards(saved_input, cotangent, w_in, bias_in, w_out, residual_logit, branch_scale):
    size = lax.axis_size("seq")
    levels = size.bit_length() - 1
    rows, width = saved_input.shape
    double, units = w_in.shape
    block = rows // size
    half = rows // 2
    me = lax.axis_index("seq").astype(jnp.int32).reshape(1)
    if block % 8 == 0:
        both = call(
            pack_kernel,
            struct((size, block, double), bf16),
            scratch=[pltpu.VMEM((width, rows), bf16)] * 2 + [pltpu.SemaphoreType.DMA((2,))],
            specs=[HBM] * 2,
            grant=None,
            cost_estimate=pl.CostEstimate(flops=0, bytes_accessed=7 * 10**6, transcendentals=0),
        )(saved_input.T, cotangent.T)
    else:
        both = jnp.concatenate([saved_input, cotangent], axis=1).reshape(size, block, double)
    both = lax.all_to_all(both, "seq", split_axis=0, concat_axis=0, tiled=True)
    lanes = -(-width // 128) * 128
    parameters = call(
        fetch_kernel,
        [struct(shape, bf16) for shape in ((2 * lanes, units), (units, 2 * lanes)) + ((units, 2 * lanes), (2 * lanes, units))]
        + [struct((1, count), f32) for count in (units, 2 * lanes, 2 * lanes)],
        scratch=[pltpu.VMEM(w_in.shape, bf16), pltpu.VMEM(w_out.shape, bf16), pltpu.SemaphoreType.DMA((2,))],
        specs=[HBM] * 2 + [VMEM] * 3,
    )(w_in, w_out, bias_in, residual_logit, branch_scale)
    total = levels * half
    riding = block % 8 == 0 and levels == 5
    rider = struct((rows // 4, double), bf16)
    grad_state, send, *factors = call(
        functools.partial(switch_kernel, levels, block),
        [
            rider if riding else struct((rows, width), bf16),
            struct((units + rider.shape[0] * riding, double), bf16),
            struct((total, 2 * lanes), bf16),
            struct((total, units), bf16),
            struct((total, units), bf16),
            struct((total, double), bf16),
        ],
        scratch=[
            pltpu.VMEM((total, units), f32),
            pltpu.VMEM((2, total, lanes), f32),
            pltpu.VMEM((total, 1), f32),
            pltpu.VMEM((half, double), f32),
        ],
        specs=[SMEM] + [VMEM] * 8,
        grant=20,
    )(me, both, *parameters)
    keep = call(
        keep_kernel,
        struct((units, double), f32),
        specs=[SMEM] + [VMEM] * 4,
        grant=16,
        cost_estimate=pl.CostEstimate(
            flops=2 * total * units * double, bytes_accessed=8 * total * units, transcendentals=0
        ),
    )(me, *factors)
    factor = float(rows * size) ** (-0.5)
    if not riding:
        grad_state = lax.all_to_all(
            grad_state.reshape(size, block, width), "seq", split_axis=0, concat_axis=0, tiled=True
        ).reshape(rows, width)
    shapes = [struct((double, units), f32), struct((units, double), f32)]
    (grad_in, grad_out), grad_state = sum_over_devices(me, grad_state, keep, send, size, factor, riding, shapes)
    if riding:
        grad_state = call(
            functools.partial(unpack_kernel, block),
            struct((width, rows), bf16),
            scratch=[pltpu.VMEM((rows, width), f32)],
            specs=[SMEM] + [VMEM] * len(grad_state),
        )(me, *grad_state).T
    return (grad_state, grad_in, grad_out)


def solution(mesh):
    in_specs = (P("seq", None), P("seq", None), P(), P(), P(), P(), P())
    out_specs = (P("seq", None), P(), P())
    return jax.shard_map(shards, mesh=mesh, in_specs=in_specs, out_specs=out_specs, check_vma=False)
```

```python
import functools

import jax
import jax.numpy as jnp
from jax import lax
from jax.experimental import pallas as pl
from jax.experimental.pallas import tpu as pltpu
from jax.sharding import PartitionSpec as P

epsilon = 1e-05
tanh_scale = 0.7978845608028654
cubic_coef = 0.044715
f32 = jnp.float32
bf16 = jnp.bfloat16
VMEM = pl.BlockSpec(memory_space=pltpu.VMEM)
SMEM = pl.BlockSpec(memory_space=pltpu.SMEM)
HBM = pl.BlockSpec(memory_space=pltpu.HBM)
tile = 16


def dot(left, right, contract):
    return lax.dot_general(left, right, ((contract[:1], contract[1:]), ((), ())), preferred_element_type=f32)


def pair_rows(state, stride):
    rows, width = state.shape
    groups = rows // (2 * stride)
    if stride >= 8:
        viewed = state.reshape(groups, 2, stride, width)
        return [viewed[:, side].reshape(rows // 2, width) for side in (0, 1)]
    halves = []
    for side in (0, 1):
        row = lax.broadcasted_iota(jnp.int32, (rows // 2, rows), 0)
        col = lax.broadcasted_iota(jnp.int32, (rows // 2, rows), 1)
        pick = (row // stride) * (2 * stride) + row % stride + side * stride
        halves.append(dot((col == pick).astype(bf16), state.astype(bf16), (1, 0)))
    return halves


def unpair_rows(halves, stride):
    half, width = halves[0].shape
    if stride >= 8:
        parts = [part.reshape(half // stride, 1, stride, width) for part in halves]
        return jnp.concatenate(parts, axis=1).reshape(2 * half, width)
    total = jnp.zeros((2 * half, width), f32)
    for side, part in enumerate(halves):
        row = lax.broadcasted_iota(jnp.int32, (2 * half, half), 0)
        col = lax.broadcasted_iota(jnp.int32, (2 * half, half), 1)
        place = (col // stride) * (2 * stride) + col % stride + side * stride
        total = total + dot((row == place).astype(bf16), part.astype(bf16), (1, 0))
    return total


def mean_of(halves, count):
    return jnp.sum(halves[0] + halves[1], axis=-1, keepdims=True) * (1.0 / count)


def widen(part, lanes):
    rows, width = part.shape
    return part if width == lanes else jnp.concatenate([part, jnp.zeros((rows, lanes - width), part.dtype)], axis=1)


def pack_kernel(x_ref, g_ref, out_ref, x_s, g_s, sem):
    copies = [
        pltpu.make_async_copy(ref, scratch, sem.at[side])
        for side, (ref, scratch) in enumerate(((x_ref, x_s), (g_ref, g_s)))
    ]
    for copy in copies:
        copy.start()
    for copy in copies:
        copy.wait()
    both = jnp.concatenate([x_s[...], g_s[...]], axis=0).T
    out_ref[...] = both.astype(f32).reshape(out_ref.shape).astype(bf16)


def fetch_kernel(w_in_ref, w_out_ref, bias_ref, logit_ref, scale_ref, *refs):
    w_in_o, w_out_o, w_in_turned_o, w_out_turned_o, bias_o, gate_o, scale_o, w_in_s, w_out_s, sem = refs
    copies = [
        pltpu.make_async_copy(ref, to, sem.at[i])
        for i, (ref, to) in enumerate(((w_in_ref, w_in_s), (w_out_ref, w_out_s)))
    ]
    for copy in copies:
        copy.start()
    width, lanes = w_in_ref.shape[0] // 2, w_in_o.shape[0] // 2
    bias_o[...] = bias_ref[...].reshape(bias_o.shape)
    gate = jax.nn.sigmoid(logit_ref[...].reshape(1, 2 * width))
    scale = scale_ref[...].reshape(1, 2 * width)
    for copy in copies:
        copy.wait()
    for side in range(2):
        first, at = side * width, side * lanes
        gate_o[:, at : at + lanes] = widen(gate[:, first : first + width], lanes)
        scale_o[:, at : at + lanes] = widen(scale[:, first : first + width], lanes)
        w_out_o[:, at : at + lanes] = widen(w_out_s[:, first : first + width], lanes)
        w_in_o[at : at + width, :] = w_in_s[first : first + width, :]
        if lanes > width:
            w_in_o[at + width : at + lanes, :] = jnp.zeros((lanes - width, w_in_o.shape[1]), bf16)
    w_in_turned_o[...] = w_in_o[...].astype(f32).T.astype(bf16)
    w_out_turned_o[...] = w_out_o[...].astype(f32).T.astype(bf16)


def switch_kernel(
    levels, block, me_ref, both_ref, w_in_ref, w_out_ref, w_in_turned_ref, w_out_turned_ref, bias_ref, gate_ref, scale_ref,
    send_ref, low_s, pre_s, act_s, bg_s, upstream_ref, normed_ref, inverse_ref,
    slope_s, normed_s, inverse_s,
):
    half, double = upstream_ref.shape[1], bg_s.shape[1]
    rows, width = 2 * half, double // 2
    sides = range(2)
    lanes = w_in_ref.shape[0] // 2
    gate = [gate_ref[:, side * lanes : (side + 1) * lanes] for side in sides]
    scale = [scale_ref[:, side * lanes : (side + 1) * lanes] for side in sides]
    both = both_ref[...].astype(f32).reshape(rows, double)
    state = widen(both[:, :width], lanes)
    inside = lax.broadcasted_iota(jnp.int32, (half, lanes), 1) < width
    for level in range(levels):
        at = pl.ds(level * half, half)
        paired = pair_rows(state, block * 2**level)
        average = mean_of(paired, double)
        centered = [jnp.where(inside, part - average, 0.0) for part in paired]
        inverse = lax.rsqrt(mean_of([part * part for part in centered], double) + epsilon)
        normed = [part * inverse for part in centered]
        low = jnp.concatenate([part.astype(bf16) for part in normed], axis=1)
        low_s[at, :] = low
        inverse_s[at, :] = inverse
        for side in sides:
            normed_s[side, at, :] = normed[side]
        u = dot(low, w_in_ref[...], (1, 0)) + bias_ref[...]
        square = u * u
        tangent = jnp.tanh(u * (tanh_scale + tanh_scale * cubic_coef * square))
        rise = 0.5 + 0.5 * tangent
        value = u * rise
        act = value.astype(bf16)
        slope_s[at, :] = rise + value * (1.0 - tangent) * (tanh_scale + 3.0 * tanh_scale * cubic_coef * square)
        act_s[at, :] = act
        if level < levels - 1:
            branch = dot(act, w_out_ref[...], (1, 0))
            result = [
                (gate[side] * paired[side] + scale[side] * branch[:, side * lanes : (side + 1) * lanes])
                .astype(bf16)
                .astype(f32)
                for side in sides
            ]
            state = unpair_rows(result, block * 2**level)
    grad = widen(both[:, width:], lanes)
    for level in reversed(range(levels)):
        at = pl.ds(level * half, half)
        upstream = pair_rows(grad, block * 2**level)
        branch_grad = [(scale[side] * upstream[side]).astype(bf16) for side in sides]
        bg_s[at, :] = jnp.concatenate([part[:, :width] for part in branch_grad], axis=1)
        act_grad = dot(jnp.concatenate(branch_grad, axis=1), w_out_turned_ref[...], (1, 0))
        pre_grad = (act_grad * slope_s[at, :]).astype(bf16)
        pre_s[at, :] = pre_grad
        normed = [normed_s[side, at, :] for side in sides]
        if level > 0:
            result = input_grad(pre_grad, w_in_turned_ref, gate, upstream, normed, inverse_s[at, :], double)
            grad = unpair_rows(result, block * 2**level)
    for side in sides:
        upstream_ref[side] = upstream[side]
        normed_ref[side] = normed[side]
    inverse_ref[...] = inverse_s[0:half, :]
    put_products(me_ref[0] % 2 == 0, send_ref, low_s, pre_s, act_s, bg_s)


def input_grad(pre_grad, w_in_turned_ref, gate, upstream, normed, inverse, double):
    sides, lanes = range(2), w_in_turned_ref.shape[1] // 2
    normed_grad = dot(pre_grad, w_in_turned_ref[...], (1, 0))
    normed_grad = [normed_grad[:, side * lanes : (side + 1) * lanes] for side in sides]
    average = mean_of(normed_grad, double)
    product = mean_of([normed_grad[side] * normed[side] for side in sides], double)
    return [
        (gate[side] * upstream[side] + inverse * (normed_grad[side] - average - normed[side] * product))
        .astype(bf16)
        .astype(f32)
        for side in sides
    ]


def keep_kernel(me_ref, *refs):
    put_products(me_ref[0] % 2 == 1, refs[-1], *refs[:-1])


def first_kernel(
    block, me_ref, pre_ref, upstream_ref, normed_ref, inverse_ref, w_in_turned_ref, gate_ref, *refs
):
    *riders, paired_s = refs
    half, double = paired_s.shape
    width, lanes, sides = double // 2, upstream_ref.shape[2], range(2)
    gate = [gate_ref[:, side * lanes : (side + 1) * lanes] for side in sides]
    upstream, normed = [upstream_ref[side] for side in sides], [normed_ref[side] for side in sides]
    result = input_grad(pre_ref[0:half, :], w_in_turned_ref, gate, upstream, normed, inverse_ref[...], double)
    if len(riders) == 2:
        core = me_ref[0] % 2
        paired_s[:, :width] = jnp.where(core == 0, result[0], result[1])[:, :width]
        paired_s[:, width:] = jnp.where(core == 0, result[1], result[0])[:, :width]
        pairs = half // block
        kept, sent = [], []
        for low in range(pairs // 8):
            for plane in range(4):
                found = []
                for high in range(2):
                    chip = ((high * (pairs // 8) + low) * 4 + plane) ^ (me_ref[0] >> 1)
                    found.append(paired_s[pl.ds(pl.multiple_of(chip * block, 8), block), :])
                kept.append(jnp.concatenate([part[:, :width] for part in found], axis=1))
                sent.append(jnp.concatenate([part[:, width:] for part in found], axis=1))
        riders[0][...] = jnp.concatenate(kept, axis=0).astype(bf16)
        riders[1][...] = jnp.concatenate(sent, axis=0).astype(bf16)
    else:
        riders[0][...] = unpair_rows(result, block)[:, :width].astype(bf16)


def put_products(out_first, half_ref, low_ref, pre_ref, act_ref, bg_ref):
    units, double = pre_ref.shape[1], bg_ref.shape[1]
    width, lanes = double // 2, low_ref.shape[1] // 2

    @pl.when(out_first)
    def _():
        half_ref[0:units, :] = dot(act_ref[...], bg_ref[...], (0, 0)).astype(half_ref.dtype)

    @pl.when(jnp.logical_not(out_first))
    def _():
        grad_in = dot(low_ref[...], pre_ref[...], (0, 0))
        grad_in = jnp.concatenate([grad_in[side * lanes : side * lanes + width] for side in range(2)], axis=0)
        for first in range(0, units, double):
            half_ref[first : first + double, :] = grad_in[:, first : first + double].astype(half_ref.dtype)


def split_kernel(radix, shift, me_ref, keep_ref, arrived_ref, *outs):
    rows = outs[0].shape[0]
    place = (me_ref[0] >> shift) & (radix - 1)
    for other in range(radix):
        at = pl.ds(pl.multiple_of((place ^ other) * rows, tile), rows)
        total = keep_ref[at, :].astype(f32) + arrived_ref[at, :].astype(f32)
        outs[other][...] = total.astype(outs[other].dtype)


def cores_kernel(kept_ref, arrived_ref, *outs):
    width = kept_ref.shape[1] // 2
    sources = [kept_ref[...].astype(f32), arrived_ref[...].astype(f32)]
    for high in range(2):
        lanes = [source[:, high * width : (high + 1) * width] for source in sources]
        outs[high][...] = jnp.concatenate(lanes, axis=1).astype(bf16)


def total_of(refs):
    rows = refs[-1].shape[0]
    total = refs[0][0:rows, :].astype(f32)
    for ref in refs[1:-1]:
        total = total + ref[0:rows, :].astype(f32)
    return total


def total_kernel(factor, *refs):
    refs[-1][...] = (total_of(refs) * factor).astype(refs[-1].dtype)


def line_kernel(*refs):
    parts, sources, (out_ref, kept_ref) = refs[:-4], refs[-4:-2], refs[-2:]
    rows = parts[0].shape[0]
    out_ref[0:rows, :] = total_of([*parts, parts[0]]).astype(bf16)
    half = sources[0].shape[0] // 2
    for first, ref, at in ((0, kept_ref, 0), (half, out_ref, rows)):
        for source in sources:
            ref[at : at + half, :] = source[first : first + half, :]
            at += half


def plane_kernel(factor, *refs):
    parts, (kept_ref, came_ref), outs = refs[:2], refs[2:4], refs[4:]
    rows = outs[0].shape[0]
    mine = (total_of([*parts, outs[0]]) * factor).astype(bf16)
    outs[0][...] = mine
    sources = [kept_ref[...].astype(f32), came_ref[rows:, :].astype(f32)]
    block = sources[0].shape[0] // 8
    for plane in range(4):
        riders = jnp.concatenate(
            [
                source[(high * 4 + plane) * block : (high * 4 + plane + 1) * block]
                for source in sources
                for high in range(2)
            ],
            axis=0,
        ).astype(bf16)
        if plane == 0:
            outs[4][...] = riders
        else:
            outs[plane][0:rows, :] = mine
            outs[plane][rows:, :] = riders


def unpack_kernel(block, me_ref, *refs):
    parts, out_ref, rows_s = refs[:-2], refs[-2], refs[-1]
    width = rows_s.shape[1]
    for plane, part in enumerate(parts):
        values = part[part.shape[0] - 4 * block :, :].astype(f32)
        for low in range(2):
            for high in range(2):
                for core in range(2):
                    source = me_ref[0] ^ (high * 16 + low * 8 + plane * 2 + core)
                    first = (low * 2 + high) * block
                    rows_s[pl.ds(pl.multiple_of(source * block, 8), block), :] = values[
                        first : first + block, core * width : (core + 1) * width
                    ]
    out_ref[...] = rows_s[...].T.astype(bf16)


def place_kernel(bit, pieces, slots, placed, me_ref, *refs):
    parts, (in_ref, out_ref, wide_s, sem) = refs[: len(slots)], refs[len(slots) + placed :]
    step, double = wide_s.shape[1:]
    me = me_ref[0]
    base = (me >> bit) & (pieces - 1)
    for core in range(2):

        @pl.when(me % 2 == core)
        def _():
            copies = []
            for i, slot in enumerate(slots):
                first = ((slot % pieces) ^ base) * step
                if (slot >= pieces) == (core == 1):
                    lane = (first // double) * double
                    to = in_ref.at[
                        pl.ds(pl.multiple_of(first - lane, tile), step), pl.ds(pl.multiple_of(lane, 128), double)
                    ]
                else:
                    to = out_ref.at[pl.ds(pl.multiple_of(first, tile), step), :]
                wide_s[i] = parts[i][0:step, :].astype(f32)
                copy = pltpu.make_async_copy(wide_s.at[i], to, sem.at[i])
                copy.start()
                copies.append(copy)
            for copy in copies:
                copy.wait()


def place(me, shapes, quarters, slots, placed):
    pieces = len(quarters) // 2
    step, double = min(quarter.shape for quarter in quarters if quarter is not None)
    return call(
        functools.partial(place_kernel, 1, pieces, slots, len(placed)),
        shapes,
        scratch=[pltpu.VMEM((len(slots), step, double), f32), pltpu.SemaphoreType.DMA((len(slots),))],
        specs=[SMEM] + [VMEM] * len(slots) + [HBM] * len(placed),
        out_specs=[HBM] * 2,
        input_output_aliases={1 + len(slots) + i: i for i in range(len(placed))},
    )(me, *[quarters[slot] for slot in slots], *placed)


def call(kernel, outs, scratch=(), specs=None, count=0, grant=8, **more):
    return pl.pallas_call(
        kernel,
        out_shape=outs,
        in_specs=specs if specs is not None else [VMEM] * count,
        out_specs=more.pop("out_specs", jax.tree.map(lambda _: VMEM, outs)),
        scratch_shapes=list(scratch),
        compiler_params=pltpu.CompilerParams(vmem_limit_bytes=grant and grant * 2**20),
        **more,
    )


def struct(shape, dtype):
    return jax.ShapeDtypeStruct(shape, dtype)


def exchange(value, masks, size):
    return [lax.ppermute(value if not isinstance(value, list) else value[i], "seq",
                         [(d, d ^ mask) for d in range(size)]) for i, mask in enumerate(masks)]


def sum_over_devices(me, ride, ride_send, keep, send, size, factor, riding, shapes):
    bits = size.bit_length() - 1
    rows, double = keep.shape
    radix = min(4, size // 2)
    masks = [m << 1 for m in range(1, radix)]
    rows = rows // radix
    piece, rider = struct((rows, double), bf16), struct(ride.shape, bf16)
    (arrived,) = exchange([send], [1], size)
    if riding:
        (came,) = exchange([ride_send], [1], size)
        arrived, came = lax.optimization_barrier((arrived, came))
    pieces = call(
        functools.partial(split_kernel, radix, 1),
        [struct((rows, double), f32)] + [piece] * (radix - 1),
        specs=[SMEM, VMEM, VMEM],
    )(me, keep, arrived)
    parts = [pieces[0]] + exchange(list(pieces[1:]), masks, size)
    if riding:
        high = call(cores_kernel, [rider] * 2, count=2)(ride, came)
        riders = [high[0]] + exchange([high[1]], [16], size)
        total, kept = call(
            line_kernel, [struct((rows + ride.shape[0], double), bf16), rider], count=len(parts) + 2
        )(*parts, *riders)
        (came,) = exchange([total], [8], size)
        second = call(functools.partial(total_kernel, 1.0), piece, count=2)
        total = second(total, came)
        (last,) = exchange([total], [24], size)
        joined = struct((rows + ride.shape[0] // 2, double), bf16)
        mine, *sends, ride = call(
            functools.partial(plane_kernel, factor),
            [piece] + [joined] * 3 + [struct((ride.shape[0] // 2, double), bf16)],
            count=4,
        )(total, last, kept, came)
        got = exchange(sends, masks, size)
        ride = [ride] + got
    else:
        for rest in range(radix.bit_length(), bits):
            total = call(functools.partial(total_kernel, 1.0), piece, count=len(parts))(*parts)
            parts = [total] + exchange([total], [1 << rest], size)
        mine = call(functools.partial(total_kernel, factor), piece, count=len(parts))(*parts)
        mine, ride = lax.optimization_barrier((mine, ride))
        got = exchange([mine] * (radix - 1), masks, size)
    (first,) = exchange([mine], [1], size)
    got[0], first = lax.optimization_barrier((got[0], first))
    quarters = [mine] + got + [first] + [None] * (radix - 1)
    early = [slot for slot in (0, radix, 1) if riding]
    placed = place(me, shapes, quarters, early, []) if early else []
    if early:
        *got[1:], placed = lax.optimization_barrier((*got[1:], placed))
    quarters = [mine] + got + [first] + exchange(got, [1] * (radix - 1), size)
    placed = place(me, shapes, quarters, [slot for slot in range(2 * radix) if slot not in early], placed)
    return placed, ride


def shards(saved_input, cotangent, w_in, bias_in, w_out, residual_logit, branch_scale):
    size = lax.axis_size("seq")
    levels = size.bit_length() - 1
    rows, width = saved_input.shape
    double, units = w_in.shape
    block = rows // size
    half = rows // 2
    me = lax.axis_index("seq").astype(jnp.int32).reshape(1)
    if block % 8 == 0:
        both = call(
            pack_kernel,
            struct((size, block, double), bf16),
            scratch=[pltpu.VMEM((width, rows), bf16)] * 2 + [pltpu.SemaphoreType.DMA((2,))],
            specs=[HBM] * 2,
            grant=None,
            cost_estimate=pl.CostEstimate(flops=0, bytes_accessed=7 * 10**6, transcendentals=0),
        )(saved_input.T, cotangent.T)
    else:
        both = jnp.concatenate([saved_input, cotangent], axis=1).reshape(size, block, double)
    both = lax.all_to_all(both, "seq", split_axis=0, concat_axis=0, tiled=True)
    lanes = -(-width // 128) * 128
    parameters = call(
        fetch_kernel,
        [struct(shape, bf16) for shape in ((2 * lanes, units), (units, 2 * lanes)) + ((units, 2 * lanes), (2 * lanes, units))]
        + [struct((1, count), f32) for count in (units, 2 * lanes, 2 * lanes)],
        scratch=[pltpu.VMEM(w_in.shape, bf16), pltpu.VMEM(w_out.shape, bf16), pltpu.SemaphoreType.DMA((2,))],
        specs=[HBM] * 2 + [VMEM] * 3,
    )(w_in, w_out, bias_in, residual_logit, branch_scale)
    total = levels * half
    riding = block % 8 == 0 and levels == 5
    rider = struct((rows // 4, double), bf16)
    send, *factors = call(
        functools.partial(switch_kernel, levels, block),
        [
            struct((units, double), bf16),
            struct((total, 2 * lanes), bf16),
            struct((total, units), bf16),
            struct((total, units), bf16),
            struct((total, double), bf16),
            struct((2, half, lanes), f32),
            struct((2, half, lanes), f32),
            struct((half, 1), f32),
        ],
        scratch=[
            pltpu.VMEM((total, units), f32),
            pltpu.VMEM((2, total, lanes), f32),
            pltpu.VMEM((total, 1), f32),
        ],
        specs=[SMEM] + [VMEM] * 8,
        grant=20,
    )(me, both, *parameters)
    factors, rest = factors[:4], factors[4:]
    grad_state, *ride_send = call(
        functools.partial(first_kernel, block),
        [rider] * 2 if riding else [struct((rows, width), bf16)],
        scratch=[pltpu.VMEM((half, double), f32)],
        specs=[SMEM] + [VMEM] * 6,
        cost_estimate=pl.CostEstimate(flops=rows * units * double, bytes_accessed=rows * units, transcendentals=0),
    )(me, factors[1], *rest, parameters[2], parameters[5])
    keep = call(
        keep_kernel,
        struct((units, double), f32),
        specs=[SMEM] + [VMEM] * 4,
        grant=16,
        cost_estimate=pl.CostEstimate(
            flops=2 * total * units * double, bytes_accessed=8 * total * units, transcendentals=0
        ),
    )(me, *factors)
    ride_send = ride_send[0] if riding else None
    factor = float(rows * size) ** (-0.5)
    if not riding:
        grad_state = lax.all_to_all(
            grad_state.reshape(size, block, width), "seq", split_axis=0, concat_axis=0, tiled=True
        ).reshape(rows, width)
    shapes = [struct((double, units), f32), struct((units, double), f32)]
    (grad_in, grad_out), grad_state = sum_over_devices(me, grad_state, ride_send, keep, send, size, factor, riding, shapes)
    if riding:
        grad_state = call(
            functools.partial(unpack_kernel, block),
            struct((width, rows), bf16),
            scratch=[pltpu.VMEM((rows, width), f32)],
            specs=[SMEM] + [VMEM] * len(grad_state),
        )(me, *grad_state).T
    return (grad_state, grad_in, grad_out)


def solution(mesh):
    in_specs = (P("seq", None), P("seq", None), P(), P(), P(), P(), P())
    out_specs = (P("seq", None), P(), P())
    return jax.shard_map(shards, mesh=mesh, in_specs=in_specs, out_specs=out_specs, check_vma=False)
```

```python
import functools

import jax
import jax.numpy as jnp
from jax import lax
from jax.experimental import pallas as pl
from jax.experimental.pallas import tpu as pltpu
from jax.sharding import PartitionSpec as P

epsilon = 1e-05
tanh_scale = 0.7978845608028654
cubic_coef = 0.044715
f32 = jnp.float32
bf16 = jnp.bfloat16
VMEM = pl.BlockSpec(memory_space=pltpu.VMEM)
SMEM = pl.BlockSpec(memory_space=pltpu.SMEM)
HBM = pl.BlockSpec(memory_space=pltpu.HBM)
tile = 16


def dot(left, right, contract):
    return lax.dot_general(left, right, ((contract[:1], contract[1:]), ((), ())), preferred_element_type=f32)


def pair_rows(state, stride):
    rows, width = state.shape
    groups = rows // (2 * stride)
    if stride >= 8:
        viewed = state.reshape(groups, 2, stride, width)
        return [viewed[:, side].reshape(rows // 2, width) for side in (0, 1)]
    halves = []
    for side in (0, 1):
        row = lax.broadcasted_iota(jnp.int32, (rows // 2, rows), 0)
        col = lax.broadcasted_iota(jnp.int32, (rows // 2, rows), 1)
        pick = (row // stride) * (2 * stride) + row % stride + side * stride
        halves.append(dot((col == pick).astype(bf16), state.astype(bf16), (1, 0)))
    return halves


def unpair_rows(halves, stride):
    half, width = halves[0].shape
    if stride >= 8:
        parts = [part.reshape(half // stride, 1, stride, width) for part in halves]
        return jnp.concatenate(parts, axis=1).reshape(2 * half, width)
    total = jnp.zeros((2 * half, width), f32)
    for side, part in enumerate(halves):
        row = lax.broadcasted_iota(jnp.int32, (2 * half, half), 0)
        col = lax.broadcasted_iota(jnp.int32, (2 * half, half), 1)
        place = (col // stride) * (2 * stride) + col % stride + side * stride
        total = total + dot((row == place).astype(bf16), part.astype(bf16), (1, 0))
    return total


def mean_of(halves, count):
    return jnp.sum(halves[0] + halves[1], axis=-1, keepdims=True) * (1.0 / count)


def widen(part, lanes):
    rows, width = part.shape
    return part if width == lanes else jnp.concatenate([part, jnp.zeros((rows, lanes - width), part.dtype)], axis=1)


def pack_kernel(x_ref, g_ref, out_ref, x_s, g_s, sem):
    copies = [
        pltpu.make_async_copy(ref, scratch, sem.at[side])
        for side, (ref, scratch) in enumerate(((x_ref, x_s), (g_ref, g_s)))
    ]
    for copy in copies:
        copy.start()
    for copy in copies:
        copy.wait()
    both = jnp.concatenate([x_s[...], g_s[...]], axis=0).T
    out_ref[...] = both.astype(f32).reshape(out_ref.shape).astype(bf16)


def fetch_kernel(w_in_ref, w_out_ref, bias_ref, logit_ref, scale_ref, *refs):
    w_in_o, w_out_o, w_in_turned_o, w_out_turned_o, bias_o, gate_o, scale_o, w_in_s, w_out_s, sem = refs
    copies = [
        pltpu.make_async_copy(ref, to, sem.at[i])
        for i, (ref, to) in enumerate(((w_in_ref, w_in_s), (w_out_ref, w_out_s)))
    ]
    for copy in copies:
        copy.start()
    width, lanes = w_in_ref.shape[0] // 2, w_in_o.shape[0] // 2
    bias_o[...] = bias_ref[...].reshape(bias_o.shape)
    gate = jax.nn.sigmoid(logit_ref[...].reshape(1, 2 * width))
    scale = scale_ref[...].reshape(1, 2 * width)
    for copy in copies:
        copy.wait()
    for side in range(2):
        first, at = side * width, side * lanes
        gate_o[:, at : at + lanes] = widen(gate[:, first : first + width], lanes)
        scale_o[:, at : at + lanes] = widen(scale[:, first : first + width], lanes)
        w_out_o[:, at : at + lanes] = widen(w_out_s[:, first : first + width], lanes)
        w_in_o[at : at + width, :] = w_in_s[first : first + width, :]
        if lanes > width:
            w_in_o[at + width : at + lanes, :] = jnp.zeros((lanes - width, w_in_o.shape[1]), bf16)
    w_in_turned_o[...] = w_in_o[...].astype(f32).T.astype(bf16)
    w_out_turned_o[...] = w_out_o[...].astype(f32).T.astype(bf16)


def switch_kernel(
    levels, block, me_ref, both_ref, w_in_ref, w_out_ref, w_in_turned_ref, w_out_turned_ref, bias_ref, gate_ref, scale_ref,
    send_ref, low_s, pre_s, act_s, bg_s, upstream_ref, normed_ref, inverse_ref,
    slope_s, normed_s, inverse_s,
):
    half, double = upstream_ref.shape[1], bg_s.shape[1]
    rows, width = 2 * half, double // 2
    sides = range(2)
    lanes = w_in_ref.shape[0] // 2
    gate = [gate_ref[:, side * lanes : (side + 1) * lanes] for side in sides]
    scale = [scale_ref[:, side * lanes : (side + 1) * lanes] for side in sides]
    both = both_ref[...].astype(f32).reshape(rows, double)
    state = widen(both[:, :width], lanes)
    inside = lax.broadcasted_iota(jnp.int32, (half, lanes), 1) < width
    for level in range(levels):
        at = pl.ds(level * half, half)
        paired = pair_rows(state, block * 2**level)
        average = mean_of(paired, double)
        centered = [jnp.where(inside, part - average, 0.0) for part in paired]
        inverse = lax.rsqrt(mean_of([part * part for part in centered], double) + epsilon)
        normed = [part * inverse for part in centered]
        low = jnp.concatenate([part.astype(bf16) for part in normed], axis=1)
        low_s[at, :] = low
        inverse_s[at, :] = inverse
        for side in sides:
            normed_s[side, at, :] = normed[side]
        u = dot(low, w_in_ref[...], (1, 0)) + bias_ref[...]
        square = u * u
        tangent = jnp.tanh(u * (tanh_scale + tanh_scale * cubic_coef * square))
        rise = 0.5 + 0.5 * tangent
        value = u * rise
        act = value.astype(bf16)
        slope_s[at, :] = rise + value * (1.0 - tangent) * (tanh_scale + 3.0 * tanh_scale * cubic_coef * square)
        act_s[at, :] = act
        if level < levels - 1:
            branch = dot(act, w_out_ref[...], (1, 0))
            result = [
                (gate[side] * paired[side] + scale[side] * branch[:, side * lanes : (side + 1) * lanes])
                .astype(bf16)
                .astype(f32)
                for side in sides
            ]
            state = unpair_rows(result, block * 2**level)
    grad = widen(both[:, width:], lanes)
    for level in reversed(range(levels)):
        at = pl.ds(level * half, half)
        upstream = pair_rows(grad, block * 2**level)
        branch_grad = [(scale[side] * upstream[side]).astype(bf16) for side in sides]
        bg_s[at, :] = jnp.concatenate([part[:, :width] for part in branch_grad], axis=1)
        act_grad = dot(jnp.concatenate(branch_grad, axis=1), w_out_turned_ref[...], (1, 0))
        pre_grad = (act_grad * slope_s[at, :]).astype(bf16)
        pre_s[at, :] = pre_grad
        normed = [normed_s[side, at, :] for side in sides]
        if level > 0:
            result = input_grad(pre_grad, w_in_turned_ref, gate, upstream, normed, inverse_s[at, :], double)
            grad = unpair_rows(result, block * 2**level)
    for side in sides:
        upstream_ref[side] = upstream[side]
        normed_ref[side] = normed[side]
    inverse_ref[...] = inverse_s[0:half, :]
    put_products(me_ref[0] % 2 == 0, send_ref, low_s, pre_s, act_s, bg_s)


def input_grad(pre_grad, w_in_turned_ref, gate, upstream, normed, inverse, double):
    sides, lanes = range(2), w_in_turned_ref.shape[1] // 2
    normed_grad = dot(pre_grad, w_in_turned_ref[...], (1, 0))
    normed_grad = [normed_grad[:, side * lanes : (side + 1) * lanes] for side in sides]
    average = mean_of(normed_grad, double)
    product = mean_of([normed_grad[side] * normed[side] for side in sides], double)
    return [
        (gate[side] * upstream[side] + inverse * (normed_grad[side] - average - normed[side] * product))
        .astype(bf16)
        .astype(f32)
        for side in sides
    ]


def keep_kernel(me_ref, *refs):
    put_products(me_ref[0] % 2 == 1, refs[-1], *refs[:-1])


def first_kernel(
    block, me_ref, pre_ref, upstream_ref, normed_ref, inverse_ref, w_in_turned_ref, gate_ref, *refs
):
    *riders, paired_s = refs
    half, double = paired_s.shape
    width, lanes, sides = double // 2, upstream_ref.shape[2], range(2)
    gate = [gate_ref[:, side * lanes : (side + 1) * lanes] for side in sides]
    upstream, normed = [upstream_ref[side] for side in sides], [normed_ref[side] for side in sides]
    result = input_grad(pre_ref[0:half, :], w_in_turned_ref, gate, upstream, normed, inverse_ref[...], double)
    if len(riders) == 2:
        core = me_ref[0] % 2
        paired_s[:, :width] = jnp.where(core == 0, result[0], result[1])[:, :width]
        paired_s[:, width:] = jnp.where(core == 0, result[1], result[0])[:, :width]
        pairs = half // block
        kept, sent = [], []
        for low in range(pairs // 8):
            for plane in range(4):
                found = []
                for high in range(2):
                    chip = ((high * (pairs // 8) + low) * 4 + plane) ^ (me_ref[0] >> 1)
                    found.append(paired_s[pl.ds(pl.multiple_of(chip * block, 8), block), :])
                kept.append(jnp.concatenate([part[:, :width] for part in found], axis=1))
                sent.append(jnp.concatenate([part[:, width:] for part in found], axis=1))
        riders[0][...] = jnp.concatenate(kept, axis=0).astype(bf16)
        riders[1][...] = jnp.concatenate(sent, axis=0).astype(bf16)
    else:
        riders[0][...] = unpair_rows(result, block)[:, :width].astype(bf16)


def put_products(out_first, half_ref, low_ref, pre_ref, act_ref, bg_ref):
    units, double = pre_ref.shape[1], bg_ref.shape[1]
    width, lanes = double // 2, low_ref.shape[1] // 2

    @pl.when(out_first)
    def _():
        half_ref[0:units, :] = dot(act_ref[...], bg_ref[...], (0, 0)).astype(half_ref.dtype)

    @pl.when(jnp.logical_not(out_first))
    def _():
        grad_in = dot(low_ref[...], pre_ref[...], (0, 0))
        grad_in = jnp.concatenate([grad_in[side * lanes : side * lanes + width] for side in range(2)], axis=0)
        for first in range(0, units, double):
            half_ref[first : first + double, :] = grad_in[:, first : first + double].astype(half_ref.dtype)


def split_kernel(radix, shift, me_ref, keep_ref, arrived_ref, *outs):
    rows = outs[0].shape[0]
    place = (me_ref[0] >> shift) & (radix - 1)
    for other in range(radix):
        at = pl.ds(pl.multiple_of((place ^ other) * rows, tile), rows)
        total = keep_ref[at, :].astype(f32) + arrived_ref[at, :].astype(f32)
        outs[other][...] = total.astype(outs[other].dtype)


def cores_kernel(kept_ref, arrived_ref, *outs):
    width = kept_ref.shape[1] // 2
    sources = [kept_ref[...].astype(f32), arrived_ref[...].astype(f32)]
    for high in range(2):
        lanes = [source[:, high * width : (high + 1) * width] for source in sources]
        outs[high][...] = jnp.concatenate(lanes, axis=1).astype(bf16)


def total_of(refs):
    rows = refs[-1].shape[0]
    total = refs[0][0:rows, :].astype(f32)
    for ref in refs[1:-1]:
        total = total + ref[0:rows, :].astype(f32)
    return total


def total_kernel(factor, *refs):
    refs[-1][...] = (total_of(refs) * factor).astype(refs[-1].dtype)


def line_kernel(*refs):
    parts, sources, (out_ref, kept_ref, sent_ref) = refs[:-5], refs[-5:-3], refs[-3:]
    out_ref[...] = total_of([*parts, out_ref]).astype(bf16)
    half = sources[0].shape[0] // 2
    for first, ref in ((0, kept_ref), (half, sent_ref)):
        for i, source in enumerate(sources):
            ref[i * half : (i + 1) * half, :] = source[first : first + half, :]


def plane_kernel(factor, *refs):
    parts, (kept_ref, came_ref), outs = refs[:2], refs[2:4], refs[4:]
    rows = outs[0].shape[0]
    mine = (total_of([*parts, outs[0]]) * factor).astype(bf16)
    outs[0][...] = mine
    sources = [kept_ref[...].astype(f32), came_ref[...].astype(f32)]
    block = sources[0].shape[0] // 8
    for plane in range(4):
        riders = jnp.concatenate(
            [
                source[(high * 4 + plane) * block : (high * 4 + plane + 1) * block]
                for source in sources
                for high in range(2)
            ],
            axis=0,
        ).astype(bf16)
        if plane == 0:
            outs[4][...] = riders
        else:
            outs[plane][0:rows, :] = mine
            outs[plane][rows:, :] = riders


def unpack_kernel(block, me_ref, *refs):
    parts, out_ref, rows_s = refs[:-2], refs[-2], refs[-1]
    width = rows_s.shape[1]
    for plane, part in enumerate(parts):
        values = part[part.shape[0] - 4 * block :, :].astype(f32)
        for low in range(2):
            for high in range(2):
                for core in range(2):
                    source = me_ref[0] ^ (high * 16 + low * 8 + plane * 2 + core)
                    first = (low * 2 + high) * block
                    rows_s[pl.ds(pl.multiple_of(source * block, 8), block), :] = values[
                        first : first + block, core * width : (core + 1) * width
                    ]
    out_ref[...] = rows_s[...].T.astype(bf16)


def place_kernel(bit, pieces, slots, placed, me_ref, *refs):
    parts, (in_ref, out_ref, wide_s, sem) = refs[: len(slots)], refs[len(slots) + placed :]
    step, double = wide_s.shape[1:]
    me = me_ref[0]
    base = (me >> bit) & (pieces - 1)
    for core in range(2):

        @pl.when(me % 2 == core)
        def _():
            copies = []
            for i, slot in enumerate(slots):
                first = ((slot % pieces) ^ base) * step
                if (slot >= pieces) == (core == 1):
                    lane = (first // double) * double
                    to = in_ref.at[
                        pl.ds(pl.multiple_of(first - lane, tile), step), pl.ds(pl.multiple_of(lane, 128), double)
                    ]
                else:
                    to = out_ref.at[pl.ds(pl.multiple_of(first, tile), step), :]
                wide_s[i] = parts[i][0:step, :].astype(f32)
                copy = pltpu.make_async_copy(wide_s.at[i], to, sem.at[i])
                copy.start()
                copies.append(copy)
            for copy in copies:
                copy.wait()


def place(me, shapes, quarters, slots, placed):
    pieces = len(quarters) // 2
    step, double = min(quarter.shape for quarter in quarters if quarter is not None)
    return call(
        functools.partial(place_kernel, 1, pieces, slots, len(placed)),
        shapes,
        scratch=[pltpu.VMEM((len(slots), step, double), f32), pltpu.SemaphoreType.DMA((len(slots),))],
        specs=[SMEM] + [VMEM] * len(slots) + [HBM] * len(placed),
        out_specs=[HBM] * 2,
        input_output_aliases={1 + len(slots) + i: i for i in range(len(placed))},
    )(me, *[quarters[slot] for slot in slots], *placed)


def call(kernel, outs, scratch=(), specs=None, count=0, grant=8, **more):
    return pl.pallas_call(
        kernel,
        out_shape=outs,
        in_specs=specs if specs is not None else [VMEM] * count,
        out_specs=more.pop("out_specs", jax.tree.map(lambda _: VMEM, outs)),
        scratch_shapes=list(scratch),
        compiler_params=pltpu.CompilerParams(vmem_limit_bytes=grant and grant * 2**20),
        **more,
    )


def struct(shape, dtype):
    return jax.ShapeDtypeStruct(shape, dtype)


def exchange(value, masks, size):
    return [lax.ppermute(value if not isinstance(value, list) else value[i], "seq",
                         [(d, d ^ mask) for d in range(size)]) for i, mask in enumerate(masks)]


def sum_over_devices(me, ride, ride_send, keep, send, size, factor, riding, shapes):
    bits = size.bit_length() - 1
    rows, double = keep.shape
    radix = min(4, size // 2)
    masks = [m << 1 for m in range(1, radix)]
    rows = rows // radix
    piece, rider = struct((rows, double), bf16), struct(ride.shape, bf16)
    (arrived,) = exchange([send], [1], size)
    if riding:
        (came,) = exchange([ride_send], [1], size)
        arrived, came = lax.optimization_barrier((arrived, came))
    pieces = call(
        functools.partial(split_kernel, radix, 1),
        [struct((rows, double), f32)] + [piece] * (radix - 1),
        specs=[SMEM, VMEM, VMEM],
    )(me, keep, arrived)
    parts = [pieces[0]] + exchange(list(pieces[1:]), masks, size)
    if riding:
        high = call(cores_kernel, [rider] * 2, count=2)(ride, came)
        riders = [high[0]] + exchange([high[1]], [16], size)
        parts, riders = lax.optimization_barrier((parts, riders))
        total = call(functools.partial(total_kernel, 1.0), piece, count=len(parts))(*parts)
        (came,) = exchange([total], [8], size)
        total, kept, sent = call(line_kernel, [piece, rider, rider], count=4)(total, came, *riders)
        last, came = exchange([total, sent], [24, 8], size)
        joined = struct((rows + ride.shape[0] // 2, double), bf16)
        mine, *sends, ride = call(
            functools.partial(plane_kernel, factor),
            [piece] + [joined] * 3 + [struct((ride.shape[0] // 2, double), bf16)],
            count=4,
        )(total, last, kept, came)
        got = exchange(sends, masks, size)
        ride = [ride] + got
    else:
        for rest in range(radix.bit_length(), bits):
            total = call(functools.partial(total_kernel, 1.0), piece, count=len(parts))(*parts)
            parts = [total] + exchange([total], [1 << rest], size)
        mine = call(functools.partial(total_kernel, factor), piece, count=len(parts))(*parts)
        mine, ride = lax.optimization_barrier((mine, ride))
        got = exchange([mine] * (radix - 1), masks, size)
    (first,) = exchange([mine], [1], size)
    got[0], first = lax.optimization_barrier((got[0], first))
    quarters = [mine] + got + [first] + [None] * (radix - 1)
    early = [slot for slot in (0, radix, 1) if riding]
    placed = place(me, shapes, quarters, early, []) if early else []
    if early:
        *got[1:], placed = lax.optimization_barrier((*got[1:], placed))
    quarters = [mine] + got + [first] + exchange(got, [1] * (radix - 1), size)
    placed = place(me, shapes, quarters, [slot for slot in range(2 * radix) if slot not in early], placed)
    return placed, ride


def shards(saved_input, cotangent, w_in, bias_in, w_out, residual_logit, branch_scale):
    size = lax.axis_size("seq")
    levels = size.bit_length() - 1
    rows, width = saved_input.shape
    double, units = w_in.shape
    block = rows // size
    half = rows // 2
    me = lax.axis_index("seq").astype(jnp.int32).reshape(1)
    if block % 8 == 0:
        both = call(
            pack_kernel,
            struct((size, block, double), bf16),
            scratch=[pltpu.VMEM((width, rows), bf16)] * 2 + [pltpu.SemaphoreType.DMA((2,))],
            specs=[HBM] * 2,
            grant=None,
            cost_estimate=pl.CostEstimate(flops=0, bytes_accessed=7 * 10**6, transcendentals=0),
        )(saved_input.T, cotangent.T)
    else:
        both = jnp.concatenate([saved_input, cotangent], axis=1).reshape(size, block, double)
    both = lax.all_to_all(both, "seq", split_axis=0, concat_axis=0, tiled=True)
    lanes = -(-width // 128) * 128
    parameters = call(
        fetch_kernel,
        [struct(shape, bf16) for shape in ((2 * lanes, units), (units, 2 * lanes)) + ((units, 2 * lanes), (2 * lanes, units))]
        + [struct((1, count), f32) for count in (units, 2 * lanes, 2 * lanes)],
        scratch=[pltpu.VMEM(w_in.shape, bf16), pltpu.VMEM(w_out.shape, bf16), pltpu.SemaphoreType.DMA((2,))],
        specs=[HBM] * 2 + [VMEM] * 3,
    )(w_in, w_out, bias_in, residual_logit, branch_scale)
    total = levels * half
    riding = block % 8 == 0 and levels == 5
    rider = struct((rows // 4, double), bf16)
    send, *factors = call(
        functools.partial(switch_kernel, levels, block),
        [
            struct((units, double), bf16),
            struct((total, 2 * lanes), bf16),
            struct((total, units), bf16),
            struct((total, units), bf16),
            struct((total, double), bf16),
            struct((2, half, lanes), f32),
            struct((2, half, lanes), f32),
            struct((half, 1), f32),
        ],
        scratch=[
            pltpu.VMEM((total, units), f32),
            pltpu.VMEM((2, total, lanes), f32),
            pltpu.VMEM((total, 1), f32),
        ],
        specs=[SMEM] + [VMEM] * 8,
        grant=20,
    )(me, both, *parameters)
    factors, rest = factors[:4], factors[4:]
    grad_state, *ride_send = call(
        functools.partial(first_kernel, block),
        [rider] * 2 if riding else [struct((rows, width), bf16)],
        scratch=[pltpu.VMEM((half, double), f32)],
        specs=[SMEM] + [VMEM] * 6,
        cost_estimate=pl.CostEstimate(flops=rows * units * double, bytes_accessed=rows * units, transcendentals=0),
    )(me, factors[1], *rest, parameters[2], parameters[5])
    keep = call(
        keep_kernel,
        struct((units, double), f32),
        specs=[SMEM] + [VMEM] * 4,
        grant=16,
        cost_estimate=pl.CostEstimate(
            flops=2 * total * units * double, bytes_accessed=8 * total * units, transcendentals=0
        ),
    )(me, *factors)
    ride_send = ride_send[0] if riding else None
    factor = float(rows * size) ** (-0.5)
    if not riding:
        grad_state = lax.all_to_all(
            grad_state.reshape(size, block, width), "seq", split_axis=0, concat_axis=0, tiled=True
        ).reshape(rows, width)
    shapes = [struct((double, units), f32), struct((units, double), f32)]
    (grad_in, grad_out), grad_state = sum_over_devices(me, grad_state, ride_send, keep, send, size, factor, riding, shapes)
    if riding:
        grad_state = call(
            functools.partial(unpack_kernel, block),
            struct((width, rows), bf16),
            scratch=[pltpu.VMEM((rows, width), f32)],
            specs=[SMEM] + [VMEM] * len(grad_state),
        )(me, *grad_state).T
    return (grad_state, grad_in, grad_out)


def solution(mesh):
    in_specs = (P("seq", None), P("seq", None), P(), P(), P(), P(), P())
    out_specs = (P("seq", None), P(), P())
    return jax.shard_map(shards, mesh=mesh, in_specs=in_specs, out_specs=out_specs, check_vma=False)
```

```python
import functools

import jax
import jax.numpy as jnp
from jax import lax
from jax.experimental import pallas as pl
from jax.experimental.pallas import tpu as pltpu
from jax.sharding import PartitionSpec as P

epsilon = 1e-05
tanh_scale = 0.7978845608028654
cubic_coef = 0.044715
f32 = jnp.float32
bf16 = jnp.bfloat16
VMEM = pl.BlockSpec(memory_space=pltpu.VMEM)
SMEM = pl.BlockSpec(memory_space=pltpu.SMEM)
HBM = pl.BlockSpec(memory_space=pltpu.HBM)
tile = 16


def dot(left, right, contract):
    return lax.dot_general(left, right, ((contract[:1], contract[1:]), ((), ())), preferred_element_type=f32)


def pair_rows(state, stride):
    rows, width = state.shape
    groups = rows // (2 * stride)
    if stride >= 8:
        viewed = state.reshape(groups, 2, stride, width)
        return [viewed[:, side].reshape(rows // 2, width) for side in (0, 1)]
    halves = []
    for side in (0, 1):
        row = lax.broadcasted_iota(jnp.int32, (rows // 2, rows), 0)
        col = lax.broadcasted_iota(jnp.int32, (rows // 2, rows), 1)
        pick = (row // stride) * (2 * stride) + row % stride + side * stride
        halves.append(dot((col == pick).astype(bf16), state.astype(bf16), (1, 0)))
    return halves


def unpair_rows(halves, stride):
    half, width = halves[0].shape
    if stride >= 8:
        parts = [part.reshape(half // stride, 1, stride, width) for part in halves]
        return jnp.concatenate(parts, axis=1).reshape(2 * half, width)
    total = jnp.zeros((2 * half, width), f32)
    for side, part in enumerate(halves):
        row = lax.broadcasted_iota(jnp.int32, (2 * half, half), 0)
        col = lax.broadcasted_iota(jnp.int32, (2 * half, half), 1)
        place = (col // stride) * (2 * stride) + col % stride + side * stride
        total = total + dot((row == place).astype(bf16), part.astype(bf16), (1, 0))
    return total


def mean_of(halves, count):
    return jnp.sum(halves[0] + halves[1], axis=-1, keepdims=True) * (1.0 / count)


def widen(part, lanes):
    rows, width = part.shape
    return part if width == lanes else jnp.concatenate([part, jnp.zeros((rows, lanes - width), part.dtype)], axis=1)


def pack_kernel(x_ref, g_ref, out_ref, both_s, rows_s, in_sem, out_sem):
    width, count = x_ref.shape[0], in_sem.shape[1]
    some = width // count
    loads = [
        pltpu.make_async_copy(
            ref.at[part * some : (part + 1) * some, :],
            both_s.at[side * width + part * some : side * width + (part + 1) * some, :],
            in_sem.at[side, part],
        )
        for side, ref in enumerate((x_ref, g_ref))
        for part in range(count)
    ]
    for load in loads:
        load.start()
    for load in loads:
        load.wait()
    blocks = rows_s.shape[1]
    stores = []
    for part in range(rows_s.shape[0]):
        positions = blocks * rows_s.shape[2]
        turned = both_s[:, part * positions : (part + 1) * positions].T
        rows_s[part] = turned.astype(f32).reshape(rows_s.shape[1:]).astype(bf16)
        store = pltpu.make_async_copy(
            rows_s.at[part], out_ref.at[part * blocks : (part + 1) * blocks], out_sem.at[part]
        )
        store.start()
        stores.append(store)
    for store in stores:
        store.wait()


def fetch_kernel(w_in_ref, w_out_ref, bias_ref, logit_ref, scale_ref, *refs):
    w_in_o, w_out_o, w_in_turned_o, w_out_turned_o, bias_o, gate_o, scale_o, w_in_s, w_out_s, sem = refs
    copies = [
        pltpu.make_async_copy(ref, to, sem.at[i])
        for i, (ref, to) in enumerate(((w_in_ref, w_in_s), (w_out_ref, w_out_s)))
    ]
    for copy in copies:
        copy.start()
    width, lanes = w_in_ref.shape[0] // 2, w_in_o.shape[0] // 2
    bias_o[...] = bias_ref[...].reshape(bias_o.shape)
    gate = jax.nn.sigmoid(logit_ref[...].reshape(1, 2 * width))
    scale = scale_ref[...].reshape(1, 2 * width)
    for copy in copies:
        copy.wait()
    for side in range(2):
        first, at = side * width, side * lanes
        gate_o[:, at : at + lanes] = widen(gate[:, first : first + width], lanes)
        scale_o[:, at : at + lanes] = widen(scale[:, first : first + width], lanes)
        w_out_o[:, at : at + lanes] = widen(w_out_s[:, first : first + width], lanes)
        w_in_o[at : at + width, :] = w_in_s[first : first + width, :]
        if lanes > width:
            w_in_o[at + width : at + lanes, :] = jnp.zeros((lanes - width, w_in_o.shape[1]), bf16)
    w_in_turned_o[...] = w_in_o[...].astype(f32).T.astype(bf16)
    w_out_turned_o[...] = w_out_o[...].astype(f32).T.astype(bf16)


def switch_kernel(
    levels, block, me_ref, both_ref, w_in_ref, w_out_ref, w_in_turned_ref, w_out_turned_ref, bias_ref, gate_ref, scale_ref,
    send_ref, low_s, pre_s, act_s, bg_s, upstream_ref, normed_ref, inverse_ref,
    slope_s, normed_s, inverse_s,
):
    half, double = upstream_ref.shape[1], bg_s.shape[1]
    rows, width = 2 * half, double // 2
    sides = range(2)
    lanes = w_in_ref.shape[0] // 2
    gate = [gate_ref[:, side * lanes : (side + 1) * lanes] for side in sides]
    scale = [scale_ref[:, side * lanes : (side + 1) * lanes] for side in sides]
    both = both_ref[...].astype(f32).reshape(rows, double)
    state = widen(both[:, :width], lanes)
    inside = lax.broadcasted_iota(jnp.int32, (half, lanes), 1) < width
    for level in range(levels):
        at = pl.ds(level * half, half)
        paired = pair_rows(state, block * 2**level)
        average = mean_of(paired, double)
        centered = [jnp.where(inside, part - average, 0.0) for part in paired]
        inverse = lax.rsqrt(mean_of([part * part for part in centered], double) + epsilon)
        normed = [part * inverse for part in centered]
        low = jnp.concatenate([part.astype(bf16) for part in normed], axis=1)
        low_s[at, :] = jnp.concatenate([part[:, :width].astype(bf16) for part in normed], axis=1)
        inverse_s[at, :] = inverse
        for side in sides:
            normed_s[side, at, :] = normed[side]
        u = dot(low, w_in_ref[...], (1, 0)) + bias_ref[...]
        square = u * u
        tangent = jnp.tanh(u * (tanh_scale + tanh_scale * cubic_coef * square))
        rise = 0.5 + 0.5 * tangent
        value = u * rise
        act = value.astype(bf16)
        slope_s[at, :] = rise + value * (1.0 - tangent) * (tanh_scale + 3.0 * tanh_scale * cubic_coef * square)
        act_s[at, :] = act
        if level < levels - 1:
            branch = dot(act, w_out_ref[...], (1, 0))
            result = [
                (gate[side] * paired[side] + scale[side] * branch[:, side * lanes : (side + 1) * lanes])
                .astype(bf16)
                .astype(f32)
                for side in sides
            ]
            state = unpair_rows(result, block * 2**level)
    grad = widen(both[:, width:], lanes)
    for level in reversed(range(levels)):
        at = pl.ds(level * half, half)
        upstream = pair_rows(grad, block * 2**level)
        branch_grad = [(scale[side] * upstream[side]).astype(bf16) for side in sides]
        bg_s[at, :] = jnp.concatenate([part[:, :width] for part in branch_grad], axis=1)
        act_grad = dot(jnp.concatenate(branch_grad, axis=1), w_out_turned_ref[...], (1, 0))
        pre_grad = (act_grad * slope_s[at, :]).astype(bf16)
        pre_s[at, :] = pre_grad
        normed = [normed_s[side, at, :] for side in sides]
        if level > 0:
            result = input_grad(pre_grad, w_in_turned_ref, gate, upstream, normed, inverse_s[at, :], double)
            grad = unpair_rows(result, block * 2**level)
    for side in sides:
        upstream_ref[side] = upstream[side]
        normed_ref[side] = normed[side]
    inverse_ref[...] = inverse_s[0:half, :]
    put_products(me_ref[0] % 2 == 0, send_ref, low_s, pre_s, act_s, bg_s)


def input_grad(pre_grad, w_in_turned_ref, gate, upstream, normed, inverse, double):
    sides, lanes = range(2), w_in_turned_ref.shape[1] // 2
    normed_grad = dot(pre_grad, w_in_turned_ref[...], (1, 0))
    normed_grad = [normed_grad[:, side * lanes : (side + 1) * lanes] for side in sides]
    average = mean_of(normed_grad, double)
    product = mean_of([normed_grad[side] * normed[side] for side in sides], double)
    return [
        (gate[side] * upstream[side] + inverse * (normed_grad[side] - average - normed[side] * product))
        .astype(bf16)
        .astype(f32)
        for side in sides
    ]


def keep_kernel(me_ref, *refs):
    put_products(me_ref[0] % 2 == 1, refs[-1], *refs[:-1])


def first_kernel(
    block, me_ref, pre_ref, upstream_ref, normed_ref, inverse_ref, w_in_turned_ref, gate_ref, *refs
):
    *riders, paired_s = refs
    half, double = paired_s.shape
    width, lanes, sides = double // 2, upstream_ref.shape[2], range(2)
    gate = [gate_ref[:, side * lanes : (side + 1) * lanes] for side in sides]
    upstream, normed = [upstream_ref[side] for side in sides], [normed_ref[side] for side in sides]
    result = input_grad(pre_ref[0:half, :], w_in_turned_ref, gate, upstream, normed, inverse_ref[...], double)
    if len(riders) == 2:
        core = me_ref[0] % 2
        paired_s[:, :width] = jnp.where(core == 0, result[0], result[1])[:, :width]
        paired_s[:, width:] = jnp.where(core == 0, result[1], result[0])[:, :width]
        pairs = half // block
        kept, sent = [], []
        for low in range(pairs // 8):
            for plane in range(4):
                found = []
                for high in range(2):
                    chip = ((high * (pairs // 8) + low) * 4 + plane) ^ (me_ref[0] >> 1)
                    found.append(paired_s[pl.ds(pl.multiple_of(chip * block, 8), block), :])
                kept.append(jnp.concatenate([part[:, :width] for part in found], axis=1))
                sent.append(jnp.concatenate([part[:, width:] for part in found], axis=1))
        riders[0][...] = jnp.concatenate(kept, axis=0).astype(bf16)
        riders[1][...] = jnp.concatenate(sent, axis=0).astype(bf16)
    else:
        riders[0][...] = unpair_rows(result, block)[:, :width].astype(bf16)


def put_products(out_first, half_ref, low_ref, pre_ref, act_ref, bg_ref):
    units, double = pre_ref.shape[1], bg_ref.shape[1]

    @pl.when(out_first)
    def _():
        half_ref[0:units, :] = dot(act_ref[...], bg_ref[...], (0, 0)).astype(half_ref.dtype)

    @pl.when(jnp.logical_not(out_first))
    def _():
        grad_in = dot(low_ref[...], pre_ref[...], (0, 0))
        for first in range(0, units, double):
            half_ref[first : first + double, :] = grad_in[:, first : first + double].astype(half_ref.dtype)


def split_kernel(radix, shift, me_ref, keep_ref, arrived_ref, *outs):
    rows = outs[0].shape[0]
    place = (me_ref[0] >> shift) & (radix - 1)
    for other in range(radix):
        at = pl.ds(pl.multiple_of((place ^ other) * rows, tile), rows)
        total = keep_ref[at, :].astype(f32) + arrived_ref[at, :].astype(f32)
        outs[other][...] = total.astype(outs[other].dtype)


def cores_kernel(kept_ref, arrived_ref, *outs):
    width = kept_ref.shape[1] // 2
    sources = [kept_ref[...].astype(f32), arrived_ref[...].astype(f32)]
    for high in range(2):
        lanes = [source[:, high * width : (high + 1) * width] for source in sources]
        outs[high][...] = jnp.concatenate(lanes, axis=1).astype(bf16)


def total_of(refs):
    rows = refs[-1].shape[0]
    total = refs[0][0:rows, :].astype(f32)
    for ref in refs[1:-1]:
        total = total + ref[0:rows, :].astype(f32)
    return total


def total_kernel(factor, *refs):
    refs[-1][...] = (total_of(refs) * factor).astype(refs[-1].dtype)


def line_kernel(*refs):
    parts, sources, (out_ref, kept_ref, sent_ref) = refs[:-5], refs[-5:-3], refs[-3:]
    out_ref[...] = total_of([*parts, out_ref]).astype(bf16)
    half = sources[0].shape[0] // 2
    for first, ref in ((0, kept_ref), (half, sent_ref)):
        for i, source in enumerate(sources):
            ref[i * half : (i + 1) * half, :] = source[first : first + half, :]


def plane_kernel(factor, *refs):
    parts, (kept_ref, came_ref), outs = refs[:2], refs[2:4], refs[4:]
    rows = outs[0].shape[0]
    mine = (total_of([*parts, outs[0]]) * factor).astype(bf16)
    outs[0][...] = mine
    sources = [kept_ref[...].astype(f32), came_ref[...].astype(f32)]
    block = sources[0].shape[0] // 8
    for plane in range(4):
        riders = jnp.concatenate(
            [
                source[(high * 4 + plane) * block : (high * 4 + plane + 1) * block]
                for source in sources
                for high in range(2)
            ],
            axis=0,
        ).astype(bf16)
        if plane == 0:
            outs[4][...] = riders
        else:
            outs[plane][0:rows, :] = mine
            outs[plane][rows:, :] = riders


def unpack_kernel(block, me_ref, *refs):
    parts, out_ref, rows_s = refs[:-2], refs[-2], refs[-1]
    width = rows_s.shape[1]
    for plane, part in enumerate(parts):
        values = part[part.shape[0] - 4 * block :, :].astype(f32)
        for low in range(2):
            for high in range(2):
                for core in range(2):
                    source = me_ref[0] ^ (high * 16 + low * 8 + plane * 2 + core)
                    first = (low * 2 + high) * block
                    rows_s[pl.ds(pl.multiple_of(source * block, 8), block), :] = values[
                        first : first + block, core * width : (core + 1) * width
                    ]
    out_ref[...] = rows_s[...].T.astype(bf16)


def place_kernel(bit, pieces, slots, placed, me_ref, *refs):
    parts, (in_ref, out_ref, wide_s, sem) = refs[: len(slots)], refs[len(slots) + placed :]
    step, double = wide_s.shape[1:]
    me = me_ref[0]
    base = (me >> bit) & (pieces - 1)
    for core in range(2):

        @pl.when(me % 2 == core)
        def _():
            copies = []
            for i, slot in enumerate(slots):
                first = ((slot % pieces) ^ base) * step
                if (slot >= pieces) == (core == 1):
                    lane = (first // double) * double
                    to = in_ref.at[
                        pl.ds(pl.multiple_of(first - lane, tile), step), pl.ds(pl.multiple_of(lane, 128), double)
                    ]
                else:
                    to = out_ref.at[pl.ds(pl.multiple_of(first, tile), step), :]
                wide_s[i] = parts[i][0:step, :].astype(f32)
                copy = pltpu.make_async_copy(wide_s.at[i], to, sem.at[i])
                copy.start()
                copies.append(copy)
            for copy in copies:
                copy.wait()


def place(me, shapes, quarters, slots, placed):
    pieces = len(quarters) // 2
    step, double = min(quarter.shape for quarter in quarters if quarter is not None)
    return call(
        functools.partial(place_kernel, 1, pieces, slots, len(placed)),
        shapes,
        scratch=[pltpu.VMEM((len(slots), step, double), f32), pltpu.SemaphoreType.DMA((len(slots),))],
        specs=[SMEM] + [VMEM] * len(slots) + [HBM] * len(placed),
        out_specs=[HBM] * 2,
        input_output_aliases={1 + len(slots) + i: i for i in range(len(placed))},
    )(me, *[quarters[slot] for slot in slots], *placed)


def call(kernel, outs, scratch=(), specs=None, count=0, grant=8, **more):
    return pl.pallas_call(
        kernel,
        out_shape=outs,
        in_specs=specs if specs is not None else [VMEM] * count,
        out_specs=more.pop("out_specs", jax.tree.map(lambda _: VMEM, outs)),
        scratch_shapes=list(scratch),
        compiler_params=pltpu.CompilerParams(vmem_limit_bytes=grant and grant * 2**20),
        **more,
    )


def struct(shape, dtype):
    return jax.ShapeDtypeStruct(shape, dtype)


def exchange(value, masks, size):
    return [lax.ppermute(value if not isinstance(value, list) else value[i], "seq",
                         [(d, d ^ mask) for d in range(size)]) for i, mask in enumerate(masks)]


def sum_over_devices(me, ride, ride_send, keep, send, size, factor, riding, shapes):
    bits = size.bit_length() - 1
    rows, double = keep.shape
    radix = min(4, size // 2)
    masks = [m << 1 for m in range(1, radix)]
    rows = rows // radix
    piece, rider = struct((rows, double), bf16), struct(ride.shape, bf16)
    (arrived,) = exchange([send], [1], size)
    if riding:
        (came,) = exchange([ride_send], [1], size)
        arrived, came = lax.optimization_barrier((arrived, came))
    pieces = call(
        functools.partial(split_kernel, radix, 1),
        [struct((rows, double), f32)] + [piece] * (radix - 1),
        specs=[SMEM, VMEM, VMEM],
    )(me, keep, arrived)
    parts = [pieces[0]] + exchange(list(pieces[1:]), masks, size)
    if riding:
        high = call(cores_kernel, [rider] * 2, count=2)(ride, came)
        riders = [high[0]] + exchange([high[1]], [16], size)
        parts, riders = lax.optimization_barrier((parts, riders))
        total = call(functools.partial(total_kernel, 1.0), piece, count=len(parts))(*parts)
        (came,) = exchange([total], [8], size)
        total, kept, sent = call(line_kernel, [piece, rider, rider], count=4)(total, came, *riders)
        last, came = exchange([total, sent], [24, 8], size)
        joined = struct((rows + ride.shape[0] // 2, double), bf16)
        mine, *sends, ride = call(
            functools.partial(plane_kernel, factor),
            [piece] + [joined] * 3 + [struct((ride.shape[0] // 2, double), bf16)],
            count=4,
        )(total, last, kept, came)
        got = exchange(sends, masks, size)
        ride = [ride] + got
    else:
        for rest in range(radix.bit_length(), bits):
            total = call(functools.partial(total_kernel, 1.0), piece, count=len(parts))(*parts)
            parts = [total] + exchange([total], [1 << rest], size)
        mine = call(functools.partial(total_kernel, factor), piece, count=len(parts))(*parts)
        mine, ride = lax.optimization_barrier((mine, ride))
        got = exchange([mine] * (radix - 1), masks, size)
    (first,) = exchange([mine], [1], size)
    got[0], first = lax.optimization_barrier((got[0], first))
    quarters = [mine] + got + [first] + [None] * (radix - 1)
    early = [slot for slot in (0, radix, 1) if riding]
    placed = place(me, shapes, quarters, early, []) if early else []
    if early:
        *got[1:], placed = lax.optimization_barrier((*got[1:], placed))
    quarters = [mine] + got + [first] + exchange(got, [1] * (radix - 1), size)
    placed = place(me, shapes, quarters, [slot for slot in range(2 * radix) if slot not in early], placed)
    return placed, ride


def shards(saved_input, cotangent, w_in, bias_in, w_out, residual_logit, branch_scale):
    size = lax.axis_size("seq")
    levels = size.bit_length() - 1
    rows, width = saved_input.shape
    double, units = w_in.shape
    block = rows // size
    half = rows // 2
    me = lax.axis_index("seq").astype(jnp.int32).reshape(1)
    if block % 8 == 0:
        parts = rows // 128
        both = call(
            pack_kernel,
            struct((size, block, double), bf16),
            scratch=[
                pltpu.VMEM((double, rows), bf16),
                pltpu.VMEM((parts, size // parts, block, double), bf16),
                pltpu.SemaphoreType.DMA((2, 2)),
                pltpu.SemaphoreType.DMA((parts,)),
            ],
            specs=[HBM] * 2,
            out_specs=HBM,
            grant=None,
            cost_estimate=pl.CostEstimate(flops=0, bytes_accessed=7 * 10**6, transcendentals=0),
        )(saved_input.T, cotangent.T)
    else:
        both = jnp.concatenate([saved_input, cotangent], axis=1).reshape(size, block, double)
    both = lax.all_to_all(both, "seq", split_axis=0, concat_axis=0, tiled=True)
    lanes = -(-width // 128) * 128
    parameters = call(
        fetch_kernel,
        [struct(shape, bf16) for shape in ((2 * lanes, units), (units, 2 * lanes)) + ((units, 2 * lanes), (2 * lanes, units))]
        + [struct((1, count), f32) for count in (units, 2 * lanes, 2 * lanes)],
        scratch=[pltpu.VMEM(w_in.shape, bf16), pltpu.VMEM(w_out.shape, bf16), pltpu.SemaphoreType.DMA((2,))],
        specs=[HBM] * 2 + [VMEM] * 3,
    )(w_in, w_out, bias_in, residual_logit, branch_scale)
    total = levels * half
    riding = block % 8 == 0 and levels == 5
    rider = struct((rows // 4, double), bf16)
    send, *factors = call(
        functools.partial(switch_kernel, levels, block),
        [
            struct((units, double), bf16),
            struct((total, double), bf16),
            struct((total, units), bf16),
            struct((total, units), bf16),
            struct((total, double), bf16),
            struct((2, half, lanes), f32),
            struct((2, half, lanes), f32),
            struct((half, 1), f32),
        ],
        scratch=[
            pltpu.VMEM((total, units), f32),
            pltpu.VMEM((2, total, lanes), f32),
            pltpu.VMEM((total, 1), f32),
        ],
        specs=[SMEM] + [VMEM] * 8,
        grant=20,
    )(me, both, *parameters)
    factors, rest = factors[:4], factors[4:]
    grad_state, *ride_send = call(
        functools.partial(first_kernel, block),
        [rider] * 2 if riding else [struct((rows, width), bf16)],
        scratch=[pltpu.VMEM((half, double), f32)],
        specs=[SMEM] + [VMEM] * 6,
        cost_estimate=pl.CostEstimate(flops=rows * units * double, bytes_accessed=rows * units, transcendentals=0),
    )(me, factors[1], *rest, parameters[2], parameters[5])
    keep = call(
        keep_kernel,
        struct((units, double), f32),
        specs=[SMEM] + [VMEM] * 4,
        grant=16,
        cost_estimate=pl.CostEstimate(
            flops=2 * total * units * double, bytes_accessed=8 * total * units, transcendentals=0
        ),
    )(me, *factors)
    ride_send = ride_send[0] if riding else None
    factor = float(rows * size) ** (-0.5)
    if not riding:
        grad_state = lax.all_to_all(
            grad_state.reshape(size, block, width), "seq", split_axis=0, concat_axis=0, tiled=True
        ).reshape(rows, width)
    shapes = [struct((double, units), f32), struct((units, double), f32)]
    (grad_in, grad_out), grad_state = sum_over_devices(me, grad_state, ride_send, keep, send, size, factor, riding, shapes)
    if riding:
        grad_state = call(
            functools.partial(unpack_kernel, block),
            struct((width, rows), bf16),
            scratch=[pltpu.VMEM((rows, width), f32)],
            specs=[SMEM] + [VMEM] * len(grad_state),
        )(me, *grad_state).T
    return (grad_state, grad_in, grad_out)


def solution(mesh):
    in_specs = (P("seq", None), P("seq", None), P(), P(), P(), P(), P())
    out_specs = (P("seq", None), P(), P())
    return jax.shard_map(shards, mesh=mesh, in_specs=in_specs, out_specs=out_specs, check_vma=False)
```

```python
import functools

import jax
import jax.numpy as jnp
from jax import lax
from jax.experimental import pallas as pl
from jax.experimental.pallas import tpu as pltpu
from jax.sharding import PartitionSpec as P

epsilon = 1e-05
tanh_scale = 0.7978845608028654
cubic_coef = 0.044715
f32 = jnp.float32
bf16 = jnp.bfloat16
VMEM = pl.BlockSpec(memory_space=pltpu.VMEM)
SMEM = pl.BlockSpec(memory_space=pltpu.SMEM)
HBM = pl.BlockSpec(memory_space=pltpu.HBM)
tile = 16


def dot(left, right, contract):
    return lax.dot_general(left, right, ((contract[:1], contract[1:]), ((), ())), preferred_element_type=f32)


def pair_rows(state, stride):
    rows, width = state.shape
    groups = rows // (2 * stride)
    if stride >= 8:
        viewed = state.reshape(groups, 2, stride, width)
        return [viewed[:, side].reshape(rows // 2, width) for side in (0, 1)]
    halves = []
    for side in (0, 1):
        row = lax.broadcasted_iota(jnp.int32, (rows // 2, rows), 0)
        col = lax.broadcasted_iota(jnp.int32, (rows // 2, rows), 1)
        pick = (row // stride) * (2 * stride) + row % stride + side * stride
        halves.append(dot((col == pick).astype(bf16), state.astype(bf16), (1, 0)))
    return halves


def unpair_rows(halves, stride):
    half, width = halves[0].shape
    if stride >= 8:
        parts = [part.reshape(half // stride, 1, stride, width) for part in halves]
        return jnp.concatenate(parts, axis=1).reshape(2 * half, width)
    total = jnp.zeros((2 * half, width), f32)
    for side, part in enumerate(halves):
        row = lax.broadcasted_iota(jnp.int32, (2 * half, half), 0)
        col = lax.broadcasted_iota(jnp.int32, (2 * half, half), 1)
        place = (col // stride) * (2 * stride) + col % stride + side * stride
        total = total + dot((row == place).astype(bf16), part.astype(bf16), (1, 0))
    return total


def mean_of(halves, count):
    return jnp.sum(halves[0] + halves[1], axis=-1, keepdims=True) * (1.0 / count)


def widen(part, lanes):
    rows, width = part.shape
    return part if width == lanes else jnp.concatenate([part, jnp.zeros((rows, lanes - width), part.dtype)], axis=1)


def pack_kernel(x_ref, g_ref, out_ref, both_s, rows_s, in_sem, out_sem):
    width, count = x_ref.shape[0], in_sem.shape[1]
    some = width // count
    loads = [
        pltpu.make_async_copy(
            ref.at[part * some : (part + 1) * some, :],
            both_s.at[side * width + part * some : side * width + (part + 1) * some, :],
            in_sem.at[side, part],
        )
        for side, ref in enumerate((x_ref, g_ref))
        for part in range(count)
    ]
    for load in loads:
        load.start()
    for load in loads:
        load.wait()
    blocks = rows_s.shape[1]
    stores = []
    for part in range(rows_s.shape[0]):
        positions = blocks * rows_s.shape[2]
        turned = both_s[:, part * positions : (part + 1) * positions].T
        rows_s[part] = turned.astype(f32).reshape(rows_s.shape[1:]).astype(bf16)
        store = pltpu.make_async_copy(
            rows_s.at[part], out_ref.at[part * blocks : (part + 1) * blocks], out_sem.at[part]
        )
        store.start()
        stores.append(store)
    for store in stores:
        store.wait()


def fetch_kernel(w_in_ref, w_out_ref, bias_ref, logit_ref, scale_ref, *refs):
    w_in_o, w_out_o, w_in_turned_o, w_out_turned_o, bias_o, gate_o, scale_o, w_in_s, w_out_s, sem = refs
    copies = [
        pltpu.make_async_copy(ref, to, sem.at[i])
        for i, (ref, to) in enumerate(((w_in_ref, w_in_s), (w_out_ref, w_out_s)))
    ]
    for copy in copies:
        copy.start()
    width, lanes = w_in_ref.shape[0] // 2, w_in_o.shape[0] // 2
    bias_o[...] = bias_ref[...].reshape(bias_o.shape)
    gate = jax.nn.sigmoid(logit_ref[...].reshape(1, 2 * width))
    scale = scale_ref[...].reshape(1, 2 * width)
    for copy in copies:
        copy.wait()
    for side in range(2):
        first, at = side * width, side * lanes
        gate_o[:, at : at + lanes] = widen(gate[:, first : first + width], lanes)
        scale_o[:, at : at + lanes] = widen(scale[:, first : first + width], lanes)
        w_out_o[:, at : at + lanes] = widen(w_out_s[:, first : first + width], lanes)
        w_in_o[at : at + width, :] = w_in_s[first : first + width, :]
        if lanes > width:
            w_in_o[at + width : at + lanes, :] = jnp.zeros((lanes - width, w_in_o.shape[1]), bf16)
    w_in_turned_o[...] = w_in_o[...].astype(f32).T.astype(bf16)
    w_out_turned_o[...] = w_out_o[...].astype(f32).T.astype(bf16)


def switch_kernel(
    levels, block, me_ref, both_ref, w_in_ref, w_out_ref, w_in_turned_ref, w_out_turned_ref, bias_ref, gate_ref, scale_ref,
    send_ref, low_s, pre_s, act_s, bg_s, upstream_ref, normed_ref, inverse_ref,
    slope_s, normed_s, inverse_s, early_s,
):
    half, double = upstream_ref.shape[1], bg_s.shape[1]
    rows, width = 2 * half, double // 2
    sides = range(2)
    lanes = w_in_ref.shape[0] // 2
    gate = [gate_ref[:, side * lanes : (side + 1) * lanes] for side in sides]
    scale = [scale_ref[:, side * lanes : (side + 1) * lanes] for side in sides]
    both = both_ref[...].astype(f32).reshape(rows, double)
    state = widen(both[:, :width], lanes)
    inside = lax.broadcasted_iota(jnp.int32, (half, lanes), 1) < width

    def scaled_pairs(grad, level):
        upstream = pair_rows(grad, block * 2**level)
        return upstream, [(scale[side] * upstream[side]).astype(bf16) for side in sides]

    def product_of(branch_grad):
        return dot(jnp.concatenate(branch_grad, axis=1), w_out_turned_ref[...], (1, 0))

    for level in range(levels):
        at = pl.ds(level * half, half)
        paired = pair_rows(state, block * 2**level)
        average = mean_of(paired, double)
        centered = [jnp.where(inside, part - average, 0.0) for part in paired]
        inverse = lax.rsqrt(mean_of([part * part for part in centered], double) + epsilon)
        normed = [part * inverse for part in centered]
        low = jnp.concatenate([part.astype(bf16) for part in normed], axis=1)
        low_s[at, :] = jnp.concatenate([part[:, :width].astype(bf16) for part in normed], axis=1)
        inverse_s[at, :] = inverse
        for side in sides:
            normed_s[side, at, :] = normed[side]
        u = dot(low, w_in_ref[...], (1, 0)) + bias_ref[...]
        if level == 0:
            early_s[...] = product_of(scaled_pairs(widen(both[:, width:], lanes), levels - 1)[1])
        square = u * u
        tangent = jnp.tanh(u * (tanh_scale + tanh_scale * cubic_coef * square))
        rise = 0.5 + 0.5 * tangent
        value = u * rise
        act = value.astype(bf16)
        slope_s[at, :] = rise + value * (1.0 - tangent) * (tanh_scale + 3.0 * tanh_scale * cubic_coef * square)
        act_s[at, :] = act
        if level < levels - 1:
            branch = dot(act, w_out_ref[...], (1, 0))
            result = [
                (gate[side] * paired[side] + scale[side] * branch[:, side * lanes : (side + 1) * lanes])
                .astype(bf16)
                .astype(f32)
                for side in sides
            ]
            state = unpair_rows(result, block * 2**level)
    grad = widen(both[:, width:], lanes)
    for level in reversed(range(levels)):
        at = pl.ds(level * half, half)
        upstream, branch_grad = scaled_pairs(grad, level)
        bg_s[at, :] = jnp.concatenate([part[:, :width] for part in branch_grad], axis=1)
        act_grad = early_s[...] if level == levels - 1 else product_of(branch_grad)
        pre_grad = (act_grad * slope_s[at, :]).astype(bf16)
        pre_s[at, :] = pre_grad
        normed = [normed_s[side, at, :] for side in sides]
        if level > 0:
            result = input_grad(pre_grad, w_in_turned_ref, gate, upstream, normed, inverse_s[at, :], double)
            grad = unpair_rows(result, block * 2**level)
    for side in sides:
        upstream_ref[side] = upstream[side]
        normed_ref[side] = normed[side]
    inverse_ref[...] = inverse_s[0:half, :]
    put_products(me_ref[0] % 2 == 0, send_ref, low_s, pre_s, act_s, bg_s)


def input_grad(pre_grad, w_in_turned_ref, gate, upstream, normed, inverse, double):
    sides, lanes = range(2), w_in_turned_ref.shape[1] // 2
    normed_grad = dot(pre_grad, w_in_turned_ref[...], (1, 0))
    normed_grad = [normed_grad[:, side * lanes : (side + 1) * lanes] for side in sides]
    average = mean_of(normed_grad, double)
    product = mean_of([normed_grad[side] * normed[side] for side in sides], double)
    return [
        (gate[side] * upstream[side] + inverse * (normed_grad[side] - average - normed[side] * product))
        .astype(bf16)
        .astype(f32)
        for side in sides
    ]


def keep_kernel(me_ref, *refs):
    put_products(me_ref[0] % 2 == 1, refs[-1], *refs[:-1])


def first_kernel(
    block, me_ref, pre_ref, upstream_ref, normed_ref, inverse_ref, w_in_turned_ref, gate_ref, *refs
):
    *riders, paired_s = refs
    half, double = paired_s.shape
    width, lanes, sides = double // 2, upstream_ref.shape[2], range(2)
    gate = [gate_ref[:, side * lanes : (side + 1) * lanes] for side in sides]
    upstream, normed = [upstream_ref[side] for side in sides], [normed_ref[side] for side in sides]
    result = input_grad(pre_ref[0:half, :], w_in_turned_ref, gate, upstream, normed, inverse_ref[...], double)
    if len(riders) == 2:
        core = me_ref[0] % 2
        paired_s[:, :width] = jnp.where(core == 0, result[0], result[1])[:, :width]
        paired_s[:, width:] = jnp.where(core == 0, result[1], result[0])[:, :width]
        pairs = half // block
        kept, sent = [], []
        for low in range(pairs // 8):
            for plane in range(4):
                found = []
                for high in range(2):
                    chip = ((high * (pairs // 8) + low) * 4 + plane) ^ (me_ref[0] >> 1)
                    found.append(paired_s[pl.ds(pl.multiple_of(chip * block, 8), block), :])
                kept.append(jnp.concatenate([part[:, :width] for part in found], axis=1))
                sent.append(jnp.concatenate([part[:, width:] for part in found], axis=1))
        riders[0][...] = jnp.concatenate(kept, axis=0).astype(bf16)
        riders[1][...] = jnp.concatenate(sent, axis=0).astype(bf16)
    else:
        riders[0][...] = unpair_rows(result, block)[:, :width].astype(bf16)


def put_products(out_first, half_ref, low_ref, pre_ref, act_ref, bg_ref):
    units, double = pre_ref.shape[1], bg_ref.shape[1]

    @pl.when(out_first)
    def _():
        half_ref[0:units, :] = dot(act_ref[...], bg_ref[...], (0, 0)).astype(half_ref.dtype)

    @pl.when(jnp.logical_not(out_first))
    def _():
        grad_in = dot(low_ref[...], pre_ref[...], (0, 0))
        for first in range(0, units, double):
            half_ref[first : first + double, :] = grad_in[:, first : first + double].astype(half_ref.dtype)


def split_kernel(radix, shift, me_ref, keep_ref, arrived_ref, *outs):
    rows = outs[0].shape[0]
    place = (me_ref[0] >> shift) & (radix - 1)
    for other in range(radix):
        at = pl.ds(pl.multiple_of((place ^ other) * rows, tile), rows)
        total = keep_ref[at, :].astype(f32) + arrived_ref[at, :].astype(f32)
        outs[other][...] = total.astype(outs[other].dtype)


def cores_kernel(kept_ref, arrived_ref, *outs):
    width = kept_ref.shape[1] // 2
    sources = [kept_ref[...].astype(f32), arrived_ref[...].astype(f32)]
    for high in range(2):
        lanes = [source[:, high * width : (high + 1) * width] for source in sources]
        outs[high][...] = jnp.concatenate(lanes, axis=1).astype(bf16)


def total_of(refs):
    rows = refs[-1].shape[0]
    total = refs[0][0:rows, :].astype(f32)
    for ref in refs[1:-1]:
        total = total + ref[0:rows, :].astype(f32)
    return total


def total_kernel(factor, *refs):
    refs[-1][...] = (total_of(refs) * factor).astype(refs[-1].dtype)


def line_kernel(*refs):
    parts, sources, (out_ref, kept_ref, sent_ref) = refs[:-5], refs[-5:-3], refs[-3:]
    out_ref[...] = total_of([*parts, out_ref]).astype(bf16)
    half = sources[0].shape[0] // 2
    for first, ref in ((0, kept_ref), (half, sent_ref)):
        for i, source in enumerate(sources):
            ref[i * half : (i + 1) * half, :] = source[first : first + half, :]


def plane_kernel(factor, *refs):
    parts, (kept_ref, came_ref), outs = refs[:2], refs[2:4], refs[4:]
    rows = outs[0].shape[0]
    mine = (total_of([*parts, outs[0]]) * factor).astype(bf16)
    outs[0][...] = mine
    sources = [kept_ref[...].astype(f32), came_ref[...].astype(f32)]
    block = sources[0].shape[0] // 8
    for plane in range(4):
        riders = jnp.concatenate(
            [
                source[(high * 4 + plane) * block : (high * 4 + plane + 1) * block]
                for source in sources
                for high in range(2)
            ],
            axis=0,
        ).astype(bf16)
        if plane == 0:
            outs[4][...] = riders
        else:
            outs[plane][0:rows, :] = mine
            outs[plane][rows:, :] = riders


def unpack_kernel(block, me_ref, *refs):
    parts, out_ref, rows_s = refs[:-2], refs[-2], refs[-1]
    width = rows_s.shape[1]
    for plane, part in enumerate(parts):
        values = part[part.shape[0] - 4 * block :, :].astype(f32)
        for low in range(2):
            for high in range(2):
                for core in range(2):
                    source = me_ref[0] ^ (high * 16 + low * 8 + plane * 2 + core)
                    first = (low * 2 + high) * block
                    rows_s[pl.ds(pl.multiple_of(source * block, 8), block), :] = values[
                        first : first + block, core * width : (core + 1) * width
                    ]
    out_ref[...] = rows_s[...].T.astype(bf16)


def place_kernel(bit, pieces, slots, placed, me_ref, *refs):
    parts, (in_ref, out_ref, wide_s, sem) = refs[: len(slots)], refs[len(slots) + placed :]
    step, double = wide_s.shape[1:]
    me = me_ref[0]
    base = (me >> bit) & (pieces - 1)
    for core in range(2):

        @pl.when(me % 2 == core)
        def _():
            copies = []
            for i, slot in enumerate(slots):
                first = ((slot % pieces) ^ base) * step
                if (slot >= pieces) == (core == 1):
                    lane = (first // double) * double
                    to = in_ref.at[
                        pl.ds(pl.multiple_of(first - lane, tile), step), pl.ds(pl.multiple_of(lane, 128), double)
                    ]
                else:
                    to = out_ref.at[pl.ds(pl.multiple_of(first, tile), step), :]
                wide_s[i] = parts[i][0:step, :].astype(f32)
                copy = pltpu.make_async_copy(wide_s.at[i], to, sem.at[i])
                copy.start()
                copies.append(copy)
            for copy in copies:
                copy.wait()


def place(me, shapes, quarters, slots, placed):
    pieces = len(quarters) // 2
    step, double = min(quarter.shape for quarter in quarters if quarter is not None)
    return call(
        functools.partial(place_kernel, 1, pieces, slots, len(placed)),
        shapes,
        scratch=[pltpu.VMEM((len(slots), step, double), f32), pltpu.SemaphoreType.DMA((len(slots),))],
        specs=[SMEM] + [VMEM] * len(slots) + [HBM] * len(placed),
        out_specs=[HBM] * 2,
        input_output_aliases={1 + len(slots) + i: i for i in range(len(placed))},
    )(me, *[quarters[slot] for slot in slots], *placed)


def call(kernel, outs, scratch=(), specs=None, count=0, grant=8, **more):
    return pl.pallas_call(
        kernel,
        out_shape=outs,
        in_specs=specs if specs is not None else [VMEM] * count,
        out_specs=more.pop("out_specs", jax.tree.map(lambda _: VMEM, outs)),
        scratch_shapes=list(scratch),
        compiler_params=pltpu.CompilerParams(vmem_limit_bytes=grant and grant * 2**20),
        **more,
    )


def struct(shape, dtype):
    return jax.ShapeDtypeStruct(shape, dtype)


def exchange(value, masks, size):
    return [lax.ppermute(value if not isinstance(value, list) else value[i], "seq",
                         [(d, d ^ mask) for d in range(size)]) for i, mask in enumerate(masks)]


def sum_over_devices(me, ride, ride_send, keep, send, size, factor, riding, shapes):
    bits = size.bit_length() - 1
    rows, double = keep.shape
    radix = min(4, size // 2)
    masks = [m << 1 for m in range(1, radix)]
    rows = rows // radix
    piece, rider = struct((rows, double), bf16), struct(ride.shape, bf16)
    (arrived,) = exchange([send], [1], size)
    if riding:
        (came,) = exchange([ride_send], [1], size)
        arrived, came = lax.optimization_barrier((arrived, came))
    pieces = call(
        functools.partial(split_kernel, radix, 1),
        [struct((rows, double), f32)] + [piece] * (radix - 1),
        specs=[SMEM, VMEM, VMEM],
    )(me, keep, arrived)
    parts = [pieces[0]] + exchange(list(pieces[1:]), masks, size)
    if riding:
        high = call(cores_kernel, [rider] * 2, count=2)(ride, came)
        riders = [high[0]] + exchange([high[1]], [16], size)
        parts, riders = lax.optimization_barrier((parts, riders))
        total = call(functools.partial(total_kernel, 1.0), piece, count=len(parts))(*parts)
        (came,) = exchange([total], [8], size)
        total, kept, sent = call(line_kernel, [piece, rider, rider], count=4)(total, came, *riders)
        last, came = exchange([total, sent], [24, 8], size)
        joined = struct((rows + ride.shape[0] // 2, double), bf16)
        mine, *sends, ride = call(
            functools.partial(plane_kernel, factor),
            [piece] + [joined] * 3 + [struct((ride.shape[0] // 2, double), bf16)],
            count=4,
        )(total, last, kept, came)
        got = exchange(sends, masks, size)
        ride = [ride] + got
    else:
        for rest in range(radix.bit_length(), bits):
            total = call(functools.partial(total_kernel, 1.0), piece, count=len(parts))(*parts)
            parts = [total] + exchange([total], [1 << rest], size)
        mine = call(functools.partial(total_kernel, factor), piece, count=len(parts))(*parts)
        mine, ride = lax.optimization_barrier((mine, ride))
        got = exchange([mine] * (radix - 1), masks, size)
    (first,) = exchange([mine], [1], size)
    got[0], first = lax.optimization_barrier((got[0], first))
    quarters = [mine] + got + [first] + [None] * (radix - 1)
    early = [slot for slot in (0, radix, 1) if riding]
    placed = place(me, shapes, quarters, early, []) if early else []
    if early:
        *got[1:], placed = lax.optimization_barrier((*got[1:], placed))
    quarters = [mine] + got + [first] + exchange(got, [1] * (radix - 1), size)
    placed = place(me, shapes, quarters, [slot for slot in range(2 * radix) if slot not in early], placed)
    return placed, ride


def shards(saved_input, cotangent, w_in, bias_in, w_out, residual_logit, branch_scale):
    size = lax.axis_size("seq")
    levels = size.bit_length() - 1
    rows, width = saved_input.shape
    double, units = w_in.shape
    block = rows // size
    half = rows // 2
    me = lax.axis_index("seq").astype(jnp.int32).reshape(1)
    if block % 8 == 0:
        parts = rows // 128
        both = call(
            pack_kernel,
            struct((size, block, double), bf16),
            scratch=[
                pltpu.VMEM((double, rows), bf16),
                pltpu.VMEM((parts, size // parts, block, double), bf16),
                pltpu.SemaphoreType.DMA((2, 2)),
                pltpu.SemaphoreType.DMA((parts,)),
            ],
            specs=[HBM] * 2,
            out_specs=HBM,
            grant=None,
            cost_estimate=pl.CostEstimate(flops=0, bytes_accessed=7 * 10**6, transcendentals=0),
        )(saved_input.T, cotangent.T)
    else:
        both = jnp.concatenate([saved_input, cotangent], axis=1).reshape(size, block, double)
    both = lax.all_to_all(both, "seq", split_axis=0, concat_axis=0, tiled=True)
    lanes = -(-width // 128) * 128
    parameters = call(
        fetch_kernel,
        [struct(shape, bf16) for shape in ((2 * lanes, units), (units, 2 * lanes)) + ((units, 2 * lanes), (2 * lanes, units))]
        + [struct((1, count), f32) for count in (units, 2 * lanes, 2 * lanes)],
        scratch=[pltpu.VMEM(w_in.shape, bf16), pltpu.VMEM(w_out.shape, bf16), pltpu.SemaphoreType.DMA((2,))],
        specs=[HBM] * 2 + [VMEM] * 3,
    )(w_in, w_out, bias_in, residual_logit, branch_scale)
    total = levels * half
    riding = block % 8 == 0 and levels == 5
    rider = struct((rows // 4, double), bf16)
    send, *factors = call(
        functools.partial(switch_kernel, levels, block),
        [
            struct((units, double), bf16),
            struct((total, double), bf16),
            struct((total, units), bf16),
            struct((total, units), bf16),
            struct((total, double), bf16),
            struct((2, half, lanes), f32),
            struct((2, half, lanes), f32),
            struct((half, 1), f32),
        ],
        scratch=[
            pltpu.VMEM((total, units), f32),
            pltpu.VMEM((2, total, lanes), f32),
            pltpu.VMEM((total, 1), f32),
            pltpu.VMEM((half, units), f32),
        ],
        specs=[SMEM] + [VMEM] * 8,
        grant=20,
    )(me, both, *parameters)
    factors, rest = factors[:4], factors[4:]
    grad_state, *ride_send = call(
        functools.partial(first_kernel, block),
        [rider] * 2 if riding else [struct((rows, width), bf16)],
        scratch=[pltpu.VMEM((half, double), f32)],
        specs=[SMEM] + [VMEM] * 6,
        cost_estimate=pl.CostEstimate(flops=rows * units * double, bytes_accessed=rows * units, transcendentals=0),
    )(me, factors[1], *rest, parameters[2], parameters[5])
    keep = call(
        keep_kernel,
        struct((units, double), f32),
        specs=[SMEM] + [VMEM] * 4,
        grant=16,
        cost_estimate=pl.CostEstimate(
            flops=2 * total * units * double, bytes_accessed=8 * total * units, transcendentals=0
        ),
    )(me, *factors)
    ride_send = ride_send[0] if riding else None
    factor = float(rows * size) ** (-0.5)
    if not riding:
        grad_state = lax.all_to_all(
            grad_state.reshape(size, block, width), "seq", split_axis=0, concat_axis=0, tiled=True
        ).reshape(rows, width)
    shapes = [struct((double, units), f32), struct((units, double), f32)]
    (grad_in, grad_out), grad_state = sum_over_devices(me, grad_state, ride_send, keep, send, size, factor, riding, shapes)
    if riding:
        grad_state = call(
            functools.partial(unpack_kernel, block),
            struct((width, rows), bf16),
            scratch=[pltpu.VMEM((rows, width), f32)],
            specs=[SMEM] + [VMEM] * len(grad_state),
        )(me, *grad_state).T
    return (grad_state, grad_in, grad_out)


def solution(mesh):
    in_specs = (P("seq", None), P("seq", None), P(), P(), P(), P(), P())
    out_specs = (P("seq", None), P(), P())
    return jax.shard_map(shards, mesh=mesh, in_specs=in_specs, out_specs=out_specs, check_vma=False)
```

```python
import functools

import jax
import jax.numpy as jnp
from jax import lax
from jax.experimental import pallas as pl
from jax.experimental.pallas import tpu as pltpu
from jax.sharding import PartitionSpec as P

epsilon = 1e-05
tanh_scale = 0.7978845608028654
cubic_coef = 0.044715
f32 = jnp.float32
bf16 = jnp.bfloat16
VMEM = pl.BlockSpec(memory_space=pltpu.VMEM)
SMEM = pl.BlockSpec(memory_space=pltpu.SMEM)
HBM = pl.BlockSpec(memory_space=pltpu.HBM)
tile = 16


def dot(left, right, contract):
    return lax.dot_general(left, right, ((contract[:1], contract[1:]), ((), ())), preferred_element_type=f32)


def pair_rows(state, stride):
    rows, width = state.shape
    groups = rows // (2 * stride)
    if stride >= 8:
        viewed = state.reshape(groups, 2, stride, width)
        return [viewed[:, side].reshape(rows // 2, width) for side in (0, 1)]
    halves = []
    for side in (0, 1):
        row = lax.broadcasted_iota(jnp.int32, (rows // 2, rows), 0)
        col = lax.broadcasted_iota(jnp.int32, (rows // 2, rows), 1)
        pick = (row // stride) * (2 * stride) + row % stride + side * stride
        halves.append(dot((col == pick).astype(bf16), state.astype(bf16), (1, 0)))
    return halves


def unpair_rows(halves, stride):
    half, width = halves[0].shape
    if stride >= 8:
        parts = [part.reshape(half // stride, 1, stride, width) for part in halves]
        return jnp.concatenate(parts, axis=1).reshape(2 * half, width)
    total = jnp.zeros((2 * half, width), f32)
    for side, part in enumerate(halves):
        row = lax.broadcasted_iota(jnp.int32, (2 * half, half), 0)
        col = lax.broadcasted_iota(jnp.int32, (2 * half, half), 1)
        place = (col // stride) * (2 * stride) + col % stride + side * stride
        total = total + dot((row == place).astype(bf16), part.astype(bf16), (1, 0))
    return total


def mean_of(halves, count):
    return jnp.sum(halves[0] + halves[1], axis=-1, keepdims=True) * (1.0 / count)


def widen(part, lanes):
    rows, width = part.shape
    return part if width == lanes else jnp.concatenate([part, jnp.zeros((rows, lanes - width), part.dtype)], axis=1)


def pack_kernel(x_ref, g_ref, out_ref, both_s, rows_s, in_sem, out_sem):
    width, count = x_ref.shape[0], in_sem.shape[1]
    some = width // count
    loads = [
        pltpu.make_async_copy(
            ref.at[part * some : (part + 1) * some, :],
            both_s.at[side * width + part * some : side * width + (part + 1) * some, :],
            in_sem.at[side, part],
        )
        for side, ref in enumerate((x_ref, g_ref))
        for part in range(count)
    ]
    for load in loads:
        load.start()
    for load in loads:
        load.wait()
    blocks = rows_s.shape[1]
    stores = []
    for part in range(rows_s.shape[0]):
        positions = blocks * rows_s.shape[2]
        turned = both_s[:, part * positions : (part + 1) * positions].T
        rows_s[part] = turned.astype(f32).reshape(rows_s.shape[1:]).astype(bf16)
        store = pltpu.make_async_copy(
            rows_s.at[part], out_ref.at[part * blocks : (part + 1) * blocks], out_sem.at[part]
        )
        store.start()
        stores.append(store)
    for store in stores:
        store.wait()


def fetch_kernel(w_in_ref, w_out_ref, bias_ref, logit_ref, scale_ref, *refs):
    w_in_o, w_out_o, w_in_turned_o, w_out_turned_o, bias_o, gate_o, scale_o, w_in_s, w_out_s, sem = refs
    copies = [
        pltpu.make_async_copy(ref, to, sem.at[i])
        for i, (ref, to) in enumerate(((w_in_ref, w_in_s), (w_out_ref, w_out_s)))
    ]
    for copy in copies:
        copy.start()
    width, lanes = w_in_ref.shape[0] // 2, w_in_o.shape[0] // 2
    bias_o[...] = bias_ref[...].reshape(bias_o.shape)
    gate = jax.nn.sigmoid(logit_ref[...].reshape(1, 2 * width))
    scale = scale_ref[...].reshape(1, 2 * width)
    for copy in copies:
        copy.wait()
    for side in range(2):
        first, at = side * width, side * lanes
        gate_o[:, at : at + lanes] = widen(gate[:, first : first + width], lanes)
        scale_o[:, at : at + lanes] = widen(scale[:, first : first + width], lanes)
        w_out_o[:, at : at + lanes] = widen(w_out_s[:, first : first + width], lanes)
        w_in_o[at : at + width, :] = w_in_s[first : first + width, :]
        if lanes > width:
            w_in_o[at + width : at + lanes, :] = jnp.zeros((lanes - width, w_in_o.shape[1]), bf16)
    w_in_turned_o[...] = w_in_o[...].astype(f32).T.astype(bf16)
    w_out_turned_o[...] = w_out_o[...].astype(f32).T.astype(bf16)


def switch_kernel(
    levels, block, me_ref, both_ref, w_in_ref, w_out_ref, w_in_turned_ref, w_out_turned_ref, bias_ref, gate_ref, scale_ref,
    send_ref, low_s, pre_s, act_s, bg_s, upstream_ref, normed_ref, inverse_ref,
    slope_s, normed_s, inverse_s,
):
    half, double = upstream_ref.shape[1], bg_s.shape[1]
    rows, width = 2 * half, double // 2
    sides = range(2)
    lanes = w_in_ref.shape[0] // 2
    gate = [gate_ref[:, side * lanes : (side + 1) * lanes] for side in sides]
    scale = [scale_ref[:, side * lanes : (side + 1) * lanes] for side in sides]
    both = both_ref[...].astype(f32).reshape(rows, double)
    state = widen(both[:, :width], lanes)
    inside = lax.broadcasted_iota(jnp.int32, (half, lanes), 1) < width
    for level in range(levels):
        at = pl.ds(level * half, half)
        paired = pair_rows(state, block * 2**level)
        average = mean_of(paired, double)
        centered = [jnp.where(inside, part - average, 0.0) for part in paired]
        inverse = lax.rsqrt(mean_of([part * part for part in centered], double) + epsilon)
        normed = [part * inverse for part in centered]
        low = jnp.concatenate([part.astype(bf16) for part in normed], axis=1)
        low_s[at, :] = jnp.concatenate([part[:, :width].astype(bf16) for part in normed], axis=1)
        inverse_s[at, :] = inverse
        for side in sides:
            normed_s[side, at, :] = normed[side]
        u = dot(low, w_in_ref[...], (1, 0)) + bias_ref[...]
        square = u * u
        tangent = jnp.tanh(u * (tanh_scale + tanh_scale * cubic_coef * square))
        rise = 0.5 + 0.5 * tangent
        value = u * rise
        act = value.astype(bf16)
        slope_s[at, :] = rise + value * (1.0 - tangent) * (tanh_scale + 3.0 * tanh_scale * cubic_coef * square)
        act_s[at, :] = act
        if level < levels - 1:
            branch = dot(act, w_out_ref[...], (1, 0))
            result = [
                (gate[side] * paired[side] + scale[side] * branch[:, side * lanes : (side + 1) * lanes])
                .astype(bf16)
                .astype(f32)
                for side in sides
            ]
            state = unpair_rows(result, block * 2**level)
    grad = widen(both[:, width:], lanes)
    for level in reversed(range(levels)):
        at = pl.ds(level * half, half)
        upstream = pair_rows(grad, block * 2**level)
        branch_grad = [(scale[side] * upstream[side]).astype(bf16) for side in sides]
        bg_s[at, :] = jnp.concatenate([part[:, :width] for part in branch_grad], axis=1)
        act_grad = dot(jnp.concatenate(branch_grad, axis=1), w_out_turned_ref[...], (1, 0))
        pre_grad = (act_grad * slope_s[at, :]).astype(bf16)
        pre_s[at, :] = pre_grad
        normed = [normed_s[side, at, :] for side in sides]
        if level > 0:
            result = input_grad(pre_grad, w_in_turned_ref, gate, upstream, normed, inverse_s[at, :], double)
            grad = unpair_rows(result, block * 2**level)
    for side in sides:
        upstream_ref[side] = upstream[side]
        normed_ref[side] = normed[side]
    inverse_ref[...] = inverse_s[0:half, :]
    put_products(me_ref[0] % 2 == 0, send_ref, low_s, pre_s, act_s, bg_s)


def input_grad(pre_grad, w_in_turned_ref, gate, upstream, normed, inverse, double):
    sides, lanes = range(2), w_in_turned_ref.shape[1] // 2
    normed_grad = dot(pre_grad, w_in_turned_ref[...], (1, 0))
    normed_grad = [normed_grad[:, side * lanes : (side + 1) * lanes] for side in sides]
    average = mean_of(normed_grad, double)
    product = mean_of([normed_grad[side] * normed[side] for side in sides], double)
    return [
        (gate[side] * upstream[side] + inverse * (normed_grad[side] - average - normed[side] * product))
        .astype(bf16)
        .astype(f32)
        for side in sides
    ]


def keep_kernel(me_ref, *refs):
    put_products(me_ref[0] % 2 == 1, refs[-1], *refs[:-1])


def first_kernel(
    block, me_ref, pre_ref, upstream_ref, normed_ref, inverse_ref, w_in_turned_ref, gate_ref, *refs
):
    *riders, paired_s = refs
    half, double = paired_s.shape
    width, lanes, sides = double // 2, upstream_ref.shape[2], range(2)
    gate = [gate_ref[:, side * lanes : (side + 1) * lanes] for side in sides]
    upstream, normed = [upstream_ref[side] for side in sides], [normed_ref[side] for side in sides]
    result = input_grad(pre_ref[0:half, :], w_in_turned_ref, gate, upstream, normed, inverse_ref[...], double)
    if len(riders) == 2:
        core = me_ref[0] % 2
        paired_s[:, :width] = jnp.where(core == 0, result[0], result[1])[:, :width]
        paired_s[:, width:] = jnp.where(core == 0, result[1], result[0])[:, :width]
        pairs = half // block
        kept, sent = [], []
        for low in range(pairs // 8):
            for plane in range(4):
                found = []
                for high in range(2):
                    chip = ((high * (pairs // 8) + low) * 4 + plane) ^ (me_ref[0] >> 1)
                    found.append(paired_s[pl.ds(pl.multiple_of(chip * block, 8), block), :])
                kept.append(jnp.concatenate([part[:, :width] for part in found], axis=1))
                sent.append(jnp.concatenate([part[:, width:] for part in found], axis=1))
        riders[0][...] = jnp.concatenate(kept, axis=0).astype(bf16)
        riders[1][...] = jnp.concatenate(sent, axis=0).astype(bf16)
    else:
        riders[0][...] = unpair_rows(result, block)[:, :width].astype(bf16)


def put_products(out_first, half_ref, low_ref, pre_ref, act_ref, bg_ref):
    units, double = pre_ref.shape[1], bg_ref.shape[1]

    @pl.when(out_first)
    def _():
        half_ref[0:units, :] = dot(act_ref[...], bg_ref[...], (0, 0)).astype(half_ref.dtype)

    @pl.when(jnp.logical_not(out_first))
    def _():
        grad_in = dot(low_ref[...], pre_ref[...], (0, 0))
        for first in range(0, units, double):
            half_ref[first : first + double, :] = grad_in[:, first : first + double].astype(half_ref.dtype)


def split_kernel(radix, shift, me_ref, keep_ref, arrived_ref, *outs):
    rows = outs[0].shape[0]
    place = (me_ref[0] >> shift) & (radix - 1)
    for other in range(radix):
        at = pl.ds(pl.multiple_of((place ^ other) * rows, tile), rows)
        total = keep_ref[at, :].astype(f32) + arrived_ref[at, :].astype(f32)
        outs[other][...] = total.astype(outs[other].dtype)


def cores_kernel(kept_ref, arrived_ref, *outs):
    width = kept_ref.shape[1] // 2
    sources = [kept_ref[...].astype(f32), arrived_ref[...].astype(f32)]
    for high in range(2):
        lanes = [source[:, high * width : (high + 1) * width] for source in sources]
        outs[high][...] = jnp.concatenate(lanes, axis=1).astype(bf16)


def total_of(refs):
    rows = refs[-1].shape[0]
    total = refs[0][0:rows, :].astype(f32)
    for ref in refs[1:-1]:
        total = total + ref[0:rows, :].astype(f32)
    return total


def total_kernel(factor, *refs):
    refs[-1][...] = (total_of(refs) * factor).astype(refs[-1].dtype)


def line_kernel(*refs):
    parts, sources, (out_ref, kept_ref, sent_ref) = refs[:-5], refs[-5:-3], refs[-3:]
    out_ref[...] = total_of([*parts, out_ref]).astype(bf16)
    half = sources[0].shape[0] // 2
    for first, ref in ((0, kept_ref), (half, sent_ref)):
        for i, source in enumerate(sources):
            ref[i * half : (i + 1) * half, :] = source[first : first + half, :]


def plane_kernel(factor, *refs):
    parts, (kept_ref, came_ref), outs = refs[:2], refs[2:4], refs[4:]
    rows = outs[0].shape[0]
    mine = (total_of([*parts, outs[0]]) * factor).astype(bf16)
    outs[0][...] = mine
    sources = [kept_ref[...].astype(f32), came_ref[...].astype(f32)]
    block = sources[0].shape[0] // 8
    for plane in range(4):
        riders = jnp.concatenate(
            [
                source[(high * 4 + plane) * block : (high * 4 + plane + 1) * block]
                for source in sources
                for high in range(2)
            ],
            axis=0,
        ).astype(bf16)
        if plane == 0:
            outs[4][...] = riders
        else:
            outs[plane][0:rows, :] = mine
            outs[plane][rows:, :] = riders


def unpack_kernel(block, me_ref, *refs):
    parts, out_ref, rows_s = refs[:-2], refs[-2], refs[-1]
    width = rows_s.shape[1]
    for plane, part in enumerate(parts):
        values = part[part.shape[0] - 4 * block :, :].astype(f32)
        for low in range(2):
            for high in range(2):
                for core in range(2):
                    source = me_ref[0] ^ (high * 16 + low * 8 + plane * 2 + core)
                    first = (low * 2 + high) * block
                    rows_s[pl.ds(pl.multiple_of(source * block, 8), block), :] = values[
                        first : first + block, core * width : (core + 1) * width
                    ]
    out_ref[...] = rows_s[...].T.astype(bf16)


def place_kernel(bit, pieces, slots, placed, me_ref, *refs):
    parts, (in_ref, out_ref, wide_s, sem) = refs[: len(slots)], refs[len(slots) + placed :]
    step, double = wide_s.shape[1:]
    me = me_ref[0]
    base = (me >> bit) & (pieces - 1)
    for core in range(2):

        @pl.when(me % 2 == core)
        def _():
            copies = []
            for i, slot in enumerate(slots):
                first = ((slot % pieces) ^ base) * step
                if (slot >= pieces) == (core == 1):
                    lane = (first // double) * double
                    to = in_ref.at[
                        pl.ds(pl.multiple_of(first - lane, tile), step), pl.ds(pl.multiple_of(lane, 128), double)
                    ]
                else:
                    to = out_ref.at[pl.ds(pl.multiple_of(first, tile), step), :]
                wide_s[i] = parts[i][0:step, :].astype(f32)
                copy = pltpu.make_async_copy(wide_s.at[i], to, sem.at[i])
                copy.start()
                copies.append(copy)
            for copy in copies:
                copy.wait()


def place(me, shapes, quarters, slots, placed):
    pieces = len(quarters) // 2
    step, double = min(quarter.shape for quarter in quarters if quarter is not None)
    return call(
        functools.partial(place_kernel, 1, pieces, slots, len(placed)),
        shapes,
        scratch=[pltpu.VMEM((len(slots), step, double), f32), pltpu.SemaphoreType.DMA((len(slots),))],
        specs=[SMEM] + [VMEM] * len(slots) + [HBM] * len(placed),
        out_specs=[HBM] * 2,
        input_output_aliases={1 + len(slots) + i: i for i in range(len(placed))},
    )(me, *[quarters[slot] for slot in slots], *placed)


def call(kernel, outs, scratch=(), specs=None, count=0, grant=8, **more):
    return pl.pallas_call(
        kernel,
        out_shape=outs,
        in_specs=specs if specs is not None else [VMEM] * count,
        out_specs=more.pop("out_specs", jax.tree.map(lambda _: VMEM, outs)),
        scratch_shapes=list(scratch),
        compiler_params=pltpu.CompilerParams(vmem_limit_bytes=grant and grant * 2**20),
        **more,
    )


def struct(shape, dtype):
    return jax.ShapeDtypeStruct(shape, dtype)


def exchange(value, masks, size):
    return [lax.ppermute(value if not isinstance(value, list) else value[i], "seq",
                         [(d, d ^ mask) for d in range(size)]) for i, mask in enumerate(masks)]


def sum_over_devices(me, ride, ride_send, keep, send, size, factor, riding, shapes):
    bits = size.bit_length() - 1
    rows, double = keep.shape
    radix = min(4, size // 2)
    masks = [m << 1 for m in range(1, radix)]
    rows = rows // radix
    piece, rider = struct((rows, double), bf16), struct(ride.shape, bf16)
    (arrived,) = exchange([send], [1], size)
    if riding:
        (came,) = exchange([ride_send], [1], size)
        arrived, came = lax.optimization_barrier((arrived, came))
    pieces = call(
        functools.partial(split_kernel, radix, 1),
        [struct((rows, double), f32)] + [piece] * (radix - 1),
        specs=[SMEM, VMEM, VMEM],
    )(me, keep, arrived)
    parts = [pieces[0]] + exchange(list(pieces[1:]), masks, size)
    if riding:
        high = call(cores_kernel, [rider] * 2, count=2)(ride, came)
        riders = [high[0]] + exchange([high[1]], [16], size)
        parts, riders = lax.optimization_barrier((parts, riders))
        total = call(functools.partial(total_kernel, 1.0), piece, count=len(parts))(*parts)
        (came,) = exchange([total], [8], size)
        total, kept, sent = call(line_kernel, [piece, rider, rider], count=4)(total, came, *riders)
        last, came = exchange([total, sent], [24, 8], size)
        joined = struct((rows + ride.shape[0] // 2, double), bf16)
        mine, *sends, ride = call(
            functools.partial(plane_kernel, factor),
            [piece] + [joined] * 3 + [struct((ride.shape[0] // 2, double), bf16)],
            count=4,
        )(total, last, kept, came)
        got = exchange(sends, masks, size)
        ride = [ride] + got
    else:
        for rest in range(radix.bit_length(), bits):
            total = call(functools.partial(total_kernel, 1.0), piece, count=len(parts))(*parts)
            parts = [total] + exchange([total], [1 << rest], size)
        mine = call(functools.partial(total_kernel, factor), piece, count=len(parts))(*parts)
        mine, ride = lax.optimization_barrier((mine, ride))
        got = exchange([mine] * (radix - 1), masks, size)
    (first,) = exchange([mine], [1], size)
    got[0], first = lax.optimization_barrier((got[0], first))
    quarters = [mine] + got + [first] + [None] * (radix - 1)
    early = [slot for slot in (0, radix, 1) if riding]
    placed = place(me, shapes, quarters, early, []) if early else []
    if early:
        *got[1:], placed = lax.optimization_barrier((*got[1:], placed))
    quarters = [mine] + got + [first] + exchange([part[:rows] for part in got], [1] * (radix - 1), size)
    placed = place(me, shapes, quarters, [slot for slot in range(2 * radix) if slot not in early], placed)
    return placed, ride


def shards(saved_input, cotangent, w_in, bias_in, w_out, residual_logit, branch_scale):
    size = lax.axis_size("seq")
    levels = size.bit_length() - 1
    rows, width = saved_input.shape
    double, units = w_in.shape
    block = rows // size
    half = rows // 2
    me = lax.axis_index("seq").astype(jnp.int32).reshape(1)
    if block % 8 == 0:
        parts = rows // 128
        both = call(
            pack_kernel,
            struct((size, block, double), bf16),
            scratch=[
                pltpu.VMEM((double, rows), bf16),
                pltpu.VMEM((parts, size // parts, block, double), bf16),
                pltpu.SemaphoreType.DMA((2, 2)),
                pltpu.SemaphoreType.DMA((parts,)),
            ],
            specs=[HBM] * 2,
            out_specs=HBM,
            grant=None,
            cost_estimate=pl.CostEstimate(flops=0, bytes_accessed=7 * 10**6, transcendentals=0),
        )(saved_input.T, cotangent.T)
    else:
        both = jnp.concatenate([saved_input, cotangent], axis=1).reshape(size, block, double)
    both = lax.all_to_all(both, "seq", split_axis=0, concat_axis=0, tiled=True)
    lanes = -(-width // 128) * 128
    parameters = call(
        fetch_kernel,
        [struct(shape, bf16) for shape in ((2 * lanes, units), (units, 2 * lanes)) + ((units, 2 * lanes), (2 * lanes, units))]
        + [struct((1, count), f32) for count in (units, 2 * lanes, 2 * lanes)],
        scratch=[pltpu.VMEM(w_in.shape, bf16), pltpu.VMEM(w_out.shape, bf16), pltpu.SemaphoreType.DMA((2,))],
        specs=[HBM] * 2 + [VMEM] * 3,
    )(w_in, w_out, bias_in, residual_logit, branch_scale)
    total = levels * half
    riding = block % 8 == 0 and levels == 5
    rider = struct((rows // 4, double), bf16)
    send, *factors = call(
        functools.partial(switch_kernel, levels, block),
        [
            struct((units, double), bf16),
            struct((total, double), bf16),
            struct((total, units), bf16),
            struct((total, units), bf16),
            struct((total, double), bf16),
            struct((2, half, lanes), f32),
            struct((2, half, lanes), f32),
            struct((half, 1), f32),
        ],
        scratch=[
            pltpu.VMEM((total, units), f32),
            pltpu.VMEM((2, total, lanes), f32),
            pltpu.VMEM((total, 1), f32),
        ],
        specs=[SMEM] + [VMEM] * 8,
        grant=20,
    )(me, both, *parameters)
    factors, rest = factors[:4], factors[4:]
    grad_state, *ride_send = call(
        functools.partial(first_kernel, block),
        [rider] * 2 if riding else [struct((rows, width), bf16)],
        scratch=[pltpu.VMEM((half, double), f32)],
        specs=[SMEM] + [VMEM] * 6,
        cost_estimate=pl.CostEstimate(flops=rows * units * double, bytes_accessed=rows * units, transcendentals=0),
    )(me, factors[1], *rest, parameters[2], parameters[5])
    keep = call(
        keep_kernel,
        struct((units, double), f32),
        specs=[SMEM] + [VMEM] * 4,
        grant=16,
        cost_estimate=pl.CostEstimate(
            flops=2 * total * units * double, bytes_accessed=8 * total * units, transcendentals=0
        ),
    )(me, *factors)
    ride_send = ride_send[0] if riding else None
    factor = float(rows * size) ** (-0.5)
    if not riding:
        grad_state = lax.all_to_all(
            grad_state.reshape(size, block, width), "seq", split_axis=0, concat_axis=0, tiled=True
        ).reshape(rows, width)
    shapes = [struct((double, units), f32), struct((units, double), f32)]
    (grad_in, grad_out), grad_state = sum_over_devices(me, grad_state, ride_send, keep, send, size, factor, riding, shapes)
    if riding:
        grad_state = call(
            functools.partial(unpack_kernel, block),
            struct((width, rows), bf16),
            scratch=[pltpu.VMEM((rows, width), f32)],
            specs=[SMEM] + [VMEM] * len(grad_state),
        )(me, *grad_state).T
    return (grad_state, grad_in, grad_out)


def solution(mesh):
    in_specs = (P("seq", None), P("seq", None), P(), P(), P(), P(), P())
    out_specs = (P("seq", None), P(), P())
    return jax.shard_map(shards, mesh=mesh, in_specs=in_specs, out_specs=out_specs, check_vma=False)
```
